256 devices in a mesh: dp: 32 (over z_hi, x, y), frame: 8 (over z_lo, core).
Axes of the slice: x: 4, y: 4, z: 8 (z_hi: 2, z_lo: 4; z = z_hi * 4 + z_lo), core: 2. Of those that a mesh axis runs over, the one named last changes fastest.
Arguments:
- clip_tokens: bfloat16 [32, 32, 64, 1024], P('dp', 'frame'), may hold values from -8 to 8
- out_grad: bfloat16 [32, 32, 64, 1024], P('dp', 'frame'), may hold values from -6 to 6
- ln_gain: float32 [1024], replicated, may hold values from 0.4 to 1.6
- w_project: bfloat16 [1024, 3072], replicated, may hold values from -2 to 2
- w_expand: bfloat16 [1024, 8192], P(None, 'frame'), may hold values from -0.1875 to 0.1875
Outputs:
- token_grad: bfloat16 [32, 32, 64, 1024], P('dp', 'frame')
- project_grad: float32 [1024, 3072], P('dp', 'frame')
- expand_grad: float32 [1024, 8192], P('dp', 'frame')
- gain_grad: float32 [1024], replicated
The draws below stay inside these ranges and needn't reach their ends.
All inputs are finite; a program needn't handle non-finite values.
Results may differ from the reference program's by a relative error of at most 0.015.
The reference program's roundings to bfloat16 on the way count: a program that leaves them out, or rounds other values in their place, can miss the bound.
Values may be sent and summed in bfloat16 or wider, within the bound.
No kernel may reach another device: no remote copies, remote signals or barrier semaphores. Data moves between devices by JAX's collectives and lax.ppermute only.
A program may use at most 128 MiB of HBM per device.

```python
import math
import jax
import jax.numpy as jnp
from jax import lax

D = 1024
HEADS = 16
HEAD_DIM = 64
EMBED = 8192
PATCHES = 64
FRAMES = 32
CLIPS = 32


def draw_clip_tokens(key, part):
    key = jax.random.fold_in(key, 11)
    key_clip, key_noise, key_scale = jax.random.split(key, 3)
    shape_all = (CLIPS, FRAMES, PATCHES, D)
    clip_part = jax.random.normal(key_clip, (CLIPS, 1, 1, D))
    noise = jax.random.normal(key_noise, shape_all)
    base = 0.8 * clip_part
    scales = jnp.exp(jax.random.uniform(key_scale, (CLIPS, FRAMES, PATCHES, 1), minval=math.log(0.5), maxval=math.log(5.0)))
    return jnp.clip(base + noise * scales, -8.0, 8.0).astype(jnp.bfloat16)


def draw_w_project(key, part):
    key = jax.random.fold_in(key, 23)
    key_base = jax.random.fold_in(key, 0)
    whole = jax.random.normal(key_base, (D, 3 * D)) * D ** (-0.5)
    return jnp.clip(whole, -2.0, 2.0).astype(jnp.bfloat16)


def steps_of(own_key, dims, pieces, low, high):
    loudness, own = 1.0, jax.random.fold_in(own_key, 6)
    for position, blocks in pieces:
        steps = jnp.exp(jax.random.uniform(jax.random.fold_in(own, position), (blocks,), jnp.float32, low / len(pieces), high / len(pieces)))
        loudness = loudness * jnp.repeat(steps, dims[position] // blocks).reshape([-1 if axis == position else 1 for axis in range(len(dims))])
    return loudness


def gaussian(own_key, dims, deviation, most, cuts=(), held_as=jnp.bfloat16):
    result = deviation * jax.random.normal(own_key, dims, jnp.float32)
    if cuts:
        result = result * steps_of(own_key, dims, cuts, -0.22, 0.18)
    return jnp.clip(result, -most, most).astype(held_as)


def setup_inputs(seed: int = 0) -> dict:
    keys = jax.random.split(jax.random.key(seed), 6)
    return {
        "clip_tokens": draw_clip_tokens(jax.random.fold_in(keys[5], 71), 0),
        "out_grad": gaussian(keys[1], (CLIPS, FRAMES, PATCHES, D), 1.0, 6.0, ((0, 32), (1, 8))),
        "ln_gain": jnp.clip(1.0 + 0.12 * jax.random.normal(keys[2], (D,), jnp.float32), 0.4, 1.6),
        "w_project": draw_w_project(jax.random.fold_in(keys[5], 71), 0),
        "w_expand": gaussian(keys[4], (D, EMBED), D ** -0.5, 0.1875, ((1, 8),)),
    }


EPSILON = 1e-05

def standardize(inputs):
    center = inputs - lax.optimization_barrier(jnp.mean(inputs, axis=-1, keepdims=True))
    spread = lax.rsqrt(lax.optimization_barrier(jnp.mean(center * center, axis=-1, keepdims=True)) + EPSILON)
    return (center * spread, spread)

def clip_forward(clip_b, ln_gain, w_project):
    inputs = clip_b.astype(jnp.float32)
    standard, spread = standardize(inputs)
    normed = (standard * ln_gain).astype(jnp.bfloat16)
    projected = jnp.dot(normed.reshape(-1, D), w_project, preferred_element_type=jnp.float32).astype(jnp.bfloat16)
    split_proj = projected.reshape(FRAMES, PATCHES, 3, HEADS, HEAD_DIM).astype(jnp.float32)
    queries = split_proj[:, :, 0]
    key_rows = split_proj[:, :, 1]
    value_rows = split_proj[:, :, 2]
    scores = jnp.einsum('fphd,gphd->phfg', queries, key_rows) * HEAD_DIM ** (-0.5)
    attention = jax.nn.softmax(scores, axis=-1)
    rounded = attention.astype(jnp.bfloat16)
    attended = jnp.einsum('phfg,gphd->fphd', rounded.astype(jnp.float32), value_rows).astype(jnp.bfloat16)
    return (inputs, standard, spread, normed, queries, key_rows, value_rows, attention, rounded, attended.reshape(FRAMES, PATCHES, D))

def reference(clip_tokens, out_grad, ln_gain, w_project, w_expand):
    count_clip = FRAMES * PATCHES

    def pool_one(clip_b):
        outs = clip_forward(clip_b, ln_gain, w_project)
        return lax.optimization_barrier(jnp.sum(outs[0], axis=(0, 1))) + lax.optimization_barrier(jnp.sum(outs[9].astype(jnp.float32), axis=(0, 1)))
    pooled = lax.map(pool_one, clip_tokens) / count_clip
    pooled_b = pooled.astype(jnp.bfloat16)
    embedding = jnp.dot(pooled_b, w_expand, preferred_element_type=jnp.float32)
    centered = embedding - lax.optimization_barrier(jnp.mean(embedding, axis=0, keepdims=True))
    gram = jnp.dot(centered, centered.T, precision=lax.Precision.HIGHEST)
    variances = lax.optimization_barrier(jnp.sum(centered * centered, axis=0)) / (CLIPS - 1)
    coefficient = 100.0 * count_clip / (EMBED * (CLIPS - 1))
    embed_grad = coefficient * (jnp.dot(gram, centered, precision=lax.Precision.HIGHEST) / (CLIPS - 1) - centered * variances)
    embed_grad_b = embed_grad.astype(jnp.bfloat16)
    expand_grad = jnp.dot(pooled_b.T, embed_grad_b, preferred_element_type=jnp.float32)
    pool_grad = jnp.dot(embed_grad_b, w_expand.T, preferred_element_type=jnp.float32)

    def clip_backward(carry, items):
        clip_b, grad_b, pool_row = items
        inputs, standard, spread, normed, queries, key_rows, value_rows, attention, rounded, attended = clip_forward(clip_b, ln_gain, w_project)
        total_grad = grad_b.astype(jnp.float32) + pool_row / count_clip
        attended_grad = total_grad.astype(jnp.bfloat16).reshape(FRAMES, PATCHES, HEADS, HEAD_DIM).astype(jnp.float32)
        prob_grad = jnp.einsum('fphd,gphd->phfg', attended_grad, value_rows)
        centered_prob = prob_grad - lax.optimization_barrier(jnp.sum(attention * prob_grad, axis=-1, keepdims=True))
        score_grad = (attention * centered_prob * HEAD_DIM ** (-0.5)).astype(jnp.bfloat16).astype(jnp.float32)
        query_grad = jnp.einsum('phfg,gphd->fphd', score_grad, key_rows)
        key_grad = jnp.einsum('phfg,fphd->gphd', score_grad, queries)
        value_grad = jnp.einsum('phfg,fphd->gphd', rounded.astype(jnp.float32), attended_grad)
        projected_grad = jnp.stack([query_grad, key_grad, value_grad], axis=2).astype(jnp.bfloat16).reshape(FRAMES * PATCHES, 3 * D)
        flat_normed = normed.reshape(FRAMES * PATCHES, D)
        weight_term = jnp.dot(flat_normed.T, projected_grad, preferred_element_type=jnp.float32)
        normed_grad = jnp.dot(projected_grad, w_project.T, preferred_element_type=jnp.float32).reshape(FRAMES, PATCHES, D)
        gain_term = lax.optimization_barrier(jnp.sum(normed_grad * standard, axis=(0, 1)))
        scaled = normed_grad * ln_gain
        centered_grad = scaled - lax.optimization_barrier(jnp.mean(scaled, axis=-1, keepdims=True)) - standard * lax.optimization_barrier(jnp.mean(scaled * standard, axis=-1, keepdims=True))
        token_grad = (total_grad + spread * centered_grad).astype(jnp.bfloat16)
        return ((carry[0] + weight_term, carry[1] + gain_term), token_grad)
    start = (jnp.zeros((D, 3 * D), jnp.float32), jnp.zeros((D,), jnp.float32))
    sums, token_grad = lax.scan(clip_backward, start, (clip_tokens, out_grad, pool_grad))
    return (token_grad, sums[0], expand_grad, sums[1])
```

```python
import jax
import jax.numpy as jnp
from jax import lax
from jax.experimental import pallas as pl
from jax.experimental.pallas import tpu as pltpu
from jax.sharding import PartitionSpec as P

HEADS = 16
EPSILON = 1e-05
F32 = jnp.float32
BF16 = jnp.bfloat16
MIB = 1 << 20
NT = (((1,), (1,)), ((), ()))
TN = (((0,), (0,)), ((), ()))


def dot(a, b, dims=(((1,), (0,)), ((), ())), precision=None):
    return lax.dot_general(a, b, dims, precision=precision, preferred_element_type=F32)


def standardize(inputs):
    center = inputs - jnp.mean(inputs, axis=-1, keepdims=True)
    spread = lax.rsqrt(jnp.mean(center * center, axis=-1, keepdims=True) + EPSILON)
    return center * spread, spread


def params(mib):
    return pltpu.CompilerParams(vmem_limit_bytes=mib * MIB)


def cost(flops, moved, exps=0):
    return pl.CostEstimate(flops=flops, bytes_accessed=moved, transcendentals=exps)


def pack_kernel(source, packed):
    size = packed.shape[2]
    for group in range(packed.shape[0]):
        packed[group] = source[:, group * size : (group + 1) * size, :]


def unpack_kernel(packed, target):
    size = packed.shape[2]
    for group in range(packed.shape[0]):
        target[:, group * size : (group + 1) * size, :] = packed[group]


def pack(array, groups):
    frames, patches, width = array.shape
    shape = (groups, frames, patches // groups, width)
    return pl.pallas_call(
        pack_kernel,
        out_shape=jax.ShapeDtypeStruct(shape, array.dtype),
        compiler_params=params(8),
        cost_estimate=cost(0, 4 * array.size),
    )(array)


def unpack(array):
    groups, frames, size, width = array.shape
    return pl.pallas_call(
        unpack_kernel,
        out_shape=jax.ShapeDtypeStruct((frames, groups * size, width), array.dtype),
        compiler_params=params(8),
        cost_estimate=cost(0, 4 * array.size),
    )(array)


def lane_halves(slab):
    lane = lax.broadcasted_iota(jnp.int32, slab.shape, 1)
    low = lane < slab.shape[1] // 2
    zero = jnp.zeros_like(slab)
    return jnp.where(low, slab, zero), jnp.where(low, zero, slab)


def same_patch(rows, patches):
    first = lax.broadcasted_iota(jnp.int32, (rows, rows), 0)
    second = lax.broadcasted_iota(jnp.int32, (rows, rows), 1)
    return lax.rem(first, patches) == lax.rem(second, patches)


def softmax(query, keys, scale, mask):
    scores = jnp.where(mask, dot(query, keys, NT) * scale, -jnp.inf)
    weights = jnp.exp(scores - jnp.max(scores, axis=-1, keepdims=True))
    return weights / jnp.sum(weights, axis=-1, keepdims=True)


def forward_kernel(patches, x_ref, gain_ref, w_ref, normed_ref, proj_ref, pool_ref):
    rows, width = x_ref.shape
    inputs = x_ref[...].astype(F32)
    standard, _ = standardize(inputs)
    normed = (standard * gain_ref[...]).astype(BF16)
    normed_ref[...] = normed
    pool_ref[...] = jnp.sum(inputs, axis=0, keepdims=True)
    for part in range(6):
        cols = pl.ds(part * width // 2, width // 2)
        proj_ref[:, cols] = dot(normed, w_ref[:, cols]).astype(BF16)
    mask = same_patch(rows, patches)
    slab = 2 * width // HEADS
    scale = (width // HEADS) ** -0.5
    for pair in range(HEADS // 2):
        at = pair * slab
        query = proj_ref[:, at : at + slab]
        keys = proj_ref[:, width + at : width + at + slab]
        values = proj_ref[:, 2 * width + at : 2 * width + at + slab]
        probs = [softmax(part, keys, scale, mask).astype(BF16) for part in lane_halves(query)]
        attended = dot(jnp.concatenate(probs, 1), jnp.concatenate(lane_halves(values), 0))
        attended = attended.astype(BF16).astype(F32)
        pool_ref[:, at : at + slab] += jnp.sum(attended, axis=0, keepdims=True)


def forward(tokens, gain, w_project, patches):
    rows, width = tokens.shape
    return pl.pallas_call(
        lambda *refs: forward_kernel(patches, *refs),
        out_shape=(
            jax.ShapeDtypeStruct((rows, width), BF16),
            jax.ShapeDtypeStruct((rows, 3 * width), BF16),
            jax.ShapeDtypeStruct((1, width), F32),
        ),
        compiler_params=params(40),
        cost_estimate=cost(10 * rows * width * width, 10 * MIB, HEADS * rows * rows),
    )(tokens, gain, w_project)


def backward_kernel(patches, block, core_ref, proj_ref, grad_ref, share_ref, out_ref, send_ref):
    rows, width = grad_ref.shape
    mask = same_patch(rows, patches)
    slab = 2 * width // HEADS
    scale = (width // HEADS) ** -0.5
    for pair in range(HEADS // 2):
        at = pair * slab
        query = proj_ref[:, at : at + slab]
        keys = proj_ref[:, width + at : width + at + slab]
        values = proj_ref[:, 2 * width + at : 2 * width + at + slab]
        grads = grad_ref[:, at : at + slab].astype(F32) + share_ref[:, at : at + slab]
        grads = grads.astype(BF16)
        query_halves = lane_halves(query)
        grad_halves = lane_halves(grads)
        rounded, score_grads = [], []
        for part, grad in zip(query_halves, grad_halves):
            probs = softmax(part, keys, scale, mask)
            prob_grad = dot(grad, values, NT)
            centered = prob_grad - jnp.sum(probs * prob_grad, axis=-1, keepdims=True)
            score_grads.append((probs * centered * scale).astype(BF16))
            rounded.append(probs.astype(BF16))
        key_halves = lane_halves(keys)
        query_grad = dot(jnp.concatenate(score_grads, 1), jnp.concatenate(key_halves, 0))
        key_grad = dot(jnp.concatenate(score_grads, 0), jnp.concatenate(query_halves, 0), TN)
        value_grad = dot(jnp.concatenate(rounded, 0), jnp.concatenate(grad_halves, 0), TN)
        for first, part in zip((0, width, 2 * width), (query_grad, key_grad, value_grad)):
            start = first + at
            part = part.astype(BF16)
            out_ref[:, start : start + slab] = part
            number, inside = divmod(start, block)
            owner, place = number % 2, number // 2 * block + inside

            @pl.when(core_ref[0] != owner)
            def _():
                send_ref[:, place : place + slab] = part


def backward(core, projected, grads, share, patches, block):
    rows, width = grads.shape
    return pl.pallas_call(
        lambda *refs: backward_kernel(patches, block, *refs),
        in_specs=[pl.BlockSpec(memory_space=pltpu.SMEM)]
        + [pl.BlockSpec(memory_space=pltpu.VMEM)] * 3,
        out_shape=(
            jax.ShapeDtypeStruct(projected.shape, BF16),
            jax.ShapeDtypeStruct((rows, projected.shape[1] // 2), BF16),
        ),
        compiler_params=params(40),
        cost_estimate=cost(16 * rows * rows * width, 8 * MIB, HEADS * rows * rows),
    )(core.reshape(1), projected, grads, share)


def weight_kernel(_, own_ref, other_ref, grad_ref, other_grad_ref, out_ref, flipped):
    rows = own_ref.shape[0]

    @pl.when(pl.program_id(0) == 0)
    def _():
        flipped[:, :rows] = own_ref[...].T
        flipped[:, rows:] = other_ref[...].T

    both = jnp.concatenate([grad_ref[...], other_grad_ref[...]], axis=0)
    terms = dot(flipped[...], both).astype(BF16)
    groups, halves, block = out_ref.shape[:3]
    for half in range(halves):
        for group in range(groups):
            at = (half * groups + group) * block
            out_ref[group, half] = terms[at : at + block]


def weight_terms(core, normed, other_normed, grads, other_grads, groups, halves, steps, cores):
    rows, width = normed.shape
    cols = other_grads.shape[1]
    step = cols // steps
    block = width // (groups * halves)
    return pl.pallas_call(
        weight_kernel,
        grid_spec=pltpu.PrefetchScalarGridSpec(
            num_scalar_prefetch=1,
            grid=(steps,),
            in_specs=[
                pl.BlockSpec((rows, width), lambda i, core: (0, 0)),
                pl.BlockSpec((rows, width), lambda i, core: (0, 0)),
                pl.BlockSpec((rows, step), lambda i, core: (0, cores * i + core[0])),
                pl.BlockSpec((rows, step), lambda i, core: (0, i)),
            ],
            out_specs=pl.BlockSpec(
                (groups, halves, block, step), lambda i, core: (0, 0, 0, i)
            ),
            scratch_shapes=[pltpu.VMEM((width, 2 * rows), BF16)],
        ),
        out_shape=jax.ShapeDtypeStruct((groups, halves, block, cols), BF16),
        compiler_params=params(40),
        cost_estimate=cost(4 * rows * width * cols, 6 * MIB),
    )(core.reshape(1), normed, other_normed, grads, other_grads)


def token_kernel(x_ref, grad_ref, share_ref, gain_ref, proj_ref, w_ref, out_ref, gain_out, total):
    step = pl.program_id(0)
    term = dot(proj_ref[...], w_ref[...], NT)

    @pl.when(step == 0)
    def _():
        total[...] = term

    @pl.when(step > 0)
    def _():
        total[...] += term

    @pl.when(step == pl.num_programs(0) - 1)
    def _():
        normed_grad = total[...]
        standard, spread = standardize(x_ref[...].astype(F32))
        gain_out[...] = jnp.sum(normed_grad * standard, axis=0, keepdims=True)
        scaled = normed_grad * gain_ref[...]
        centered = (
            scaled
            - jnp.mean(scaled, axis=-1, keepdims=True)
            - standard * jnp.mean(scaled * standard, axis=-1, keepdims=True)
        )
        total_grad = grad_ref[...].astype(F32) + share_ref[...]
        out_ref[...] = (total_grad + spread * centered).astype(BF16)


def token_grads(tokens, grads, share, gain, proj_grad, w_project, blocks=3):
    rows, width = tokens.shape
    cols = w_project.shape[1] // blocks
    whole = lambda a: pl.BlockSpec(a.shape, lambda i: (0, 0))
    return pl.pallas_call(
        token_kernel,
        grid=(blocks,),
        in_specs=[
            whole(tokens),
            whole(grads),
            whole(share),
            whole(gain),
            pl.BlockSpec((rows, cols), lambda i: (0, i)),
            pl.BlockSpec((width, cols), lambda i: (0, i)),
        ],
        out_specs=(
            pl.BlockSpec((rows, width), lambda i: (0, 0)),
            pl.BlockSpec((1, width), lambda i: (0, 0)),
        ),
        out_shape=(
            jax.ShapeDtypeStruct((rows, width), BF16),
            jax.ShapeDtypeStruct((1, width), F32),
        ),
        scratch_shapes=[pltpu.VMEM((rows, width), F32)],
        compiler_params=params(40),
        cost_estimate=cost(6 * rows * width * width, 9 * MIB),
    )(tokens, grads, share, gain, proj_grad, w_project)


def embed_kernel(pooled_ref, w_ref, centered_ref, gram_ref):
    embedding = dot(pooled_ref[...], w_ref[...])
    centered = embedding - jnp.mean(embedding, axis=0, keepdims=True)
    centered_ref[...] = centered
    gram_ref[...] = dot(centered, centered, NT, lax.Precision.HIGHEST)


def embed(pooled_all, w_expand):
    clips = pooled_all.shape[0]
    return pl.pallas_call(
        embed_kernel,
        out_shape=(
            jax.ShapeDtypeStruct((clips, w_expand.shape[1]), F32),
            jax.ShapeDtypeStruct((clips, clips), F32),
        ),
        compiler_params=params(16),
        cost_estimate=cost(2 * clips * w_expand.size, 2 * MIB),
    )(pooled_all, w_expand)


def embed_grad_kernel(coefficient, gram_ref, centered_ref, own_ref, w_ref, grad_ref, pool_ref):
    clips = gram_ref.shape[0]
    centered = centered_ref[...]
    variances = jnp.sum(centered * centered, axis=0, keepdims=True) / (clips - 1)
    mixed = dot(gram_ref[...], centered, precision=lax.Precision.HIGHEST)
    grads = coefficient * (mixed / (clips - 1) - centered * variances)
    grads_b = grads.astype(BF16)
    grad_ref[...] = grads_b
    row = lax.broadcasted_iota(jnp.int32, grads.shape, 0)
    own = jnp.where(row == own_ref[0], grads, 0.0)
    own = jnp.sum(own, axis=0, keepdims=True)
    own = jnp.broadcast_to(own, (16, own.shape[1])).astype(BF16)
    pool_ref[...] = dot(own, w_ref[...], NT)[0:1]


def embed_grads(gram, centered, own_index, w_expand, coefficient):
    return pl.pallas_call(
        lambda *refs: embed_grad_kernel(coefficient, *refs),
        in_specs=[
            pl.BlockSpec(memory_space=pltpu.VMEM),
            pl.BlockSpec(memory_space=pltpu.VMEM),
            pl.BlockSpec(memory_space=pltpu.SMEM),
            pl.BlockSpec(memory_space=pltpu.VMEM),
        ],
        out_shape=(
            jax.ShapeDtypeStruct(centered.shape, BF16),
            jax.ShapeDtypeStruct((1, w_expand.shape[0]), F32),
        ),
        compiler_params=params(16),
        cost_estimate=cost(2 * 16 * w_expand.size, 2 * MIB),
    )(gram, centered, own_index.reshape(1), w_expand)


DP = ("zh", "x", "y")
FRAME = ("zl", "core")
SIZES = {"zh": 2, "x": 4, "y": 4, "zl": 4, "core": 2}
SWAP = [(0, 1), (1, 0)]


def exchange(array, axis):
    count = lax.axis_size(axis)
    copies = jnp.broadcast_to(array[None], (count,) + array.shape)
    return lax.all_to_all(copies, axis, split_axis=0, concat_axis=0, tiled=True)


def per_device(clip_tokens, out_grad, ln_gain, w_project, w_expand):
    frame_count = lax.axis_size(FRAME)
    clip_count = lax.axis_size(DP)
    core = lax.axis_index("core")
    frames_dev, patches, width = clip_tokens.shape[1:]
    patches_dev = patches // frame_count
    rows = frames_dev * patches
    tokens_clip = frames_dev * frame_count * patches
    column_block = 3 * width // frame_count
    gain = ln_gain[None, :]

    def to_patches(array):
        moved = lax.all_to_all(
            pack(array, frame_count), FRAME, split_axis=0, concat_axis=0, tiled=True
        )
        return moved.reshape(rows, width)

    tokens = to_patches(clip_tokens[0])
    grads = to_patches(out_grad[0])
    normed, projected, pool_part = forward(tokens, gain, w_project, patches_dev)
    other_normed = lax.ppermute(normed, "core", SWAP)

    pooled = jnp.sum(exchange(pool_part[0], FRAME), axis=0) / tokens_clip
    pooled_all = exchange(pooled.astype(BF16), DP)
    centered, gram_part = embed(pooled_all, w_expand)
    gram = jnp.sum(exchange(gram_part, FRAME), axis=0)
    own_index = lax.axis_index(DP)
    coefficient = 100.0 * tokens_clip / (w_expand.shape[1] * frame_count * (clip_count - 1))
    embed_grad, pool_grad_part = embed_grads(gram, centered, own_index, w_expand, coefficient)
    block_rows = width // clip_count
    row_part = lax.dynamic_slice_in_dim(pooled_all, own_index * block_rows, block_rows, 1)
    expand_grad = dot(row_part, embed_grad, TN)
    share = jnp.sum(exchange(pool_grad_part, FRAME), axis=0) / tokens_clip

    projected_grad, outgoing = backward(core, projected, grads, share, patches_dev, column_block)
    other_grad = lax.ppermute(outgoing, "core", SWAP)
    terms = weight_terms(
        core,
        normed,
        other_normed,
        projected_grad,
        other_grad,
        lax.axis_size(("x", "y")),
        lax.axis_size("zh"),
        lax.axis_size("zl"),
        lax.axis_size("core"),
    )
    terms = lax.all_to_all(terms, ("x", "y"), split_axis=0, concat_axis=0, tiled=True)
    terms = jnp.sum(terms.astype(F32), axis=0).astype(BF16)
    terms = terms.reshape(terms.shape[0], block_rows, lax.axis_size("zl"), column_block)
    terms = terms.swapaxes(1, 2).reshape(-1, block_rows, column_block)
    terms = lax.all_to_all(terms, ("zh", "zl"), split_axis=0, concat_axis=0, tiled=True)
    project_grad = jnp.sum(terms.astype(F32), axis=0)

    token_part, gain_part = token_grads(tokens, grads, share, gain, projected_grad, w_project)
    returned = lax.all_to_all(
        token_part.reshape(frame_count, frames_dev, patches_dev, width),
        FRAME,
        split_axis=0,
        concat_axis=0,
        tiled=True,
    )
    token_grad = unpack(returned)[None]
    gain_clip = jnp.sum(exchange(gain_part, FRAME), axis=0)
    gain_grad = jnp.sum(exchange(gain_clip, DP), axis=0)[0]
    return (token_grad, project_grad, expand_grad, gain_grad)


def solution(mesh):
    split = jax.sharding.Mesh(
        mesh.devices.reshape(tuple(SIZES.values())), tuple(SIZES)
    )
    return jax.shard_map(
        per_device,
        mesh=split,
        in_specs=(
            P(DP, FRAME, None, None),
            P(DP, FRAME, None, None),
            P(),
            P(),
            P(None, FRAME),
        ),
        out_specs=(P(DP, FRAME, None, None), P(DP, FRAME), P(DP, FRAME), P()),
        check_vma=False,
    )
```

```python
import jax
import jax.numpy as jnp
from jax import lax
from jax.experimental import pallas as pl
from jax.experimental.pallas import tpu as pltpu
from jax.sharding import PartitionSpec as P

HEADS = 16
EPSILON = 1e-05
F32 = jnp.float32
BF16 = jnp.bfloat16
MIB = 1 << 20
NT = (((1,), (1,)), ((), ()))
TN = (((0,), (0,)), ((), ()))


def dot(a, b, dims=(((1,), (0,)), ((), ())), precision=None):
    return lax.dot_general(a, b, dims, precision=precision, preferred_element_type=F32)


def standardize(inputs):
    center = inputs - jnp.mean(inputs, axis=-1, keepdims=True)
    spread = lax.rsqrt(jnp.mean(center * center, axis=-1, keepdims=True) + EPSILON)
    return center * spread, spread


def far(array):
    return pltpu.with_memory_space_constraint(array, pltpu.HBM)


VMEM = pl.BlockSpec(memory_space=pltpu.VMEM)
SMEM = pl.BlockSpec(memory_space=pltpu.SMEM)
HBM = pl.BlockSpec(memory_space=pltpu.HBM)


def params(mib):
    return pltpu.CompilerParams(vmem_limit_bytes=mib * MIB)


def cost(flops, moved, exps=0):
    return pl.CostEstimate(flops=flops, bytes_accessed=moved, transcendentals=exps)


def pack_kernel(source, packed):
    size = packed.shape[2]
    for group in range(packed.shape[0]):
        packed[group] = source[:, group * size : (group + 1) * size, :]


def select_kernel(index_ref, source, own, other, arrived):
    copies = [
        pltpu.make_async_copy(source.at[:, index_ref[0]], own, arrived.at[0]),
        pltpu.make_async_copy(source.at[:, index_ref[0] ^ 1], other, arrived.at[1]),
    ]
    for copy in copies:
        copy.start()
    for copy in copies:
        copy.wait()


def pack(array, groups):
    frames, patches, width = array.shape
    shape = (groups, frames, patches // groups, width)
    return pl.pallas_call(
        pack_kernel,
        out_shape=jax.ShapeDtypeStruct(shape, array.dtype),
        compiler_params=params(8),
        cost_estimate=cost(0, 4 * array.size),
    )(array)


def select(index, array):
    shape = jax.ShapeDtypeStruct(array.shape[:1] + array.shape[2:], array.dtype)
    return pl.pallas_call(
        select_kernel,
        in_specs=[SMEM, HBM],
        out_specs=[VMEM, VMEM],
        out_shape=(shape, shape),
        scratch_shapes=[pltpu.SemaphoreType.DMA((2,))],
        compiler_params=params(8),
        cost_estimate=cost(0, 4 * shape.size),
    )(index, far(array))


def merge_kernel(core_ref, own, other, out):
    out[:, core_ref[0]] = own[...]
    out[:, 1 - core_ref[0]] = other[...]


def merge(core, own, other):
    shape = jax.ShapeDtypeStruct(own.shape[:1] + (2,) + own.shape[1:], own.dtype)
    return pl.pallas_call(
        merge_kernel,
        in_specs=[SMEM, VMEM, VMEM],
        out_shape=shape,
        compiler_params=params(8),
        cost_estimate=cost(0, 4 * shape.size),
    )(core, own, other)


def place_kernel(core_ref, own, other, target):
    for group in range(own.shape[0]):
        target[:, group, core_ref[0]] = own[group]
        target[:, group, 1 - core_ref[0]] = other[group]


def place(core, own, other):
    chips, frames, size, width = own.shape
    placed = pl.pallas_call(
        place_kernel,
        in_specs=[SMEM, VMEM, VMEM],
        out_shape=jax.ShapeDtypeStruct((frames, chips, 2, size, width), own.dtype),
        compiler_params=params(8),
        cost_estimate=cost(0, 8 * own.size),
    )(core, own, other)
    return placed.reshape(frames, chips * 2 * size, width)


def row_tiles(row):
    tile = row.shape[1] // 8
    return jnp.concatenate([row[:, i * tile : (i + 1) * tile] for i in range(8)], axis=0)


def tiles_row(tiles):
    return jnp.concatenate([tiles[i : i + 1] for i in range(tiles.shape[0])], axis=1)


def lane_halves(slab):
    lane = lax.broadcasted_iota(jnp.int32, slab.shape, 1)
    low = lane < slab.shape[1] // 2
    zero = jnp.zeros_like(slab)
    return jnp.where(low, slab, zero), jnp.where(low, zero, slab)


def same_patch(rows, patches):
    first = lax.broadcasted_iota(jnp.int32, (rows, rows), 0)
    second = lax.broadcasted_iota(jnp.int32, (rows, rows), 1)
    return lax.rem(first, patches) == lax.rem(second, patches)


def softmax(query, keys, scale, mask):
    scores = jnp.where(mask, dot(query, keys, NT) * scale, -jnp.inf)
    weights = jnp.exp(scores - jnp.max(scores, axis=-1, keepdims=True))
    return weights / jnp.sum(weights, axis=-1, keepdims=True)


def forward_kernel(
    patches,
    x_ref,
    gain_ref,
    w_hbm,
    normed_hbm,
    proj_hbm,
    pool_ref,
    w_ref,
    normed_ref,
    proj_ref,
    total,
    arrived,
    sent,
):
    rows, width = x_ref.shape
    parts = arrived.shape[0]
    chunk = w_ref.shape[1] // parts
    chunks = [pl.ds(part * chunk, chunk) for part in range(parts)]
    loads = [
        pltpu.make_async_copy(w_hbm.at[:, cols], w_ref.at[:, cols], arrived.at[part])
        for part, cols in enumerate(chunks)
    ]
    for load in loads:
        load.start()
    inputs = x_ref[...].astype(F32)
    standard, _ = standardize(inputs)
    normed = (standard * gain_ref[...]).astype(BF16)
    normed_ref[...] = normed
    stores = [pltpu.make_async_copy(normed_ref, normed_hbm, sent.at[parts])]
    stores[-1].start()
    total[...] = jnp.sum(inputs, axis=0, keepdims=True)
    for part, cols in enumerate(chunks):
        loads[part].wait()
        proj_ref[:, cols] = dot(normed, w_ref[:, cols]).astype(BF16)
        stores.append(
            pltpu.make_async_copy(proj_ref.at[:, cols], proj_hbm.at[:, cols], sent.at[part])
        )
        stores[-1].start()
    mask = same_patch(rows, patches)
    slab = 2 * width // HEADS
    scale = (width // HEADS) ** -0.5
    for pair in range(HEADS // 2):
        at = pair * slab
        query = proj_ref[:, at : at + slab]
        keys = proj_ref[:, width + at : width + at + slab]
        values = proj_ref[:, 2 * width + at : 2 * width + at + slab]
        probs = [softmax(part, keys, scale, mask).astype(BF16) for part in lane_halves(query)]
        attended = dot(jnp.concatenate(probs, 1), jnp.concatenate(lane_halves(values), 0))
        attended = attended.astype(BF16).astype(F32)
        total[:, at : at + slab] += jnp.sum(attended, axis=0, keepdims=True)
    tiles = row_tiles(total[...])
    for copy in range(pool_ref.shape[0]):
        pool_ref[copy] = tiles
    for store in stores:
        store.wait()


def forward(tokens, gain, w_project, patches, copies):
    rows, width = tokens.shape
    parts = 6
    return pl.pallas_call(
        lambda *refs: forward_kernel(patches, *refs),
        in_specs=[VMEM, VMEM, HBM],
        out_specs=[HBM, HBM, VMEM],
        out_shape=(
            jax.ShapeDtypeStruct((rows, width), BF16),
            jax.ShapeDtypeStruct((rows, 3 * width), BF16),
            jax.ShapeDtypeStruct((copies, 8, width // 8), F32),
        ),
        scratch_shapes=[
            pltpu.VMEM(w_project.shape, BF16),
            pltpu.VMEM((rows, width), BF16),
            pltpu.VMEM((rows, 3 * width), BF16),
            pltpu.VMEM((1, width), F32),
            pltpu.SemaphoreType.DMA((parts,)),
            pltpu.SemaphoreType.DMA((parts + 1,)),
        ],
        compiler_params=params(56),
        cost_estimate=cost(10 * rows * width * width, 10 * MIB, HEADS * rows * rows),
    )(tokens, gain, far(w_project))


def flip_kernel(normed_ref, other_ref, w_ref, flipped, w_flipped):
    rows, width = normed_ref.shape
    flipped[:, :rows] = normed_ref[...].T
    flipped[:, rows:] = other_ref[...].T
    for part in range(w_ref.shape[1] // rows):
        w_flipped[part * rows : (part + 1) * rows] = w_ref[:, part * rows : (part + 1) * rows].T


def flip(normed, other_normed, w_project):
    rows, width = normed.shape
    return pl.pallas_call(
        flip_kernel,
        in_specs=[VMEM] * 3,
        out_shape=(
            jax.ShapeDtypeStruct((width, 2 * rows), BF16),
            jax.ShapeDtypeStruct((3 * width, width), BF16),
        ),
        compiler_params=params(56),
        cost_estimate=cost(0, 14 * MIB),
    )(normed, other_normed, w_project)


def attend_kernel(patches, proj_ref, rounded, norm):
    rows = proj_ref.shape[0]
    width = proj_ref.shape[1] // 3
    mask = same_patch(rows, patches)
    slab = 2 * width // HEADS
    scale = (width // HEADS) ** -0.5
    for pair in range(HEADS // 2):
        at = pair * slab
        query = proj_ref[:, at : at + slab]
        keys = proj_ref[:, width + at : width + at + slab]
        for half, part in enumerate(lane_halves(keys)):
            head = 2 * pair + half
            scores = jnp.where(mask, dot(part, query, NT) * scale, -jnp.inf)
            weights = jnp.exp(scores - jnp.max(scores, axis=0, keepdims=True))
            probs = (weights / jnp.sum(weights, axis=0, keepdims=True)).astype(BF16)
            rounded[head] = probs
            norm[head : head + 1] = 1.0 / jnp.sum(probs.astype(F32), axis=0, keepdims=True)


def attend(projected, patches):
    rows = projected.shape[0]
    return pl.pallas_call(
        lambda *refs: attend_kernel(patches, *refs),
        in_specs=[VMEM],
        out_shape=(
            jax.ShapeDtypeStruct((HEADS, rows, rows), BF16),
            jax.ShapeDtypeStruct((HEADS, rows), F32),
        ),
        compiler_params=params(56),
        cost_estimate=cost(rows * rows * projected.shape[1], 6 * MIB, HEADS * rows * rows),
    )(projected)


def total_share(parts_ref, count):
    return tiles_row(jnp.sum(parts_ref[...], axis=0)) / count


def value_kernel(
    block, count, core_ref, grad_ref, parts_ref, rounded_hbm, out_ref, keep_ref, send_ref, rounded, arrived
):
    rows, width = grad_ref.shape
    loads = []
    for pair in range(HEADS // 2):
        part = pl.ds(2 * pair, 2)
        loads.append(
            pltpu.make_async_copy(rounded_hbm.at[part], rounded.at[part], arrived.at[pair])
        )
        loads[-1].start()
    share = total_share(parts_ref, count)
    slab = 2 * width // HEADS
    first = width - 2 * block
    for pair in range(HEADS // 2):
        at = pair * slab
        grads = (grad_ref[:, at : at + slab].astype(F32) + share[:, at : at + slab]).astype(BF16)
        loads[pair].wait()
        probs = jnp.concatenate([rounded[2 * pair], rounded[2 * pair + 1]], 1)
        value_grad = dot(probs, jnp.concatenate(lane_halves(grads), 0)).astype(BF16)
        out_ref[:, at : at + slab] = value_grad
        if at >= first:
            owner, place = divmod(at - first, block)

            @pl.when(core_ref[0] == owner)
            def _():
                keep_ref[:, place : place + slab] = value_grad

            @pl.when(core_ref[0] != owner)
            def _():
                send_ref[:, place : place + slab] = value_grad


def value_grads(core, grads, share_parts, rounded, block, count):
    rows, width = grads.shape
    part = jax.ShapeDtypeStruct((rows, block), BF16)
    return pl.pallas_call(
        lambda *refs: value_kernel(block, count, *refs),
        in_specs=[SMEM, VMEM, VMEM, HBM],
        out_shape=(jax.ShapeDtypeStruct((rows, width), BF16), part, part),
        scratch_shapes=[
            pltpu.VMEM(rounded.shape, BF16),
            pltpu.SemaphoreType.DMA((HEADS // 2,)),
        ],
        compiler_params=params(56),
        cost_estimate=cost(4 * rows * rows * width, 4 * MIB),
    )(core, grads, share_parts, far(rounded))


def backward_kernel(
    block,
    count,
    core_ref,
    x_ref,
    proj_ref,
    grad_ref,
    parts_ref,
    rounded_hbm,
    norm_ref,
    value_ref,
    gain_ref,
    w_hbm,
    keep_ref,
    send_ref,
    token_ref,
    gain_out,
    proj_grad,
    rounded,
    w_ref,
    arrived,
):
    rows, width = grad_ref.shape
    loads = []
    for pair in range(HEADS // 2):
        part = pl.ds(2 * pair, 2)
        loads.append(
            pltpu.make_async_copy(rounded_hbm.at[part], rounded.at[part], arrived.at[pair])
        )
        loads[-1].start()
    w_load = pltpu.make_async_copy(w_hbm, w_ref, arrived.at[HEADS // 2])
    w_load.start()
    share = total_share(parts_ref, count)
    slab = 2 * width // HEADS
    scale = (width // HEADS) ** -0.5

    def hand_on(start, part):
        number, inside = divmod(start, block)
        owner, place = number % 2, number // 2 * block + inside

        @pl.when(core_ref[0] == owner)
        def _():
            keep_ref[:, place : place + slab] = part

        @pl.when(core_ref[0] != owner)
        def _():
            send_ref[:, place : place + slab] = part

    for pair in range(HEADS // 2):
        at = pair * slab
        query = proj_ref[:, at : at + slab]
        keys = proj_ref[:, width + at : width + at + slab]
        values = proj_ref[:, 2 * width + at : 2 * width + at + slab]
        grads = (grad_ref[:, at : at + slab].astype(F32) + share[:, at : at + slab]).astype(BF16)
        score_grads = []
        loads[pair].wait()
        for half, part in enumerate(lane_halves(values)):
            head = 2 * pair + half
            probs = rounded[head].astype(F32)
            prob_grad = dot(part, grads, NT)
            mean = jnp.sum(probs * prob_grad, axis=0, keepdims=True) * norm_ref[head : head + 1]
            score_grads.append((probs * (prob_grad - mean) * scale).astype(BF16))
        both = jnp.concatenate(lane_halves(query), 0)
        key_grad = dot(jnp.concatenate(score_grads, 1), both).astype(BF16)
        both = jnp.concatenate(lane_halves(keys), 0)
        query_grad = dot(jnp.concatenate(score_grads, 0), both, TN).astype(BF16)
        proj_grad[:, at : at + slab] = query_grad
        proj_grad[:, width + at : width + at + slab] = key_grad
        hand_on(at, query_grad)
        hand_on(width + at, key_grad)
        if at < width - 2 * block:
            hand_on(2 * width + at, value_ref[:, at : at + slab])

    w_load.wait()
    normed_grad = dot(proj_grad[...], w_ref[: 2 * width]) + dot(value_ref[...], w_ref[2 * width :])
    standard, spread = standardize(x_ref[...].astype(F32))
    gain_out[...] = row_tiles(jnp.sum(normed_grad * standard, axis=0, keepdims=True))
    scaled = normed_grad * gain_ref[...]
    centered = (
        scaled
        - jnp.mean(scaled, axis=-1, keepdims=True)
        - standard * jnp.mean(scaled * standard, axis=-1, keepdims=True)
    )
    total_grad = grad_ref[...].astype(F32) + share
    token_ref[...] = (total_grad + spread * centered).astype(BF16)


def backward(
    core, tokens, projected, grads, share_parts, rounded, norm, value_grad, gain, w_flipped, block, count
):
    rows, width = grads.shape
    half = jax.ShapeDtypeStruct((rows, (3 * width - 2 * block) // 2), BF16)
    return pl.pallas_call(
        lambda *refs: backward_kernel(block, count, *refs),
        in_specs=[SMEM] + [VMEM] * 4 + [HBM] + [VMEM] * 3 + [HBM],
        out_shape=(
            half,
            half,
            jax.ShapeDtypeStruct((rows, width), BF16),
            jax.ShapeDtypeStruct((8, width // 8), F32),
        ),
        scratch_shapes=[
            pltpu.VMEM((rows, 2 * width), BF16),
            pltpu.VMEM(rounded.shape, BF16),
            pltpu.VMEM(w_flipped.shape, BF16),
            pltpu.SemaphoreType.DMA((HEADS // 2 + 1,)),
        ],
        compiler_params=params(56),
        cost_estimate=cost(14 * rows * rows * width, 12 * MIB),
    )(
        core,
        tokens,
        projected,
        grads,
        share_parts,
        far(rounded),
        norm,
        value_grad,
        gain,
        far(w_flipped),
    )


def split_sum(tiles):
    high = tiles.astype(BF16).astype(F32)
    return jnp.concatenate([high, tiles - high], axis=0).astype(BF16)


def weight_kernel(halves, flipped, grad_ref, other_grad_ref, *refs):
    *gain_refs, out_hbm, staged, sent = refs
    groups, _, lanes = out_hbm.shape
    steps = sent.shape[0] - 1
    cols = grad_ref.shape[1] // steps
    tiles = cols // lanes
    block = flipped.shape[0] // (groups * halves)
    span = tiles * halves * block
    copies = []
    for step in range(steps):
        at = pl.ds(step * cols, cols)
        both = jnp.concatenate([grad_ref[:, at], other_grad_ref[:, at]], axis=0)
        terms = dot(flipped[...], both).astype(BF16)
        for tile in range(tiles):
            for half in range(halves):
                for group in range(groups):
                    start = (half * groups + group) * block
                    place = step * span + (tile * halves + half) * block
                    staged[group, place : place + block] = terms[
                        start : start + block, tile * lanes : (tile + 1) * lanes
                    ]
        part = pl.ds(step * span, span)
        copies.append(
            pltpu.make_async_copy(staged.at[:, part], out_hbm.at[:, part], sent.at[step])
        )
        copies[-1].start()
    if gain_refs:
        gains = split_sum(gain_refs[0][...] + gain_refs[1][...])
        for group in range(groups):
            staged[group, steps * span :] = gains
        part = pl.ds(steps * span, 16)
        copies.append(
            pltpu.make_async_copy(staged.at[:, part], out_hbm.at[:, part], sent.at[steps])
        )
        copies[-1].start()
    for copy in copies:
        copy.wait()


def weight_terms(flipped, grads, other_grads, gains, groups, halves, steps):
    width, rows = flipped.shape
    lanes = 128
    extra = 16 if gains else 0
    shape = (groups, width // groups * grads.shape[1] // lanes + extra, lanes)
    return pl.pallas_call(
        lambda *refs: weight_kernel(halves, *refs),
        in_specs=[VMEM] * (3 + len(gains)),
        out_specs=HBM,
        out_shape=jax.ShapeDtypeStruct(shape, BF16),
        scratch_shapes=[pltpu.VMEM(shape, BF16), pltpu.SemaphoreType.DMA((steps + 1,))],
        compiler_params=params(24),
        cost_estimate=cost(2 * rows * width * grads.shape[1], 6 * MIB),
    )(flipped, grads, other_grads, *gains)


def regroup_kernel(block, terms_ref, last_ref, out_ref):
    halves, steps, rows, _ = out_ref.shape
    tiles = (rows - 16) // block
    total = jnp.sum(terms_ref[...].astype(F32), axis=0)
    last = jnp.sum(last_ref[...].astype(F32), axis=0).astype(BF16)
    terms = total.astype(BF16)
    end = total.shape[0] - 16
    gains = split_sum(total[end : end + 8] + total[end + 8 :])
    for half in range(halves):
        for step in range(steps):
            source, first = (terms, step * tiles) if step < steps - 1 else (last, 0)
            for tile in range(tiles):
                start = ((first + tile) * halves + half) * block
                out_ref[half, step, tile * block : (tile + 1) * block] = source[
                    start : start + block
                ]
            out_ref[half, step, tiles * block :] = gains


def regroup(terms, last, halves, steps, block):
    lanes = terms.shape[2]
    shape = (halves, steps, last.shape[1] // halves + 16, lanes)
    return pl.pallas_call(
        lambda *refs: regroup_kernel(block, *refs),
        in_specs=[VMEM, VMEM],
        out_shape=jax.ShapeDtypeStruct(shape, BF16),
        compiler_params=params(32),
        cost_estimate=cost(terms.size, 4 * MIB),
    )(terms, last)


def finish_kernel(terms_ref, out_ref, gain_ref):
    total = jnp.sum(terms_ref[...].astype(F32), axis=0)
    block = out_ref.shape[0]
    lanes = total.shape[1]
    for tile in range(out_ref.shape[1] // lanes):
        out_ref[:, tile * lanes : (tile + 1) * lanes] = total[tile * block : (tile + 1) * block]
    end = total.shape[0] - 16
    gain_ref[...] = tiles_row(total[end : end + 8] + total[end + 8 :])


def finish(terms, block):
    count, rows, lanes = terms.shape
    return pl.pallas_call(
        finish_kernel,
        in_specs=[VMEM],
        out_shape=(
            jax.ShapeDtypeStruct((block, (rows - 16) // block * lanes), F32),
            jax.ShapeDtypeStruct((1, 8 * lanes), F32),
        ),
        compiler_params=params(16),
        cost_estimate=cost(terms.size, MIB),
    )(terms)


def pool_kernel(halves, tokens, parts_ref, out_ref):
    per_clip = parts_ref.shape[0] // halves
    for half in range(halves):
        pooled = jnp.sum(parts_ref[half * per_clip : (half + 1) * per_clip], axis=0) / tokens
        pooled = pooled.astype(BF16).astype(F32)
        for copy in range(out_ref.shape[0]):
            out_ref[copy, half] = pooled


def pool(parts, halves, tokens, copies):
    return pl.pallas_call(
        lambda *refs: pool_kernel(halves, tokens, *refs),
        in_specs=[VMEM],
        out_shape=jax.ShapeDtypeStruct((copies, halves) + parts.shape[1:], F32),
        compiler_params=params(8),
        cost_estimate=cost(parts.size, MIB),
    )(parts)


def embed_kernel(pooled_ref, w_ref, pooled_out, centered_ref, gram_ref, rows_ref):
    groups, halves, tiles, lanes = pooled_ref.shape
    for half in range(halves):
        for tile in range(tiles):
            rows_ref[half * groups : (half + 1) * groups, tile * lanes : (tile + 1) * lanes] = (
                pooled_ref[:, half, tile, :]
            )
    pooled = rows_ref[...].astype(BF16)
    pooled_out[...] = pooled
    embedding = dot(pooled, w_ref[...])
    centered = embedding - jnp.mean(embedding, axis=0, keepdims=True)
    centered_ref[...] = centered
    gram = dot(centered, centered, NT, lax.Precision.HIGHEST)
    size = gram_ref.shape[1]
    gram = [gram[i : i + size] for i in range(0, gram.shape[0], size)]
    gram = jnp.concatenate(gram, axis=1)
    for copy in range(gram_ref.shape[0]):
        gram_ref[copy] = gram


def embed(pooled, w_expand, copies):
    clips = pooled.shape[0] * pooled.shape[1]
    width, columns = w_expand.shape
    return pl.pallas_call(
        embed_kernel,
        in_specs=[VMEM, VMEM],
        out_shape=(
            jax.ShapeDtypeStruct((clips, width), BF16),
            jax.ShapeDtypeStruct((clips, columns), F32),
            jax.ShapeDtypeStruct((copies, min(clips, 8), clips * clips // min(clips, 8)), F32),
        ),
        scratch_shapes=[pltpu.VMEM((clips, width), F32)],
        compiler_params=params(16),
        cost_estimate=cost(2 * clips * w_expand.size, 2 * MIB),
    )(pooled, w_expand)


def embed_grad_kernel(coefficient, own_ref, gram_ref, centered_ref, w_ref, grad_ref, pool_ref):
    clips = centered_ref.shape[0]
    centered = centered_ref[...]
    gram = jnp.sum(gram_ref[...], axis=0)
    gram = [gram[:, i : i + clips] for i in range(0, gram.shape[1], clips)]
    gram = jnp.concatenate(gram, axis=0)
    variances = jnp.sum(centered * centered, axis=0, keepdims=True) / (clips - 1)
    mixed = dot(gram, centered, precision=lax.Precision.HIGHEST)
    grads = coefficient * (mixed / (clips - 1) - centered * variances)
    grad_ref[...] = grads.astype(BF16)
    row = lax.broadcasted_iota(jnp.int32, grads.shape, 0)
    own = jnp.sum(jnp.where(row == own_ref[0], grads, 0.0), axis=0, keepdims=True)
    own = jnp.broadcast_to(own, (16, own.shape[1])).astype(BF16)
    part = row_tiles(dot(own, w_ref[...], NT)[0:1])
    for copy in range(pool_ref.shape[0]):
        pool_ref[copy] = part


def embed_grads(own_index, gram_parts, centered, w_expand, coefficient):
    width = w_expand.shape[0]
    return pl.pallas_call(
        lambda *refs: embed_grad_kernel(coefficient, *refs),
        in_specs=[SMEM, VMEM, VMEM, VMEM],
        out_shape=(
            jax.ShapeDtypeStruct(centered.shape, BF16),
            jax.ShapeDtypeStruct((gram_parts.shape[0], 8, width // 8), F32),
        ),
        compiler_params=params(16),
        cost_estimate=cost(2 * 16 * w_expand.size, 2 * MIB),
    )(own_index, gram_parts, centered, w_expand)


DP = ("zh", "x", "y")
FRAME = ("zl", "core")
SIZES = {"zh": 2, "x": 4, "y": 4, "zl": 4, "core": 2}
SWAP = [(0, 1), (1, 0)]


def to_each(array, axis):
    return lax.all_to_all(array, axis, split_axis=0, concat_axis=0, tiled=True)


def per_device(clip_tokens, out_grad, ln_gain, w_project, w_expand):
    frame_count = lax.axis_size(FRAME)
    clip_count = lax.axis_size(DP)
    halves, steps = lax.axis_size("zh"), lax.axis_size("zl")
    plane = lax.axis_size(("x", "y"))
    core = lax.axis_index("core").reshape(1)
    own_frame = lax.axis_index(FRAME).reshape(1)
    own_clip = lax.axis_index(DP)
    frames_dev, patches, width = clip_tokens.shape[1:]
    patches_dev = patches // frame_count
    rows = frames_dev * patches
    tokens_clip = frames_dev * frame_count * patches
    column_block = 3 * width // frame_count
    block_rows = width // clip_count
    gain = ln_gain[None, :]

    tokens = to_each(pack(clip_tokens[0], frame_count), FRAME).reshape(rows, width)
    out_grad, tokens = lax.optimization_barrier((out_grad, tokens))
    gathered = lax.all_gather(out_grad[0], "zl", axis=0, tiled=True)
    normed, projected, pool_parts = forward(
        tokens, gain, w_project, patches_dev, halves * frame_count
    )
    other_normed = lax.ppermute(normed, "core", SWAP)

    pool_parts = to_each(pool_parts, ("zh",) + FRAME)
    pooled = to_each(pool(pool_parts, halves, tokens_clip, plane), ("x", "y"))
    flipped, w_flipped = flip(normed, other_normed, w_project)
    pooled, flipped, w_flipped = lax.optimization_barrier((pooled, flipped, w_flipped))
    pooled_all, centered, gram_parts = embed(pooled, w_expand, frame_count)
    gram_parts = to_each(gram_parts, FRAME)
    rounded, norm = attend(projected, patches_dev)
    gram_parts, rounded, norm = lax.optimization_barrier((gram_parts, rounded, norm))
    coefficient = 100.0 * tokens_clip / (w_expand.shape[1] * frame_count * (clip_count - 1))
    embed_grad, share_parts = embed_grads(
        own_clip.reshape(1), gram_parts, centered, w_expand, coefficient
    )
    gathered, share_parts = lax.optimization_barrier((gathered, share_parts))
    share_parts = to_each(share_parts, FRAME)
    row_part = lax.dynamic_slice_in_dim(pooled_all, own_clip * block_rows, block_rows, 1)
    expand_grad = dot(row_part, embed_grad, TN)

    own_part, other_part = select(
        own_frame, gathered.reshape(-1, frame_count, patches_dev, width)
    )
    other_part = lax.ppermute(other_part, "core", SWAP)
    grads = merge(
        core,
        own_part.reshape(-1, rows // frame_count, width),
        other_part.reshape(-1, rows // frame_count, width),
    ).reshape(rows, width)

    value_grad, kept, outgoing = value_grads(
        core, grads, share_parts, rounded, column_block, tokens_clip
    )
    incoming = lax.ppermute(outgoing, "core", SWAP)
    last = weight_terms(flipped, kept, incoming, (), plane, halves, 1)
    last = to_each(last, ("x", "y"))
    kept, outgoing, token_part, gain_part = backward(
        core,
        tokens,
        projected,
        grads,
        share_parts,
        rounded,
        norm,
        value_grad,
        gain,
        w_flipped,
        column_block,
        tokens_clip,
    )
    token_parts = lax.all_gather(
        token_part.reshape(frame_count, frames_dev, patches_dev, width), "zl"
    )
    incoming, other_gain = lax.ppermute((outgoing, gain_part), "core", SWAP)
    terms = weight_terms(
        flipped, kept, incoming, (gain_part, other_gain), plane, halves, steps - 1
    )
    last, terms = lax.optimization_barrier((last, terms))
    terms = to_each(terms, ("x", "y"))
    terms = regroup(terms, last, halves, steps, block_rows)
    terms = to_each(terms.reshape((-1,) + terms.shape[2:]), ("zh", "zl"))
    project_grad, gain_grad = finish(terms, block_rows)
    own_part, other_part = select(own_frame, token_parts)
    other_part = lax.ppermute(other_part, "core", SWAP)
    token_grad = place(core, own_part, other_part)[None]
    return (token_grad, project_grad, expand_grad, gain_grad[0])


def solution(mesh):
    split = jax.sharding.Mesh(
        mesh.devices.reshape(tuple(SIZES.values())), tuple(SIZES)
    )
    return jax.shard_map(
        per_device,
        mesh=split,
        in_specs=(
            P(DP, FRAME, None, None),
            P(DP, FRAME, None, None),
            P(),
            P(),
            P(None, FRAME),
        ),
        out_specs=(P(DP, FRAME, None, None), P(DP, FRAME), P(DP, FRAME), P()),
        check_vma=False,
    )
```

```python
import jax
import jax.numpy as jnp
from jax import lax
from jax.experimental import pallas as pl
from jax.experimental.pallas import tpu as pltpu
from jax.sharding import PartitionSpec as P

HEADS = 16
PARTS = 2
EPSILON = 1e-05
F32 = jnp.float32
BF16 = jnp.bfloat16
MIB = 1 << 20
NT = (((1,), (1,)), ((), ()))
TN = (((0,), (0,)), ((), ()))


def dot(a, b, dims=(((1,), (0,)), ((), ())), precision=None):
    return lax.dot_general(a, b, dims, precision=precision, preferred_element_type=F32)


def standardize(inputs):
    center = inputs - jnp.mean(inputs, axis=-1, keepdims=True)
    spread = lax.rsqrt(jnp.mean(center * center, axis=-1, keepdims=True) + EPSILON)
    return center * spread, spread


def far(array):
    return pltpu.with_memory_space_constraint(array, pltpu.HBM)


def far_shape(shape, dtype):
    return pltpu.HBM(shape, dtype)


def near(array):
    return pltpu.with_memory_space_constraint(array, pltpu.VMEM)


def near_shape(shape, dtype):
    return pltpu.VMEM(shape, dtype)


VMEM = pl.BlockSpec(memory_space=pltpu.VMEM)
SMEM = pl.BlockSpec(memory_space=pltpu.SMEM)
HBM = pl.BlockSpec(memory_space=pltpu.HBM)


def params(mib):
    return pltpu.CompilerParams(vmem_limit_bytes=mib * MIB)


def cost(flops, moved, exps=0):
    return pl.CostEstimate(flops=flops, bytes_accessed=moved, transcendentals=exps)


def pack_kernel(source, packed):
    groups, parts, rows, _ = packed.shape
    frames = source.shape[0]
    size = rows // frames
    for group in range(groups):
        for part in range(parts):
            at = (group * parts + part) * size
            pieces = [source[frame, at : at + size].astype(F32) for frame in range(frames)]
            packed[group, part] = jnp.concatenate(pieces, axis=0).astype(BF16)


def pack(array, groups):
    frames, patches, width = array.shape
    rows = frames * patches // (groups * PARTS)
    return pl.pallas_call(
        pack_kernel,
        out_shape=jax.ShapeDtypeStruct((groups, PARTS, rows, width), array.dtype),
        compiler_params=params(8),
        cost_estimate=cost(0, 4 * array.size),
    )(far(array))


def merge_kernel(index_ref, source, out, own, arrived):
    load = pltpu.make_async_copy(source.at[:, index_ref[0]], own, arrived.at[0])
    load.start()
    load.wait()
    parts, owners, rows, _ = out.shape
    frames = own.shape[0] // owners
    size = rows // frames
    for owner in range(owners):
        for part in range(parts):
            pieces = [
                own[owner * frames + frame, part * size : (part + 1) * size].astype(F32)
                for frame in range(frames)
            ]
            out[part, owner] = jnp.concatenate(pieces, axis=0).astype(BF16)


def merge(index, gathered, owners):
    frames, _, size, width = gathered.shape
    rows = frames * size // (owners * PARTS)
    return pl.pallas_call(
        merge_kernel,
        in_specs=[SMEM, HBM],
        out_specs=VMEM,
        out_shape=jax.ShapeDtypeStruct((PARTS, owners, rows, width), BF16),
        scratch_shapes=[pltpu.VMEM((frames, size, width), BF16), pltpu.SemaphoreType.DMA((1,))],
        compiler_params=params(8),
        cost_estimate=cost(0, 4 * frames * size * width),
    )(index, far(gathered))


def place_kernel(index_ref, source, target, own, arrived):
    load = pltpu.make_async_copy(source.at[:, index_ref[0]], own, arrived.at[0])
    load.start()
    load.wait()
    frames = target.shape[0]
    groups, parts, rows, _ = own.shape
    size = rows // frames
    for group in range(groups):
        for frame in range(frames):
            pieces = [
                own[group, part, frame * size : (frame + 1) * size].astype(F32)
                for part in range(parts)
            ]
            target[frame, group] = jnp.concatenate(pieces, axis=0).astype(BF16)


def place(index, gathered, frames):
    groups, _, parts, rows, width = gathered.shape
    size = parts * rows // frames
    placed = pl.pallas_call(
        place_kernel,
        in_specs=[SMEM, HBM],
        out_specs=VMEM,
        out_shape=jax.ShapeDtypeStruct((frames, groups, size, width), BF16),
        scratch_shapes=[
            pltpu.VMEM((groups, parts, rows, width), BF16),
            pltpu.SemaphoreType.DMA((1,)),
        ],
        compiler_params=params(8),
        cost_estimate=cost(0, 4 * groups * parts * rows * width),
    )(index, far(gathered))
    return placed.reshape(frames, groups * size, width)


def row_tiles(row):
    tile = row.shape[1] // 8
    return jnp.concatenate([row[:, i * tile : (i + 1) * tile] for i in range(8)], axis=0)


def tiles_row(tiles):
    return jnp.concatenate([tiles[i : i + 1] for i in range(tiles.shape[0])], axis=1)


def lane_halves(slab):
    lane = lax.broadcasted_iota(jnp.int32, slab.shape, 1)
    low = lane < slab.shape[1] // 2
    zero = jnp.zeros_like(slab)
    return jnp.where(low, slab, zero), jnp.where(low, zero, slab)


def same_patch(rows, columns, patches):
    first = lax.broadcasted_iota(jnp.int32, (rows, columns), 0)
    second = lax.broadcasted_iota(jnp.int32, (rows, columns), 1)
    return lax.rem(first, patches) == lax.rem(second, patches)


def stacked(slab):
    return jnp.concatenate(lane_halves(slab), axis=0)


def side_by_side(array):
    rows = array.shape[0] // 2
    return jnp.concatenate([array[:rows], array[rows:]], axis=1)


def fetch_kernel(source, target, arrived):
    load = pltpu.make_async_copy(source, target, arrived.at[0])
    load.start()
    load.wait()


def fetch(array):
    return pl.pallas_call(
        fetch_kernel,
        in_specs=[HBM],
        out_specs=VMEM,
        out_shape=near_shape(array.shape, array.dtype),
        scratch_shapes=[pltpu.SemaphoreType.DMA((1,))],
        compiler_params=params(4),
        cost_estimate=cost(0, 4 * array.size),
    )(far(array))


def forward_kernel(
    patches,
    x_ref,
    gain_ref,
    w_ref,
    inputs_hbm,
    normed_hbm,
    proj_hbm,
    pool_ref,
    inputs_ref,
    normed_ref,
    proj_ref,
    total,
    sent,
):
    rows, width = normed_ref.shape
    block_rows = rows // PARTS
    parts = sent.shape[0] - 2
    chunk = w_ref.shape[1] // parts
    chunks = [pl.ds(part * chunk, chunk) for part in range(parts)]
    for part in range(PARTS):
        block = x_ref[:, part]
        inputs_ref[part * block_rows : (part + 1) * block_rows] = block.reshape(block_rows, width)
    stores = [pltpu.make_async_copy(inputs_ref, inputs_hbm, sent.at[parts + 1])]
    stores[-1].start()
    inputs = inputs_ref[...].astype(F32)
    standard, _ = standardize(inputs)
    normed = (standard * gain_ref[...]).astype(BF16)
    normed_ref[...] = normed
    stores.append(pltpu.make_async_copy(normed_ref, normed_hbm, sent.at[parts]))
    stores[-1].start()
    total[...] = jnp.sum(inputs, axis=0, keepdims=True)
    for part, cols in enumerate(chunks):
        proj_ref[:, cols] = dot(normed, w_ref[:, cols]).astype(BF16)
        stores.append(
            pltpu.make_async_copy(proj_ref.at[:, cols], proj_hbm.at[:, cols], sent.at[part])
        )
        stores[-1].start()
    mask = same_patch(2 * block_rows, block_rows, patches // PARTS)
    slab = 2 * width // HEADS
    scale = (width // HEADS) ** -0.5
    for pair in range(HEADS // 2):
        at = pair * slab
        for part in range(PARTS):
            own = pl.ds(part * block_rows, block_rows)
            query = proj_ref[own, at : at + slab]
            keys = proj_ref[own, width + at : width + at + slab]
            values = proj_ref[own, 2 * width + at : 2 * width + at + slab]
            scores = jnp.where(mask, dot(stacked(query), keys, NT) * scale, -jnp.inf)
            weights = jnp.exp(scores - jnp.max(scores, axis=1, keepdims=True))
            probs = (weights / jnp.sum(weights, axis=1, keepdims=True)).astype(BF16)
            attended = dot(side_by_side(probs), stacked(values)).astype(BF16).astype(F32)
            total[:, at : at + slab] += jnp.sum(attended, axis=0, keepdims=True)
    tiles = row_tiles(total[...])
    for copy in range(pool_ref.shape[0]):
        pool_ref[copy] = tiles
    for store in stores:
        store.wait()


def forward(tokens, gain, w_project, patches, copies):
    width = tokens.shape[-1]
    rows = tokens.size // width
    parts = 6
    return pl.pallas_call(
        lambda *refs: forward_kernel(patches, *refs),
        in_specs=[VMEM] * 3,
        out_specs=[HBM, HBM, HBM, VMEM],
        out_shape=(
            far_shape((rows, width), BF16),
            far_shape((rows, width), BF16),
            far_shape((rows, 3 * width), BF16),
            jax.ShapeDtypeStruct((copies, 8, width // 8), F32),
        ),
        scratch_shapes=[
            pltpu.VMEM((rows, width), BF16),
            pltpu.VMEM((rows, width), BF16),
            pltpu.VMEM((rows, 3 * width), BF16),
            pltpu.VMEM((1, width), F32),
            pltpu.SemaphoreType.DMA((parts + 2,)),
        ],
        compiler_params=params(32),
        cost_estimate=cost(10 * rows * width * width, 10 * MIB, HEADS * rows * rows),
    )(tokens, gain, near(w_project))


def flip_kernel(*refs):
    *sources, target = refs
    at = 0
    for source in sources:
        rows, width = source.shape
        step = 256
        for start in range(0, width, step):
            target[start : start + step, at : at + rows] = source[:, start : start + step].T
        at += rows


def flip(*arrays):
    shape = (arrays[0].shape[1], sum(a.shape[0] for a in arrays))
    return pl.pallas_call(
        flip_kernel,
        in_specs=[VMEM] * len(arrays),
        out_shape=jax.ShapeDtypeStruct(shape, BF16),
        compiler_params=params(56),
        cost_estimate=cost(0, 4 * shape[0] * shape[1]),
    )(*arrays)


def attend_kernel(patches, proj_ref, rounded, norm):
    rows = rounded.shape[3]
    width = proj_ref.shape[1] // 3
    mask = same_patch(2 * rows, rows, patches // PARTS)
    slab = 2 * width // HEADS
    scale = (width // HEADS) ** -0.5
    for pair in range(HEADS // 2):
        at = pair * slab
        for part in range(PARTS):
            own = pl.ds(part * rows, rows)
            query = proj_ref[own, at : at + slab]
            keys = proj_ref[own, width + at : width + at + slab]
            scores = jnp.where(mask, dot(stacked(keys), query, NT) * scale, -jnp.inf)
            for head in range(2):
                score = scores[head * rows : (head + 1) * rows]
                weights = jnp.exp(score - jnp.max(score, axis=0, keepdims=True))
                probs = (weights / jnp.sum(weights, axis=0, keepdims=True)).astype(BF16)
                rounded[pair, part, head * rows : (head + 1) * rows] = probs
                number = (pair * PARTS + part) * 2 + head
                norm[number : number + 1] = 1.0 / jnp.sum(
                    probs.astype(F32), axis=0, keepdims=True
                )


def attend(projected, patches):
    rows = projected.shape[0] // PARTS
    pairs = HEADS // 2
    return pl.pallas_call(
        lambda *refs: attend_kernel(patches, *refs),
        in_specs=[VMEM],
        out_shape=(
            jax.ShapeDtypeStruct((pairs, PARTS, 2 * rows, rows), BF16),
            jax.ShapeDtypeStruct((HEADS * PARTS, rows), F32),
        ),
        compiler_params=params(56),
        cost_estimate=cost(rows * rows * projected.shape[1], 6 * MIB, HEADS * rows * rows),
    )(projected)


def total_share(parts_ref, count):
    return tiles_row(jnp.sum(parts_ref[...], axis=0)) / count


def backward_kernel(
    block,
    count,
    core_ref,
    x_ref,
    proj_ref,
    grad_ref,
    parts_ref,
    rounded,
    norm_ref,
    gain_ref,
    w_hbm,
    keep_hbm,
    send_hbm,
    token_ref,
    gain_out,
    proj_grad,
    sorted_grad,
    w_ref,
    arrived,
):
    rows, width = grad_ref.shape
    block_rows = rows // PARTS
    w_load = pltpu.make_async_copy(w_hbm, w_ref, arrived.at[0])
    w_load.start()
    share = tiles_row(jnp.sum(parts_ref[...], axis=0)) / count
    slab = 2 * width // HEADS
    scale = (width // HEADS) ** -0.5
    for pair in range(HEADS // 2):
        at = pair * slab
        for part in range(PARTS):
            own = pl.ds(part * block_rows, block_rows)
            query = proj_ref[own, at : at + slab]
            keys = proj_ref[own, width + at : width + at + slab]
            values = proj_ref[own, 2 * width + at : 2 * width + at + slab]
            grads = grad_ref[own, at : at + slab].astype(F32) + share[:, at : at + slab]
            grads = grads.astype(BF16)
            probs = rounded[pair, part]
            prob_grad = dot(stacked(values), grads, NT)
            score_grads = []
            for head in range(2):
                mine = slice(head * block_rows, (head + 1) * block_rows)
                number = (pair * PARTS + part) * 2 + head
                weights = probs[mine].astype(F32)
                moved = prob_grad[mine]
                mean = jnp.sum(weights * moved, axis=0, keepdims=True)
                mean = mean * norm_ref[number : number + 1]
                score_grads.append((weights * (moved - mean) * scale).astype(BF16))
            key_grad = dot(jnp.concatenate(score_grads, 1), stacked(query))
            query_grad = dot(jnp.concatenate(score_grads, 0), stacked(keys), TN)
            value_grad = dot(side_by_side(probs), stacked(grads))
            for first, grad in zip((0, width, 2 * width), (query_grad, key_grad, value_grad)):
                start = first + at
                grad = grad.astype(BF16)
                proj_grad[own, start : start + slab] = grad
                number, inside = divmod(start, block)
                owner, place = number % 2, number // 2 * block + inside
                sorted_grad[core_ref[0] ^ owner, own, place : place + slab] = grad

    stores = [
        pltpu.make_async_copy(sorted_grad.at[number], target, arrived.at[1 + number])
        for number, target in enumerate((keep_hbm, send_hbm))
    ]
    for store in stores:
        store.start()
    w_load.wait()
    normed_grad = dot(proj_grad[...], w_ref[...])
    standard, spread = standardize(x_ref[...].astype(F32))
    gain_out[...] = row_tiles(jnp.sum(normed_grad * standard, axis=0, keepdims=True))
    scaled = normed_grad * gain_ref[...]
    centered = (
        scaled
        - jnp.mean(scaled, axis=-1, keepdims=True)
        - standard * jnp.mean(scaled * standard, axis=-1, keepdims=True)
    )
    total_grad = grad_ref[...].astype(F32) + share
    token_grad = (total_grad + spread * centered).astype(BF16)
    owners, _, size, _ = token_ref.shape
    for part in range(PARTS):
        for owner in range(owners):
            start = part * block_rows + owner * size
            token_ref[owner, part] = token_grad[start : start + size]
    for store in stores:
        store.wait()


def backward(
    core, tokens, projected, grads, share_parts, rounded, norm, gain, w_flipped, block, count, owners
):
    rows, width = grads.shape
    half = jax.ShapeDtypeStruct((rows, 3 * width // 2), BF16)
    return pl.pallas_call(
        lambda *refs: backward_kernel(block, count, *refs),
        in_specs=[SMEM] + [VMEM] * 7 + [HBM],
        out_specs=[HBM, HBM, VMEM, VMEM],
        out_shape=(
            half,
            half,
            jax.ShapeDtypeStruct((owners, PARTS, rows // (owners * PARTS), width), BF16),
            jax.ShapeDtypeStruct((8, width // 8), F32),
        ),
        scratch_shapes=[
            pltpu.VMEM((rows, 3 * width), BF16),
            pltpu.VMEM((2, rows, 3 * width // 2), BF16),
            pltpu.VMEM(w_flipped.shape, BF16),
            pltpu.SemaphoreType.DMA((3,)),
        ],
        compiler_params=params(56),
        cost_estimate=cost(14 * rows * rows * width, 12 * MIB),
    )(
        core,
        tokens,
        projected,
        grads,
        share_parts,
        rounded,
        norm,
        gain,
        far(w_flipped),
    )


def split_sum(tiles):
    high = tiles.astype(BF16).astype(F32)
    return jnp.concatenate([high, tiles - high], axis=0).astype(BF16)


def weight_kernel(halves, flipped, grad_ref, other_grad_ref, *refs):
    *gain_refs, out_hbm, staged, sent = refs
    groups, _, lanes = out_hbm.shape
    steps = sent.shape[0] - 1
    cols = grad_ref.shape[1] // steps
    tiles = cols // lanes
    block = flipped.shape[0] // (groups * halves)
    span = tiles * halves * block
    copies = []
    for step in range(steps):
        at = pl.ds(step * cols, cols)
        both = jnp.concatenate([grad_ref[:, at], other_grad_ref[:, at]], axis=0)
        terms = dot(flipped[...], both).astype(BF16)
        for tile in range(tiles):
            for half in range(halves):
                for group in range(groups):
                    start = (half * groups + group) * block
                    place = step * span + (tile * halves + half) * block
                    staged[group, place : place + block] = terms[
                        start : start + block, tile * lanes : (tile + 1) * lanes
                    ]
        part = pl.ds(step * span, span)
        copies.append(
            pltpu.make_async_copy(staged.at[:, part], out_hbm.at[:, part], sent.at[step])
        )
        copies[-1].start()
    if gain_refs:
        gains = split_sum(gain_refs[0][...] + gain_refs[1][...])
        for group in range(groups):
            staged[group, steps * span :] = gains
        part = pl.ds(steps * span, 16)
        copies.append(
            pltpu.make_async_copy(staged.at[:, part], out_hbm.at[:, part], sent.at[steps])
        )
        copies[-1].start()
    for copy in copies:
        copy.wait()


def weight_terms(flipped, grads, other_grads, gains, groups, halves, steps):
    width, rows = flipped.shape
    lanes = 128
    extra = 16 if gains else 0
    shape = (groups, width // groups * grads.shape[1] // lanes + extra, lanes)
    return pl.pallas_call(
        lambda *refs: weight_kernel(halves, *refs),
        in_specs=[VMEM] * (3 + len(gains)),
        out_specs=HBM,
        out_shape=jax.ShapeDtypeStruct(shape, BF16),
        scratch_shapes=[pltpu.VMEM(shape, BF16), pltpu.SemaphoreType.DMA((steps + 1,))],
        compiler_params=params(24),
        cost_estimate=cost(2 * rows * width * grads.shape[1], 6 * MIB),
    )(flipped, grads, other_grads, *gains)


def regroup_kernel(block, terms_ref, out_ref):
    halves, steps, rows, _ = out_ref.shape
    tiles = (rows - 16) // block
    total = jnp.sum(terms_ref[...].astype(F32), axis=0)
    terms = total.astype(BF16)
    end = total.shape[0] - 16
    gains = split_sum(total[end : end + 8] + total[end + 8 :])
    for half in range(halves):
        for step in range(steps):
            for tile in range(tiles):
                start = ((step * tiles + tile) * halves + half) * block
                out_ref[half, step, tile * block : (tile + 1) * block] = terms[
                    start : start + block
                ]
            out_ref[half, step, tiles * block :] = gains


def regroup(terms, halves, steps, block):
    count, rows, lanes = terms.shape
    shape = (halves, steps, (rows - 16) // (halves * steps) + 16, lanes)
    return pl.pallas_call(
        lambda *refs: regroup_kernel(block, *refs),
        in_specs=[VMEM],
        out_shape=jax.ShapeDtypeStruct(shape, BF16),
        compiler_params=params(32),
        cost_estimate=cost(terms.size, 4 * MIB),
    )(terms)


def finish_kernel(terms_ref, out_ref, gain_ref):
    total = jnp.sum(terms_ref[...].astype(F32), axis=0)
    block = out_ref.shape[0]
    lanes = total.shape[1]
    for tile in range(out_ref.shape[1] // lanes):
        out_ref[:, tile * lanes : (tile + 1) * lanes] = total[tile * block : (tile + 1) * block]
    end = total.shape[0] - 16
    gain_ref[...] = tiles_row(total[end : end + 8] + total[end + 8 :])


def finish(terms, block):
    count, rows, lanes = terms.shape
    return pl.pallas_call(
        finish_kernel,
        in_specs=[VMEM],
        out_shape=(
            jax.ShapeDtypeStruct((block, (rows - 16) // block * lanes), F32),
            jax.ShapeDtypeStruct((1, 8 * lanes), F32),
        ),
        compiler_params=params(16),
        cost_estimate=cost(terms.size, MIB),
    )(terms)


def pool_kernel(halves, tokens, parts_ref, out_ref):
    per_clip = parts_ref.shape[0] // halves
    means = []
    for half in range(halves):
        pooled = jnp.sum(parts_ref[half * per_clip : (half + 1) * per_clip], axis=0) / tokens
        means.append(pooled)
    means = jnp.concatenate(means, axis=0).astype(BF16)
    for copy in range(out_ref.shape[0]):
        out_ref[copy] = means


def pool(parts, halves, tokens, copies):
    return pl.pallas_call(
        lambda *refs: pool_kernel(halves, tokens, *refs),
        in_specs=[VMEM],
        out_shape=jax.ShapeDtypeStruct((copies, halves * parts.shape[1], parts.shape[2]), BF16),
        compiler_params=params(8),
        cost_estimate=cost(parts.size, MIB),
    )(parts)


def embed_kernel(halves, pooled_ref, w_ref, pooled_out, centered_ref, gram_ref, rows_ref):
    groups, tiles, lanes = pooled_ref.shape
    tiles = tiles // halves
    means = pooled_ref[...].astype(F32)
    for half in range(halves):
        for tile in range(tiles):
            rows_ref[half * groups : (half + 1) * groups, tile * lanes : (tile + 1) * lanes] = (
                means[:, half * tiles + tile, :]
            )
    pooled = rows_ref[...].astype(BF16)
    pooled_out[...] = pooled
    embedding = dot(pooled, w_ref[...])
    centered = embedding - jnp.mean(embedding, axis=0, keepdims=True)
    centered_ref[...] = centered
    gram = dot(centered, centered, NT, lax.Precision.HIGHEST)
    size = gram_ref.shape[1]
    gram = [gram[i : i + size] for i in range(0, gram.shape[0], size)]
    gram = jnp.concatenate(gram, axis=1)
    for copy in range(gram_ref.shape[0]):
        gram_ref[copy] = gram


def embed(pooled, w_expand, copies, halves):
    clips = pooled.shape[0] * halves
    width, columns = w_expand.shape
    return pl.pallas_call(
        lambda *refs: embed_kernel(halves, *refs),
        in_specs=[VMEM, VMEM],
        out_shape=(
            jax.ShapeDtypeStruct((clips, width), BF16),
            jax.ShapeDtypeStruct((clips, columns), F32),
            jax.ShapeDtypeStruct((copies, min(clips, 8), clips * clips // min(clips, 8)), F32),
        ),
        scratch_shapes=[pltpu.VMEM((clips, width), F32)],
        compiler_params=params(16),
        cost_estimate=cost(2 * clips * w_expand.size, 2 * MIB),
    )(pooled, w_expand)


def embed_grad_kernel(coefficient, own_ref, gram_ref, centered_ref, w_ref, grad_ref, pool_ref):
    clips = centered_ref.shape[0]
    centered = centered_ref[...]
    gram = jnp.sum(gram_ref[...], axis=0)
    gram = [gram[:, i : i + clips] for i in range(0, gram.shape[1], clips)]
    gram = jnp.concatenate(gram, axis=0)
    variances = jnp.sum(centered * centered, axis=0, keepdims=True) / (clips - 1)
    mixed = dot(gram, centered, precision=lax.Precision.HIGHEST)
    grads = coefficient * (mixed / (clips - 1) - centered * variances)
    grad_ref[...] = grads.astype(BF16)
    row = lax.broadcasted_iota(jnp.int32, grads.shape, 0)
    own = jnp.sum(jnp.where(row == own_ref[0], grads, 0.0), axis=0, keepdims=True)
    own = jnp.broadcast_to(own, (16, own.shape[1])).astype(BF16)
    part = row_tiles(dot(own, w_ref[...], NT)[0:1])
    for copy in range(pool_ref.shape[0]):
        pool_ref[copy] = part


def embed_grads(own_index, gram_parts, centered, w_expand, coefficient):
    width = w_expand.shape[0]
    return pl.pallas_call(
        lambda *refs: embed_grad_kernel(coefficient, *refs),
        in_specs=[SMEM, VMEM, VMEM, VMEM],
        out_shape=(
            jax.ShapeDtypeStruct(centered.shape, BF16),
            jax.ShapeDtypeStruct((gram_parts.shape[0], 8, width // 8), F32),
        ),
        compiler_params=params(16),
        cost_estimate=cost(2 * 16 * w_expand.size, 2 * MIB),
    )(own_index, gram_parts, centered, w_expand)


DP = ("zh", "x", "y")
FRAME = ("zl", "core")
SIZES = {"zh": 2, "x": 4, "y": 4, "zl": 4, "core": 2}
SWAP = [(0, 1), (1, 0)]


def to_each(array, axis):
    return lax.all_to_all(array, axis, split_axis=0, concat_axis=0, tiled=True)


def per_device(clip_tokens, out_grad, ln_gain, w_project, w_expand):
    frame_count = lax.axis_size(FRAME)
    clip_count = lax.axis_size(DP)
    halves, steps = lax.axis_size("zh"), lax.axis_size("zl")
    plane = lax.axis_size(("x", "y"))
    core = lax.axis_index("core").reshape(1)
    own_frame = lax.axis_index(FRAME).reshape(1)
    own_clip = lax.axis_index(DP)
    frames_dev, patches, width = clip_tokens.shape[1:]
    patches_dev = patches // frame_count
    rows = frames_dev * patches
    tokens_clip = frames_dev * frame_count * patches
    column_block = 3 * width // frame_count
    block_rows = width // clip_count
    gain = ln_gain[None, :]

    w_near = fetch(w_project)
    tokens = to_each(pack(clip_tokens[0], frame_count), FRAME)
    out_grad, tokens, w_near = lax.optimization_barrier((out_grad, tokens, w_near))
    gathered = lax.all_gather(out_grad[0], FRAME, axis=0, tiled=True)
    tokens, normed, projected, pool_parts = forward(
        tokens, gain, w_near, patches_dev, halves * frame_count
    )
    other_normed = lax.ppermute(normed, "core", SWAP)

    pool_parts = to_each(pool_parts, ("zh",) + FRAME)
    pooled = to_each(pool(pool_parts, halves, tokens_clip, plane), ("x", "y"))
    rounded, norm = attend(projected, patches_dev)
    flipped = flip(normed, other_normed)
    pooled, rounded, norm, flipped = lax.optimization_barrier((pooled, rounded, norm, flipped))
    pooled_all, centered, gram_parts = embed(pooled, w_expand, frame_count, halves)
    gram_parts = to_each(gram_parts, FRAME)
    w_flipped = flip(w_project)
    gram_parts, w_flipped = lax.optimization_barrier((gram_parts, w_flipped))
    coefficient = 100.0 * tokens_clip / (w_expand.shape[1] * frame_count * (clip_count - 1))
    embed_grad, share_parts = embed_grads(
        own_clip.reshape(1), gram_parts, centered, w_expand, coefficient
    )
    share_parts = to_each(share_parts, FRAME)
    row_part = lax.dynamic_slice_in_dim(pooled_all, own_clip * block_rows, block_rows, 1)
    expand_grad = dot(row_part, embed_grad, TN)

    gathered, _ = lax.optimization_barrier((gathered, gram_parts))
    gathered = gathered.reshape(-1, frame_count, patches_dev, width)
    grads = merge(own_frame, gathered, frame_count).reshape(rows, width)

    kept, outgoing, token_part, gain_part = backward(
        core,
        tokens,
        projected,
        grads,
        share_parts,
        rounded,
        norm,
        gain,
        w_flipped,
        column_block,
        tokens_clip,
        frame_count,
    )
    token_parts = lax.all_gather(token_part, FRAME)
    incoming, other_gain = lax.ppermute((outgoing, gain_part), "core", SWAP)
    terms = weight_terms(
        flipped, kept, incoming, (gain_part, other_gain), plane, halves, steps
    )
    terms = to_each(terms, ("x", "y"))
    terms = regroup(terms, halves, steps, block_rows)
    terms = to_each(terms.reshape((-1,) + terms.shape[2:]), ("zh", "zl"))
    token_grad = place(own_frame, token_parts, frames_dev)[None]
    terms, token_grad = lax.optimization_barrier((terms, token_grad))
    project_grad, gain_grad = finish(terms, block_rows)
    return (token_grad, project_grad, expand_grad, gain_grad[0])


def solution(mesh):
    split = jax.sharding.Mesh(
        mesh.devices.reshape(tuple(SIZES.values())), tuple(SIZES)
    )
    return jax.shard_map(
        per_device,
        mesh=split,
        in_specs=(
            P(DP, FRAME, None, None),
            P(DP, FRAME, None, None),
            P(),
            P(),
            P(None, FRAME),
        ),
        out_specs=(P(DP, FRAME, None, None), P(DP, FRAME), P(DP, FRAME), P()),
        check_vma=False,
    )
```

```python
import jax
import jax.numpy as jnp
from jax import lax
from jax.experimental import pallas as pl
from jax.experimental.pallas import tpu as pltpu
from jax.sharding import PartitionSpec as P

HEADS = 16
PARTS = 2
EPSILON = 1e-05
F32 = jnp.float32
BF16 = jnp.bfloat16
MIB = 1 << 20
NT = (((1,), (1,)), ((), ()))
TN = (((0,), (0,)), ((), ()))


def dot(a, b, dims=(((1,), (0,)), ((), ())), precision=None):
    return lax.dot_general(a, b, dims, precision=precision, preferred_element_type=F32)


def standardize(inputs):
    center = inputs - jnp.mean(inputs, axis=-1, keepdims=True)
    spread = lax.rsqrt(jnp.mean(center * center, axis=-1, keepdims=True) + EPSILON)
    return center * spread, spread


def far(array):
    return pltpu.with_memory_space_constraint(array, pltpu.HBM)


def far_shape(shape, dtype):
    return pltpu.HBM(shape, dtype)


def near_shape(shape, dtype):
    return pltpu.VMEM(shape, dtype)


VMEM = pl.BlockSpec(memory_space=pltpu.VMEM)
SMEM = pl.BlockSpec(memory_space=pltpu.SMEM)
HBM = pl.BlockSpec(memory_space=pltpu.HBM)


def params(mib):
    return pltpu.CompilerParams(vmem_limit_bytes=mib * MIB)


def cost(flops, moved, exps=0):
    return pl.CostEstimate(flops=flops, bytes_accessed=moved, transcendentals=exps)


def pack_kernel(source, packed):
    groups, parts, rows, _ = packed.shape
    frames = source.shape[0]
    size = rows // frames
    for group in range(groups):
        for part in range(parts):
            at = (group * parts + part) * size
            pieces = [source[frame, at : at + size].astype(F32) for frame in range(frames)]
            packed[group, part] = jnp.concatenate(pieces, axis=0).astype(BF16)


def pack(array, groups):
    frames, patches, width = array.shape
    rows = frames * patches // (groups * PARTS)
    return pl.pallas_call(
        pack_kernel,
        out_shape=jax.ShapeDtypeStruct((groups, PARTS, rows, width), array.dtype),
        compiler_params=params(8),
        cost_estimate=cost(0, 4 * array.size),
    )(array)


def place_kernel(index_ref, source, target, own, arrived):
    load = pltpu.make_async_copy(source.at[:, index_ref[0]], own, arrived.at[0])
    load.start()
    load.wait()
    frames = target.shape[0]
    groups, parts, rows, _ = own.shape
    size = rows // frames
    for group in range(groups):
        for frame in range(frames):
            pieces = [
                own[group, part, frame * size : (frame + 1) * size].astype(F32)
                for part in range(parts)
            ]
            target[frame, group] = jnp.concatenate(pieces, axis=0).astype(BF16)


def place(index, gathered, frames):
    groups, _, parts, rows, width = gathered.shape
    size = parts * rows // frames
    placed = pl.pallas_call(
        place_kernel,
        in_specs=[SMEM, HBM],
        out_specs=VMEM,
        out_shape=jax.ShapeDtypeStruct((frames, groups, size, width), BF16),
        scratch_shapes=[
            pltpu.VMEM((groups, parts, rows, width), BF16),
            pltpu.SemaphoreType.DMA((1,)),
        ],
        compiler_params=params(8),
        cost_estimate=cost(0, 4 * groups * parts * rows * width),
    )(index, far(gathered))
    return placed.reshape(frames, groups * size, width)


def row_tiles(row):
    tile = row.shape[1] // 8
    return jnp.concatenate([row[:, i * tile : (i + 1) * tile] for i in range(8)], axis=0)


def tiles_row(tiles):
    return jnp.concatenate([tiles[i : i + 1] for i in range(tiles.shape[0])], axis=1)


def lane_halves(slab):
    lane = lax.broadcasted_iota(jnp.int32, slab.shape, 1)
    low = lane < slab.shape[1] // 2
    zero = jnp.zeros_like(slab)
    return jnp.where(low, slab, zero), jnp.where(low, zero, slab)


def same_patch(rows, columns, patches):
    first = lax.broadcasted_iota(jnp.int32, (rows, columns), 0)
    second = lax.broadcasted_iota(jnp.int32, (rows, columns), 1)
    return lax.rem(first, patches) == lax.rem(second, patches)


def stacked(slab):
    return jnp.concatenate(lane_halves(slab), axis=0)


def side_by_side(array):
    rows = array.shape[0] // 2
    return jnp.concatenate([array[:rows], array[rows:]], axis=1)


def forward_kernel(
    patches,
    x_ref,
    gain_ref,
    w_hbm,
    inputs_hbm,
    normed_hbm,
    proj_hbm,
    pool_ref,
    inputs_ref,
    normed_ref,
    proj_ref,
    total,
    sent,
    w_ref,
    arrived,
):
    rows, width = normed_ref.shape
    block_rows = rows // PARTS
    parts = sent.shape[0] - 1
    chunk = w_ref.shape[1] // parts
    chunks = [pl.ds(part * chunk, chunk) for part in range(parts)]
    loads = [
        pltpu.make_async_copy(w_hbm.at[:, cols], w_ref.at[:, cols], arrived.at[part])
        for part, cols in enumerate(chunks)
    ]
    for load in loads:
        load.start()
    for part in range(PARTS):
        block = x_ref[:, part]
        inputs_ref[part * block_rows : (part + 1) * block_rows] = block.reshape(block_rows, width)
    stores = [pltpu.make_async_copy(inputs_ref, inputs_hbm, sent.at[parts, 1])]
    stores[-1].start()
    inputs = inputs_ref[...].astype(F32)
    standard, _ = standardize(inputs)
    normed = (standard * gain_ref[...]).astype(BF16)
    normed_ref[...] = normed
    stores.append(pltpu.make_async_copy(normed_ref, normed_hbm, sent.at[parts, 0]))
    stores[-1].start()
    total[...] = jnp.sum(inputs, axis=0, keepdims=True)
    for part, cols in enumerate(chunks):
        loads[part].wait()
        proj_ref[:, cols] = dot(normed, w_ref[:, cols]).astype(BF16)
        for pair in range(proj_hbm.shape[0]):
            lanes = pl.ds(part * chunk + pair * proj_hbm.shape[3], proj_hbm.shape[3])
            stores.append(
                pltpu.make_async_copy(
                    proj_ref.at[:, lanes], proj_hbm.at[pair, part], sent.at[part, pair]
                )
            )
            stores[-1].start()
    mask = same_patch(2 * block_rows, block_rows, patches // PARTS)
    slab = 2 * width // HEADS
    scale = (width // HEADS) ** -0.5
    for pair in range(HEADS // 2):
        at = pair * slab
        for part in range(PARTS):
            own = pl.ds(part * block_rows, block_rows)
            query = proj_ref[own, at : at + slab]
            keys = proj_ref[own, width + at : width + at + slab]
            values = proj_ref[own, 2 * width + at : 2 * width + at + slab]
            scores = jnp.where(mask, dot(stacked(query), keys, NT) * scale, -jnp.inf)
            weights = jnp.exp(scores - jnp.max(scores, axis=1, keepdims=True))
            probs = (weights / jnp.sum(weights, axis=1, keepdims=True)).astype(BF16)
            attended = dot(side_by_side(probs), stacked(values)).astype(BF16).astype(F32)
            total[:, at : at + slab] += jnp.sum(attended, axis=0, keepdims=True)
    tiles = row_tiles(total[...])
    for copy in range(pool_ref.shape[0]):
        pool_ref[copy] = tiles
    for store in stores:
        store.wait()


def forward(tokens, gain, w_project, patches, copies):
    width = tokens.shape[-1]
    rows = tokens.size // width
    parts = 3
    return pl.pallas_call(
        lambda *refs: forward_kernel(patches, *refs),
        in_specs=[VMEM, VMEM, HBM],
        out_specs=[HBM, HBM, HBM, VMEM],
        out_shape=(
            far_shape((rows, width), BF16),
            far_shape((rows, width), BF16),
            far_shape((HEADS // 2, 3, rows, 2 * width // HEADS), BF16),
            jax.ShapeDtypeStruct((copies, 8, width // 8), F32),
        ),
        scratch_shapes=[
            pltpu.VMEM((rows, width), BF16),
            pltpu.VMEM((rows, width), BF16),
            pltpu.VMEM((rows, 3 * width), BF16),
            pltpu.VMEM((1, width), F32),
            pltpu.SemaphoreType.DMA((parts + 1, HEADS // 2)),
            pltpu.VMEM(w_project.shape, BF16),
            pltpu.SemaphoreType.DMA((parts,)),
        ],
        compiler_params=params(32),
        cost_estimate=cost(10 * rows * width * width, 10 * MIB, HEADS * rows * rows),
    )(tokens, gain, far(w_project))


def flip_kernel(*refs):
    *sources, target = refs
    at = 0
    for source in sources:
        rows, width = source.shape
        step = 256
        for start in range(0, width, step):
            target[start : start + step, at : at + rows] = source[:, start : start + step].T
        at += rows


def flip(*arrays):
    shape = (arrays[0].shape[1], sum(a.shape[0] for a in arrays))
    return pl.pallas_call(
        flip_kernel,
        in_specs=[VMEM] * len(arrays),
        out_shape=jax.ShapeDtypeStruct(shape, BF16),
        compiler_params=params(56),
        cost_estimate=cost(0, 4 * shape[0] * shape[1]),
    )(*arrays)


def attend_kernel(patches, proj_ref, rounded, norm):
    rows = rounded.shape[3]
    mask = same_patch(2 * rows, rows, patches // PARTS)
    scale = (proj_ref.shape[3] // 2) ** -0.5
    for pair in range(HEADS // 2):
        for part in range(PARTS):
            own = pl.ds(part * rows, rows)
            query = proj_ref[pair, 0, own]
            keys = proj_ref[pair, 1, own]
            scores = jnp.where(mask, dot(stacked(keys), query, NT) * scale, -jnp.inf)
            for head in range(2):
                score = scores[head * rows : (head + 1) * rows]
                weights = jnp.exp(score - jnp.max(score, axis=0, keepdims=True))
                probs = (weights / jnp.sum(weights, axis=0, keepdims=True)).astype(BF16)
                rounded[pair, part, head * rows : (head + 1) * rows] = probs
                number = (pair * PARTS + part) * 2 + head
                norm[number : number + 1] = 1.0 / jnp.sum(
                    probs.astype(F32), axis=0, keepdims=True
                )


def attend(projected, patches):
    rows = projected.shape[2] // PARTS
    pairs = HEADS // 2
    return pl.pallas_call(
        lambda *refs: attend_kernel(patches, *refs),
        in_specs=[VMEM],
        out_shape=(
            jax.ShapeDtypeStruct((pairs, PARTS, 2 * rows, rows), BF16),
            jax.ShapeDtypeStruct((HEADS * PARTS, rows), F32),
        ),
        compiler_params=params(56),
        cost_estimate=cost(8 * rows * rows * projected.shape[3], 6 * MIB, HEADS * rows * rows),
    )(projected)


def total_share(parts_ref, count):
    return tiles_row(jnp.sum(parts_ref[...], axis=0)) / count


def backward_kernel(
    block,
    count,
    core_ref,
    frame_ref,
    x_hbm,
    proj_hbm,
    gathered_hbm,
    parts_ref,
    rounded_hbm,
    norm_ref,
    gain_ref,
    w_hbm,
    keep_hbm,
    send_hbm,
    token_ref,
    gain_out,
    proj_grad,
    sorted_grad,
    w_ref,
    received,
    grad_ref,
    x_ref,
    proj_ref,
    rounded,
    arrived,
    ready,
):
    rows, width = grad_ref.shape
    block_rows = rows // PARTS
    load = pltpu.make_async_copy(gathered_hbm.at[:, frame_ref[0]], received, arrived.at[3])
    load.start()
    pairs = []
    for pair in range(HEADS // 2):
        pairs.append(
            [
                pltpu.make_async_copy(proj_hbm.at[pair], proj_ref.at[pair], ready.at[pair, 0]),
                pltpu.make_async_copy(rounded_hbm.at[pair], rounded.at[pair], ready.at[pair, 1]),
            ]
        )
        for pair_load in pairs[-1]:
            pair_load.start()
    x_load = pltpu.make_async_copy(x_hbm, x_ref, arrived.at[4])
    x_load.start()
    w_load = pltpu.make_async_copy(w_hbm, w_ref, arrived.at[0])
    w_load.start()
    load.wait()
    frames, size, _ = received.shape
    run = token_ref.shape[2] * PARTS // size
    size = size // PARTS
    for part in range(PARTS):
        for first in range(0, frames, run):
            pieces = [
                received[frame, part * size : (part + 1) * size].astype(F32)
                for frame in range(first, first + run)
            ]
            start = part * block_rows + first * size
            grad_ref[start : start + run * size] = jnp.concatenate(pieces, axis=0).astype(BF16)
    share = tiles_row(jnp.sum(parts_ref[...], axis=0)) / count
    slab = 2 * width // HEADS
    scale = (width // HEADS) ** -0.5
    for pair in range(HEADS // 2):
        at = pair * slab
        if pair % 2 == 0:
            for pair_load in pairs[pair] + pairs[pair + 1]:
                pair_load.wait()
        for part in range(PARTS):
            own = pl.ds(part * block_rows, block_rows)
            query = proj_ref[pair, 0, own]
            keys = proj_ref[pair, 1, own]
            values = proj_ref[pair, 2, own]
            grads = grad_ref[own, at : at + slab].astype(F32) + share[:, at : at + slab]
            grads = grads.astype(BF16)
            probs = rounded[pair, part]
            prob_grad = dot(stacked(values), grads, NT)
            score_grads = []
            for head in range(2):
                mine = slice(head * block_rows, (head + 1) * block_rows)
                number = (pair * PARTS + part) * 2 + head
                weights = probs[mine].astype(F32)
                moved = prob_grad[mine]
                mean = jnp.sum(weights * moved, axis=0, keepdims=True)
                mean = mean * norm_ref[number : number + 1]
                score_grads.append((weights * (moved - mean) * scale).astype(BF16))
            key_grad = dot(jnp.concatenate(score_grads, 1), stacked(query))
            query_grad = dot(jnp.concatenate(score_grads, 0), stacked(keys), TN)
            value_grad = dot(side_by_side(probs), stacked(grads))
            for first, grad in zip((0, width, 2 * width), (query_grad, key_grad, value_grad)):
                start = first + at
                grad = grad.astype(BF16)
                proj_grad[own, start : start + slab] = grad
                number, inside = divmod(start, block)
                owner, place = number % 2, number // 2 * block + inside
                sorted_grad[core_ref[0] ^ owner, own, place : place + slab] = grad

    stores = [
        pltpu.make_async_copy(sorted_grad.at[number], target, arrived.at[1 + number])
        for number, target in enumerate((keep_hbm, send_hbm))
    ]
    for store in stores:
        store.start()
    x_load.wait()
    w_load.wait()
    normed_grad = dot(proj_grad[...], w_ref[...])
    standard, spread = standardize(x_ref[...].astype(F32))
    gain_out[...] = row_tiles(jnp.sum(normed_grad * standard, axis=0, keepdims=True))
    scaled = normed_grad * gain_ref[...]
    centered = (
        scaled
        - jnp.mean(scaled, axis=-1, keepdims=True)
        - standard * jnp.mean(scaled * standard, axis=-1, keepdims=True)
    )
    total_grad = grad_ref[...].astype(F32) + share
    token_grad = (total_grad + spread * centered).astype(BF16)
    owners, _, size, _ = token_ref.shape
    for part in range(PARTS):
        for owner in range(owners):
            start = part * block_rows + owner * size
            token_ref[owner, part] = token_grad[start : start + size]
    for store in stores:
        store.wait()


def backward(
    core,
    index,
    tokens,
    projected,
    gathered,
    share_parts,
    rounded,
    norm,
    gain,
    w_flipped,
    block,
    count,
    owners,
):
    rows, width = tokens.shape
    half = jax.ShapeDtypeStruct((rows, 3 * width // 2), BF16)
    return pl.pallas_call(
        lambda *refs: backward_kernel(block, count, *refs),
        in_specs=[SMEM, SMEM, HBM, HBM, HBM, VMEM, HBM, VMEM, VMEM, HBM],
        out_specs=[HBM, HBM, VMEM, VMEM],
        out_shape=(
            half,
            half,
            far_shape((owners, PARTS, rows // (owners * PARTS), width), BF16),
            jax.ShapeDtypeStruct((8, width // 8), F32),
        ),
        scratch_shapes=[
            pltpu.VMEM((rows, 3 * width), BF16),
            pltpu.VMEM((2, rows, 3 * width // 2), BF16),
            pltpu.VMEM(w_flipped.shape, BF16),
            pltpu.VMEM(gathered.shape[:1] + gathered.shape[2:], BF16),
            pltpu.VMEM((rows, width), BF16),
            pltpu.VMEM(tokens.shape, BF16),
            pltpu.VMEM(projected.shape, BF16),
            pltpu.VMEM(rounded.shape, BF16),
            pltpu.SemaphoreType.DMA((5,)),
            pltpu.SemaphoreType.DMA((HEADS // 2, 2)),
        ],
        compiler_params=params(52),
        cost_estimate=cost(14 * rows * rows * width, 12 * MIB),
    )(
        core,
        index,
        far(tokens),
        far(projected),
        far(gathered),
        share_parts,
        far(rounded),
        norm,
        gain,
        far(w_flipped),
    )


def split_sum(tiles):
    high = tiles.astype(BF16).astype(F32)
    return jnp.concatenate([high, tiles - high], axis=0).astype(BF16)


def weight_kernel(
    halves, flipped, grad_hbm, other_ref, gain_hbm, other_gain, out_ref, grad_ref, gain_ref, arrived
):
    groups, total_rows, lanes = out_ref.shape
    width = flipped.shape[0]
    rows, cols = grad_ref.shape
    block = width // (groups * halves)
    steps = arrived.shape[0] - 1
    cols = cols // steps
    tiles = cols // lanes
    span = tiles * halves * block
    spans = [pl.ds(step * cols, cols) for step in range(steps)]
    loads = [
        pltpu.make_async_copy(grad_hbm.at[:, at], grad_ref.at[:, at], arrived.at[step])
        for step, at in enumerate(spans)
    ]
    loads.append(pltpu.make_async_copy(gain_hbm, gain_ref, arrived.at[steps]))
    for load in loads:
        load.start()
    for step, at in enumerate(spans):
        loads[step].wait()
        both = jnp.concatenate([grad_ref[:, at], other_ref[:, at]], axis=0)
        terms = dot(flipped[...], both).astype(BF16)
        for tile in range(tiles):
            for half in range(halves):
                for group in range(groups):
                    start = (half * groups + group) * block
                    place = step * span + (tile * halves + half) * block
                    out_ref[group, place : place + block] = terms[
                        start : start + block, tile * lanes : (tile + 1) * lanes
                    ]
    loads[steps].wait()
    tail = split_sum(gain_ref[...] + other_gain[...])
    for group in range(groups):
        out_ref[group, steps * span :] = tail


def weight_terms(flipped, grads, other_grads, gain, other_gain, groups, halves, steps):
    width, rows = flipped.shape
    lanes = 128
    shape = (groups, width // groups * grads.shape[1] // lanes + 16, lanes)
    return pl.pallas_call(
        lambda *refs: weight_kernel(halves, *refs),
        in_specs=[VMEM, HBM, VMEM, HBM, VMEM],
        out_specs=VMEM,
        out_shape=near_shape(shape, BF16),
        scratch_shapes=[
            pltpu.VMEM(grads.shape, BF16),
            pltpu.VMEM(gain.shape, F32),
            pltpu.SemaphoreType.DMA((steps + 1,)),
        ],
        compiler_params=params(24),
        cost_estimate=cost(2 * rows * width * grads.shape[1], 6 * MIB),
    )(flipped, far(grads), other_grads, far(gain), other_gain)


def regroup_kernel(block, terms_ref, out_ref):
    halves, steps, rows, _ = out_ref.shape
    tiles = (rows - 16) // block
    total = jnp.sum(terms_ref[...].astype(F32), axis=0)
    terms = total.astype(BF16)
    end = total.shape[0] - 16
    gains = split_sum(total[end : end + 8] + total[end + 8 :])
    for half in range(halves):
        for step in range(steps):
            for tile in range(tiles):
                start = ((step * tiles + tile) * halves + half) * block
                out_ref[half, step, tile * block : (tile + 1) * block] = terms[
                    start : start + block
                ]
            out_ref[half, step, tiles * block :] = gains


def regroup(terms, halves, steps, block):
    count, rows, lanes = terms.shape
    shape = (halves, steps, (rows - 16) // (halves * steps) + 16, lanes)
    return pl.pallas_call(
        lambda *refs: regroup_kernel(block, *refs),
        in_specs=[VMEM],
        out_shape=jax.ShapeDtypeStruct(shape, BF16),
        compiler_params=params(32),
        cost_estimate=cost(terms.size, 4 * MIB),
    )(terms)


def finish_kernel(terms_ref, out_ref, gain_ref):
    total = jnp.sum(terms_ref[...].astype(F32), axis=0)
    block = out_ref.shape[0]
    lanes = total.shape[1]
    for tile in range(out_ref.shape[1] // lanes):
        out_ref[:, tile * lanes : (tile + 1) * lanes] = total[tile * block : (tile + 1) * block]
    end = total.shape[0] - 16
    gain_ref[...] = tiles_row(total[end : end + 8] + total[end + 8 :])


def finish(terms, block):
    count, rows, lanes = terms.shape
    return pl.pallas_call(
        finish_kernel,
        in_specs=[VMEM],
        out_shape=(
            jax.ShapeDtypeStruct((block, (rows - 16) // block * lanes), F32),
            jax.ShapeDtypeStruct((1, 8 * lanes), F32),
        ),
        compiler_params=params(16),
        cost_estimate=cost(terms.size, MIB),
    )(terms)


def pool_kernel(halves, tokens, parts_ref, out_ref):
    per_clip = parts_ref.shape[0] // halves
    means = []
    for half in range(halves):
        pooled = jnp.sum(parts_ref[half * per_clip : (half + 1) * per_clip], axis=0) / tokens
        means.append(pooled)
    means = jnp.concatenate(means, axis=0).astype(BF16)
    for copy in range(out_ref.shape[0]):
        out_ref[copy] = means


def pool(parts, halves, tokens, copies):
    return pl.pallas_call(
        lambda *refs: pool_kernel(halves, tokens, *refs),
        in_specs=[VMEM],
        out_shape=jax.ShapeDtypeStruct((copies, halves * parts.shape[1], parts.shape[2]), BF16),
        compiler_params=params(8),
        cost_estimate=cost(parts.size, MIB),
    )(parts)


def embed_kernel(halves, pooled_ref, w_ref, pooled_out, centered_ref, gram_ref, rows_ref):
    groups, tiles, lanes = pooled_ref.shape
    tiles = tiles // halves
    means = pooled_ref[...].astype(F32)
    for half in range(halves):
        for tile in range(tiles):
            rows_ref[half * groups : (half + 1) * groups, tile * lanes : (tile + 1) * lanes] = (
                means[:, half * tiles + tile, :]
            )
    pooled = rows_ref[...].astype(BF16)
    pooled_out[...] = pooled
    embedding = dot(pooled, w_ref[...])
    centered = embedding - jnp.mean(embedding, axis=0, keepdims=True)
    centered_ref[...] = centered
    gram = dot(centered, centered, NT, lax.Precision.HIGHEST)
    size = gram_ref.shape[1]
    gram = [gram[i : i + size] for i in range(0, gram.shape[0], size)]
    gram = jnp.concatenate(gram, axis=1)
    for copy in range(gram_ref.shape[0]):
        gram_ref[copy] = gram


def embed(pooled, w_expand, copies, halves):
    clips = pooled.shape[0] * halves
    width, columns = w_expand.shape
    return pl.pallas_call(
        lambda *refs: embed_kernel(halves, *refs),
        in_specs=[VMEM, VMEM],
        out_shape=(
            jax.ShapeDtypeStruct((clips, width), BF16),
            jax.ShapeDtypeStruct((clips, columns), F32),
            jax.ShapeDtypeStruct((copies, min(clips, 8), clips * clips // min(clips, 8)), F32),
        ),
        scratch_shapes=[pltpu.VMEM((clips, width), F32)],
        compiler_params=params(16),
        cost_estimate=cost(2 * clips * w_expand.size, 2 * MIB),
    )(pooled, w_expand)


def embed_grad_kernel(coefficient, own_ref, gram_ref, centered_ref, w_ref, grad_ref, pool_ref):
    clips = centered_ref.shape[0]
    centered = centered_ref[...]
    gram = jnp.sum(gram_ref[...], axis=0)
    gram = [gram[:, i : i + clips] for i in range(0, gram.shape[1], clips)]
    gram = jnp.concatenate(gram, axis=0)
    variances = jnp.sum(centered * centered, axis=0, keepdims=True) / (clips - 1)
    mixed = dot(gram, centered, precision=lax.Precision.HIGHEST)
    grads = coefficient * (mixed / (clips - 1) - centered * variances)
    grad_ref[...] = grads.astype(BF16)
    row = lax.broadcasted_iota(jnp.int32, grads.shape, 0)
    own = jnp.sum(jnp.where(row == own_ref[0], grads, 0.0), axis=0, keepdims=True)
    own = jnp.broadcast_to(own, (16, own.shape[1])).astype(BF16)
    part = row_tiles(dot(own, w_ref[...], NT)[0:1])
    for copy in range(pool_ref.shape[0]):
        pool_ref[copy] = part


def embed_grads(own_index, gram_parts, centered, w_expand, coefficient):
    width = w_expand.shape[0]
    return pl.pallas_call(
        lambda *refs: embed_grad_kernel(coefficient, *refs),
        in_specs=[SMEM, VMEM, VMEM, VMEM],
        out_shape=(
            jax.ShapeDtypeStruct(centered.shape, BF16),
            jax.ShapeDtypeStruct((gram_parts.shape[0], 8, width // 8), F32),
        ),
        compiler_params=params(16),
        cost_estimate=cost(2 * 16 * w_expand.size, 2 * MIB),
    )(own_index, gram_parts, centered, w_expand)


DP = ("zh", "x", "y")
FRAME = ("zl", "core")
SIZES = {"zh": 2, "x": 4, "y": 4, "zl": 4, "core": 2}
SWAP = [(0, 1), (1, 0)]


def to_each(array, axis):
    return lax.all_to_all(array, axis, split_axis=0, concat_axis=0, tiled=True)


def per_device(clip_tokens, out_grad, ln_gain, w_project, w_expand):
    frame_count = lax.axis_size(FRAME)
    clip_count = lax.axis_size(DP)
    halves, steps = lax.axis_size("zh"), lax.axis_size("zl")
    plane = lax.axis_size(("x", "y"))
    core = lax.axis_index("core").reshape(1)
    own_frame = lax.axis_index(FRAME).reshape(1)
    own_clip = lax.axis_index(DP)
    frames_dev, patches, width = clip_tokens.shape[1:]
    patches_dev = patches // frame_count
    rows = frames_dev * patches
    tokens_clip = frames_dev * frame_count * patches
    column_block = 3 * width // frame_count
    block_rows = width // clip_count
    gain = ln_gain[None, :]

    w_flipped = flip(w_project)
    tokens = to_each(pack(clip_tokens[0], frame_count), FRAME)
    out_grad, tokens, w_flipped = lax.optimization_barrier((out_grad, tokens, w_flipped))
    gathered = lax.all_gather(out_grad[0], FRAME, axis=0, tiled=True)
    tokens, normed, projected, pool_parts = forward(
        tokens, gain, w_project, patches_dev, halves * frame_count
    )
    other_normed = lax.ppermute(normed, "core", SWAP)

    pool_parts = to_each(pool_parts, ("zh",) + FRAME)
    pooled = to_each(pool(pool_parts, halves, tokens_clip, plane), ("x", "y"))
    rounded, norm = attend(projected, patches_dev)
    pooled, rounded, norm = lax.optimization_barrier((pooled, rounded, norm))
    pooled_all, centered, gram_parts = embed(pooled, w_expand, frame_count, halves)
    gram_parts = to_each(gram_parts, FRAME)
    flipped = flip(normed, other_normed)
    gram_parts, flipped = lax.optimization_barrier((gram_parts, flipped))
    coefficient = 100.0 * tokens_clip / (w_expand.shape[1] * frame_count * (clip_count - 1))
    embed_grad, share_parts = embed_grads(
        own_clip.reshape(1), gram_parts, centered, w_expand, coefficient
    )
    share_parts = to_each(share_parts, FRAME)
    row_part = lax.dynamic_slice_in_dim(pooled_all, own_clip * block_rows, block_rows, 1)
    expand_grad = dot(row_part, embed_grad, TN)

    gathered, _ = lax.optimization_barrier((gathered, gram_parts))
    gathered = gathered.reshape(-1, frame_count, patches_dev, width)

    kept, outgoing, token_part, gain_part = backward(
        core,
        own_frame,
        tokens,
        projected,
        gathered,
        share_parts,
        rounded,
        norm,
        gain,
        w_flipped,
        column_block,
        tokens_clip,
        frame_count,
    )
    token_parts = lax.all_gather(token_part, FRAME)
    incoming, other_gain = lax.ppermute((outgoing, gain_part), "core", SWAP)
    terms = weight_terms(
        flipped, kept, incoming, gain_part, other_gain, plane, halves, steps
    )
    terms = to_each(terms, ("x", "y"))
    terms = regroup(terms, halves, steps, block_rows)
    terms = to_each(terms.reshape((-1,) + terms.shape[2:]), ("zh", "zl"))
    token_grad = place(own_frame, token_parts, frames_dev)[None]
    terms, token_grad = lax.optimization_barrier((terms, token_grad))
    project_grad, gain_grad = finish(terms, block_rows)
    return (token_grad, project_grad, expand_grad, gain_grad[0])


def solution(mesh):
    split = jax.sharding.Mesh(
        mesh.devices.reshape(tuple(SIZES.values())), tuple(SIZES)
    )
    return jax.shard_map(
        per_device,
        mesh=split,
        in_specs=(
            P(DP, FRAME, None, None),
            P(DP, FRAME, None, None),
            P(),
            P(),
            P(None, FRAME),
        ),
        out_specs=(P(DP, FRAME, None, None), P(DP, FRAME), P(DP, FRAME), P()),
        check_vma=False,
    )
```

```python
import jax
import jax.numpy as jnp
from jax import lax
from jax.experimental import pallas as pl
from jax.experimental.pallas import tpu as pltpu
from jax.sharding import PartitionSpec as P

HEADS = 16
PARTS = 2
EPSILON = 1e-05
F32 = jnp.float32
BF16 = jnp.bfloat16
MIB = 1 << 20
NT = (((1,), (1,)), ((), ()))
TN = (((0,), (0,)), ((), ()))


def dot(a, b, dims=(((1,), (0,)), ((), ())), precision=None):
    return lax.dot_general(a, b, dims, precision=precision, preferred_element_type=F32)


def standardize(inputs):
    center = inputs - jnp.mean(inputs, axis=-1, keepdims=True)
    spread = lax.rsqrt(jnp.mean(center * center, axis=-1, keepdims=True) + EPSILON)
    return center * spread, spread


def far(array):
    return pltpu.with_memory_space_constraint(array, pltpu.HBM)


def far_shape(shape, dtype):
    return pltpu.HBM(shape, dtype)


def near_shape(shape, dtype):
    return pltpu.VMEM(shape, dtype)


VMEM = pl.BlockSpec(memory_space=pltpu.VMEM)
SMEM = pl.BlockSpec(memory_space=pltpu.SMEM)
HBM = pl.BlockSpec(memory_space=pltpu.HBM)


def params(mib):
    return pltpu.CompilerParams(vmem_limit_bytes=mib * MIB)


def cost(flops, moved, exps=0):
    return pl.CostEstimate(flops=flops, bytes_accessed=moved, transcendentals=exps)


def pack_kernel(source, packed):
    groups, parts, rows, _ = packed.shape
    frames = source.shape[0]
    size = rows // frames
    for group in range(groups):
        for part in range(parts):
            at = (group * parts + part) * size
            pieces = [source[frame, at : at + size].astype(F32) for frame in range(frames)]
            packed[group, part] = jnp.concatenate(pieces, axis=0).astype(BF16)


def pack(array, groups):
    frames, patches, width = array.shape
    rows = frames * patches // (groups * PARTS)
    return pl.pallas_call(
        pack_kernel,
        out_shape=jax.ShapeDtypeStruct((groups, PARTS, rows, width), array.dtype),
        compiler_params=params(8),
        cost_estimate=cost(0, 4 * array.size),
    )(array)


def place_kernel(index_ref, source, target, own, arrived):
    load = pltpu.make_async_copy(source.at[:, index_ref[0]], own, arrived.at[0])
    load.start()
    load.wait()
    frames = target.shape[0]
    groups, parts, rows, _ = own.shape
    size = rows // frames
    for group in range(groups):
        for frame in range(frames):
            pieces = [
                own[group, part, frame * size : (frame + 1) * size].astype(F32)
                for part in range(parts)
            ]
            target[frame, group] = jnp.concatenate(pieces, axis=0).astype(BF16)


def place(index, gathered, frames):
    groups, _, parts, rows, width = gathered.shape
    size = parts * rows // frames
    placed = pl.pallas_call(
        place_kernel,
        in_specs=[SMEM, HBM],
        out_specs=VMEM,
        out_shape=jax.ShapeDtypeStruct((frames, groups, size, width), BF16),
        scratch_shapes=[
            pltpu.VMEM((groups, parts, rows, width), BF16),
            pltpu.SemaphoreType.DMA((1,)),
        ],
        compiler_params=params(8),
        cost_estimate=cost(0, 4 * groups * parts * rows * width),
    )(index, far(gathered))
    return placed.reshape(frames, groups * size, width)


def row_tiles(row):
    tile = row.shape[1] // 8
    return jnp.concatenate([row[:, i * tile : (i + 1) * tile] for i in range(8)], axis=0)


def tiles_row(tiles):
    return jnp.concatenate([tiles[i : i + 1] for i in range(tiles.shape[0])], axis=1)


def lane_halves(slab):
    lane = lax.broadcasted_iota(jnp.int32, slab.shape, 1)
    low = lane < slab.shape[1] // 2
    zero = jnp.zeros_like(slab)
    return jnp.where(low, slab, zero), jnp.where(low, zero, slab)


def same_patch(rows, columns, patches):
    first = lax.broadcasted_iota(jnp.int32, (rows, columns), 0)
    second = lax.broadcasted_iota(jnp.int32, (rows, columns), 1)
    return lax.rem(first, patches) == lax.rem(second, patches)


def stacked(slab):
    return jnp.concatenate(lane_halves(slab), axis=0)


def side_by_side(array):
    rows = array.shape[0] // 2
    return jnp.concatenate([array[:rows], array[rows:]], axis=1)


def forward_kernel(
    patches,
    x_ref,
    gain_ref,
    w_hbm,
    inputs_hbm,
    normed_hbm,
    proj_hbm,
    pool_ref,
    inputs_ref,
    normed_ref,
    proj_ref,
    total,
    sent,
    w_ref,
    arrived,
):
    rows, width = normed_ref.shape
    block_rows = rows // PARTS
    parts = sent.shape[0] - 1
    chunk = w_ref.shape[1] // parts
    chunks = [pl.ds(part * chunk, chunk) for part in range(parts)]
    loads = [
        pltpu.make_async_copy(w_hbm.at[:, cols], w_ref.at[:, cols], arrived.at[part])
        for part, cols in enumerate(chunks)
    ]
    for load in loads:
        load.start()
    for part in range(PARTS):
        block = x_ref[:, part]
        inputs_ref[part * block_rows : (part + 1) * block_rows] = block.reshape(block_rows, width)
    stores = [pltpu.make_async_copy(inputs_ref, inputs_hbm, sent.at[parts, 1])]
    stores[-1].start()
    inputs = inputs_ref[...].astype(F32)
    standard, _ = standardize(inputs)
    normed = (standard * gain_ref[...]).astype(BF16)
    normed_ref[...] = normed
    stores.append(pltpu.make_async_copy(normed_ref, normed_hbm, sent.at[parts, 0]))
    stores[-1].start()
    total[...] = jnp.sum(inputs, axis=0, keepdims=True)
    for part, cols in enumerate(chunks):
        loads[part].wait()
        proj_ref[:, cols] = dot(normed, w_ref[:, cols]).astype(BF16)
        for pair in range(proj_hbm.shape[0]):
            lanes = pl.ds(part * chunk + pair * proj_hbm.shape[3], proj_hbm.shape[3])
            stores.append(
                pltpu.make_async_copy(
                    proj_ref.at[:, lanes], proj_hbm.at[pair, part], sent.at[part, pair]
                )
            )
            stores[-1].start()
    mask = same_patch(2 * block_rows, block_rows, patches // PARTS)
    slab = 2 * width // HEADS
    scale = (width // HEADS) ** -0.5
    for pair in range(HEADS // 2):
        at = pair * slab
        for part in range(PARTS):
            own = pl.ds(part * block_rows, block_rows)
            query = proj_ref[own, at : at + slab]
            keys = proj_ref[own, width + at : width + at + slab]
            values = proj_ref[own, 2 * width + at : 2 * width + at + slab]
            scores = jnp.where(mask, dot(stacked(query), keys, NT) * scale, -jnp.inf)
            weights = jnp.exp(scores - jnp.max(scores, axis=1, keepdims=True))
            probs = (weights / jnp.sum(weights, axis=1, keepdims=True)).astype(BF16)
            attended = dot(side_by_side(probs), stacked(values)).astype(BF16).astype(F32)
            total[:, at : at + slab] += jnp.sum(attended, axis=0, keepdims=True)
    tiles = row_tiles(total[...])
    for copy in range(pool_ref.shape[0]):
        pool_ref[copy] = tiles
    for store in stores:
        store.wait()


def forward(tokens, gain, w_project, patches, copies):
    width = tokens.shape[-1]
    rows = tokens.size // width
    parts = 3
    return pl.pallas_call(
        lambda *refs: forward_kernel(patches, *refs),
        in_specs=[VMEM, VMEM, HBM],
        out_specs=[HBM, HBM, HBM, VMEM],
        out_shape=(
            far_shape((rows, width), BF16),
            far_shape((rows, width), BF16),
            far_shape((HEADS // 2, 3, rows, 2 * width // HEADS), BF16),
            jax.ShapeDtypeStruct((copies, 8, width // 8), F32),
        ),
        scratch_shapes=[
            pltpu.VMEM((rows, width), BF16),
            pltpu.VMEM((rows, width), BF16),
            pltpu.VMEM((rows, 3 * width), BF16),
            pltpu.VMEM((1, width), F32),
            pltpu.SemaphoreType.DMA((parts + 1, HEADS // 2)),
            pltpu.VMEM(w_project.shape, BF16),
            pltpu.SemaphoreType.DMA((parts,)),
        ],
        compiler_params=params(32),
        cost_estimate=cost(10 * rows * width * width, 10 * MIB, HEADS * rows * rows),
    )(tokens, gain, far(w_project))


def flip_kernel(*refs):
    *sources, target = refs
    at = 0
    for source in sources:
        rows, width = source.shape
        step = 256
        for start in range(0, width, step):
            target[start : start + step, at : at + rows] = source[:, start : start + step].T
        at += rows


def flip(*arrays):
    shape = (arrays[0].shape[1], sum(a.shape[0] for a in arrays))
    return pl.pallas_call(
        flip_kernel,
        in_specs=[VMEM] * len(arrays),
        out_shape=jax.ShapeDtypeStruct(shape, BF16),
        compiler_params=params(56),
        cost_estimate=cost(0, 4 * shape[0] * shape[1]),
    )(*arrays)


def attend_kernel(patches, proj_ref, rounded, norm):
    rows = rounded.shape[3]
    mask = same_patch(2 * rows, rows, patches // PARTS)
    scale = (proj_ref.shape[3] // 2) ** -0.5
    for pair in range(HEADS // 2):
        for part in range(PARTS):
            own = pl.ds(part * rows, rows)
            query = proj_ref[pair, 0, own]
            keys = proj_ref[pair, 1, own]
            scores = jnp.where(mask, dot(stacked(keys), query, NT) * scale, -jnp.inf)
            for head in range(2):
                score = scores[head * rows : (head + 1) * rows]
                weights = jnp.exp(score - jnp.max(score, axis=0, keepdims=True))
                probs = (weights / jnp.sum(weights, axis=0, keepdims=True)).astype(BF16)
                rounded[pair, part, head * rows : (head + 1) * rows] = probs
                number = (pair * PARTS + part) * 2 + head
                norm[number : number + 1] = 1.0 / jnp.sum(
                    probs.astype(F32), axis=0, keepdims=True
                )


def attend(projected, patches):
    rows = projected.shape[2] // PARTS
    pairs = HEADS // 2
    return pl.pallas_call(
        lambda *refs: attend_kernel(patches, *refs),
        in_specs=[VMEM],
        out_shape=(
            jax.ShapeDtypeStruct((pairs, PARTS, 2 * rows, rows), BF16),
            jax.ShapeDtypeStruct((HEADS * PARTS, rows), F32),
        ),
        compiler_params=params(56),
        cost_estimate=cost(8 * rows * rows * projected.shape[3], 6 * MIB, HEADS * rows * rows),
    )(projected)


def total_share(parts_ref, count):
    return tiles_row(jnp.sum(parts_ref[...], axis=0)) / count


def backward_kernel(
    block,
    count,
    core_ref,
    frame_ref,
    x_hbm,
    proj_hbm,
    gathered_hbm,
    parts_ref,
    rounded_hbm,
    norm_ref,
    gain_ref,
    w_hbm,
    keep_hbm,
    send_hbm,
    token_ref,
    gain_out,
    proj_grad,
    sorted_grad,
    w_ref,
    received,
    grad_ref,
    x_ref,
    proj_ref,
    rounded,
    arrived,
    ready,
):
    rows, width = grad_ref.shape
    block_rows = rows // PARTS
    load = pltpu.make_async_copy(gathered_hbm.at[:, frame_ref[0]], received, arrived.at[3])
    load.start()
    pairs = []
    for pair in range(HEADS // 2):
        pairs.append(
            [
                pltpu.make_async_copy(proj_hbm.at[pair], proj_ref.at[pair], ready.at[pair, 0]),
                pltpu.make_async_copy(rounded_hbm.at[pair], rounded.at[pair], ready.at[pair, 1]),
            ]
        )
        for pair_load in pairs[-1]:
            pair_load.start()
    x_load = pltpu.make_async_copy(x_hbm, x_ref, arrived.at[4])
    x_load.start()
    w_load = pltpu.make_async_copy(w_hbm, w_ref, arrived.at[0])
    w_load.start()
    load.wait()
    frames, size, _ = received.shape
    run = token_ref.shape[2] * PARTS // size
    size = size // PARTS
    for part in range(PARTS):
        for first in range(0, frames, run):
            pieces = [
                received[frame, part * size : (part + 1) * size].astype(F32)
                for frame in range(first, first + run)
            ]
            start = part * block_rows + first * size
            grad_ref[start : start + run * size] = jnp.concatenate(pieces, axis=0).astype(BF16)
    share = tiles_row(jnp.sum(parts_ref[...], axis=0)) / count
    slab = 2 * width // HEADS
    scale = (width // HEADS) ** -0.5
    for pair in range(HEADS // 2):
        at = pair * slab
        if pair % 2 == 0:
            for pair_load in pairs[pair] + pairs[pair + 1]:
                pair_load.wait()
        for part in range(PARTS):
            own = pl.ds(part * block_rows, block_rows)
            query = proj_ref[pair, 0, own]
            keys = proj_ref[pair, 1, own]
            values = proj_ref[pair, 2, own]
            grads = grad_ref[own, at : at + slab].astype(F32) + share[:, at : at + slab]
            grads = grads.astype(BF16)
            probs = rounded[pair, part]
            prob_grad = dot(stacked(values), grads, NT)
            score_grads = []
            for head in range(2):
                mine = slice(head * block_rows, (head + 1) * block_rows)
                number = (pair * PARTS + part) * 2 + head
                weights = probs[mine].astype(F32)
                moved = prob_grad[mine]
                mean = jnp.sum(weights * moved, axis=0, keepdims=True)
                mean = mean * norm_ref[number : number + 1]
                score_grads.append((weights * (moved - mean) * scale).astype(BF16))
            key_grad = dot(jnp.concatenate(score_grads, 1), stacked(query))
            query_grad = dot(jnp.concatenate(score_grads, 0), stacked(keys), TN)
            value_grad = dot(side_by_side(probs), stacked(grads))
            for first, grad in zip((0, width, 2 * width), (query_grad, key_grad, value_grad)):
                start = first + at
                grad = grad.astype(BF16)
                proj_grad[own, start : start + slab] = grad
                number, inside = divmod(start, block)
                owner, place = number % 2, number // 2 * block + inside
                sorted_grad[core_ref[0] ^ owner, own, place : place + slab] = grad

    stores = [
        pltpu.make_async_copy(sorted_grad.at[number], target, arrived.at[1 + number])
        for number, target in enumerate((keep_hbm, send_hbm))
    ]
    for store in stores:
        store.start()
    x_load.wait()
    w_load.wait()
    normed_grad = dot(proj_grad[...], w_ref[...])
    standard, spread = standardize(x_ref[...].astype(F32))
    gain_out[...] = row_tiles(jnp.sum(normed_grad * standard, axis=0, keepdims=True))
    scaled = normed_grad * gain_ref[...]
    centered = (
        scaled
        - jnp.mean(scaled, axis=-1, keepdims=True)
        - standard * jnp.mean(scaled * standard, axis=-1, keepdims=True)
    )
    total_grad = grad_ref[...].astype(F32) + share
    token_grad = (total_grad + spread * centered).astype(BF16)
    owners, _, size, _ = token_ref.shape
    for part in range(PARTS):
        for owner in range(owners):
            start = part * block_rows + owner * size
            token_ref[owner, part] = token_grad[start : start + size]
    for store in stores:
        store.wait()


def backward(
    core,
    index,
    tokens,
    projected,
    gathered,
    share_parts,
    rounded,
    norm,
    gain,
    w_flipped,
    block,
    count,
    owners,
):
    rows, width = tokens.shape
    half = jax.ShapeDtypeStruct((rows, 3 * width // 2), BF16)
    return pl.pallas_call(
        lambda *refs: backward_kernel(block, count, *refs),
        in_specs=[SMEM, SMEM, HBM, HBM, HBM, VMEM, HBM, VMEM, VMEM, HBM],
        out_specs=[HBM, HBM, VMEM, VMEM],
        out_shape=(
            half,
            half,
            far_shape((owners, PARTS, rows // (owners * PARTS), width), BF16),
            jax.ShapeDtypeStruct((8, width // 8), F32),
        ),
        scratch_shapes=[
            pltpu.VMEM((rows, 3 * width), BF16),
            pltpu.VMEM((2, rows, 3 * width // 2), BF16),
            pltpu.VMEM(w_flipped.shape, BF16),
            pltpu.VMEM(gathered.shape[:1] + gathered.shape[2:], BF16),
            pltpu.VMEM((rows, width), BF16),
            pltpu.VMEM(tokens.shape, BF16),
            pltpu.VMEM(projected.shape, BF16),
            pltpu.VMEM(rounded.shape, BF16),
            pltpu.SemaphoreType.DMA((5,)),
            pltpu.SemaphoreType.DMA((HEADS // 2, 2)),
        ],
        compiler_params=params(52),
        cost_estimate=cost(14 * rows * rows * width, 12 * MIB),
    )(
        core,
        index,
        far(tokens),
        far(projected),
        far(gathered),
        share_parts,
        far(rounded),
        norm,
        gain,
        far(w_flipped),
    )


def split_sum(tiles):
    high = tiles.astype(BF16).astype(F32)
    return jnp.concatenate([high, tiles - high], axis=0).astype(BF16)


def weight_kernel(
    halves, steps, flipped, grad_ref, other_ref, gain_ref, other_gain, out_ref
):
    groups, total_rows, lanes = out_ref.shape
    width = flipped.shape[0]
    rows, cols = grad_ref.shape
    block = width // (groups * halves)
    cols = cols // steps
    tiles = cols // lanes
    span = tiles * halves * block
    spans = [pl.ds(step * cols, cols) for step in range(steps)]
    for step, at in enumerate(spans):
        both = jnp.concatenate([grad_ref[:, at], other_ref[:, at]], axis=0)
        terms = dot(flipped[...], both).astype(BF16)
        for tile in range(tiles):
            for half in range(halves):
                for group in range(groups):
                    start = (half * groups + group) * block
                    place = step * span + (tile * halves + half) * block
                    out_ref[group, place : place + block] = terms[
                        start : start + block, tile * lanes : (tile + 1) * lanes
                    ]
    tail = split_sum(gain_ref[...] + other_gain[...])
    for group in range(groups):
        out_ref[group, steps * span :] = tail


def weight_terms(flipped, grads, other_grads, gain, other_gain, groups, halves, steps):
    width, rows = flipped.shape
    lanes = 128
    shape = (groups, width // groups * grads.shape[1] // lanes + 16, lanes)
    return pl.pallas_call(
        lambda *refs: weight_kernel(halves, steps, *refs),
        in_specs=[VMEM] * 5,
        out_specs=VMEM,
        out_shape=near_shape(shape, BF16),
        compiler_params=params(24),
        cost_estimate=cost(2 * rows * width * grads.shape[1], 6 * MIB),
    )(flipped, grads, other_grads, gain, other_gain)


def regroup_kernel(block, terms_ref, out_ref):
    halves, steps, rows, _ = out_ref.shape
    tiles = (rows - 16) // block
    total = jnp.sum(terms_ref[...].astype(F32), axis=0)
    terms = total.astype(BF16)
    end = total.shape[0] - 16
    gains = split_sum(total[end : end + 8] + total[end + 8 :])
    for half in range(halves):
        for step in range(steps):
            for tile in range(tiles):
                start = ((step * tiles + tile) * halves + half) * block
                out_ref[half, step, tile * block : (tile + 1) * block] = terms[
                    start : start + block
                ]
            out_ref[half, step, tiles * block :] = gains


def regroup(terms, halves, steps, block):
    count, rows, lanes = terms.shape
    shape = (halves, steps, (rows - 16) // (halves * steps) + 16, lanes)
    return pl.pallas_call(
        lambda *refs: regroup_kernel(block, *refs),
        in_specs=[VMEM],
        out_shape=jax.ShapeDtypeStruct(shape, BF16),
        compiler_params=params(32),
        cost_estimate=cost(terms.size, 4 * MIB),
    )(terms)


def finish_kernel(terms_ref, out_ref, gain_ref):
    total = jnp.sum(terms_ref[...].astype(F32), axis=0)
    block = out_ref.shape[0]
    lanes = total.shape[1]
    for tile in range(out_ref.shape[1] // lanes):
        out_ref[:, tile * lanes : (tile + 1) * lanes] = total[tile * block : (tile + 1) * block]
    end = total.shape[0] - 16
    gain_ref[...] = tiles_row(total[end : end + 8] + total[end + 8 :])


def finish(terms, block):
    count, rows, lanes = terms.shape
    return pl.pallas_call(
        finish_kernel,
        in_specs=[VMEM],
        out_shape=(
            jax.ShapeDtypeStruct((block, (rows - 16) // block * lanes), F32),
            jax.ShapeDtypeStruct((1, 8 * lanes), F32),
        ),
        compiler_params=params(16),
        cost_estimate=cost(terms.size, MIB),
    )(terms)


def pool_kernel(halves, tokens, parts_ref, out_ref):
    per_clip = parts_ref.shape[0] // halves
    means = []
    for half in range(halves):
        pooled = jnp.sum(parts_ref[half * per_clip : (half + 1) * per_clip], axis=0) / tokens
        means.append(pooled)
    means = jnp.concatenate(means, axis=0).astype(BF16)
    for copy in range(out_ref.shape[0]):
        out_ref[copy] = means


def pool(parts, halves, tokens, copies):
    return pl.pallas_call(
        lambda *refs: pool_kernel(halves, tokens, *refs),
        in_specs=[VMEM],
        out_shape=jax.ShapeDtypeStruct((copies, halves * parts.shape[1], parts.shape[2]), BF16),
        compiler_params=params(8),
        cost_estimate=cost(parts.size, MIB),
    )(parts)


def embed_kernel(halves, pooled_ref, w_ref, pooled_out, centered_ref, gram_ref, rows_ref):
    groups, tiles, lanes = pooled_ref.shape
    tiles = tiles // halves
    means = pooled_ref[...].astype(F32)
    for half in range(halves):
        for tile in range(tiles):
            rows_ref[half * groups : (half + 1) * groups, tile * lanes : (tile + 1) * lanes] = (
                means[:, half * tiles + tile, :]
            )
    pooled = rows_ref[...].astype(BF16)
    pooled_out[...] = pooled
    embedding = dot(pooled, w_ref[...])
    centered = embedding - jnp.mean(embedding, axis=0, keepdims=True)
    centered_ref[...] = centered
    gram = dot(centered, centered, NT, lax.Precision.HIGHEST)
    size = gram_ref.shape[1]
    gram = [gram[i : i + size] for i in range(0, gram.shape[0], size)]
    gram = jnp.concatenate(gram, axis=1)
    for copy in range(gram_ref.shape[0]):
        gram_ref[copy] = gram


def embed(pooled, w_expand, copies, halves):
    clips = pooled.shape[0] * halves
    width, columns = w_expand.shape
    return pl.pallas_call(
        lambda *refs: embed_kernel(halves, *refs),
        in_specs=[VMEM, VMEM],
        out_shape=(
            jax.ShapeDtypeStruct((clips, width), BF16),
            jax.ShapeDtypeStruct((clips, columns), F32),
            jax.ShapeDtypeStruct((copies, min(clips, 8), clips * clips // min(clips, 8)), F32),
        ),
        scratch_shapes=[pltpu.VMEM((clips, width), F32)],
        compiler_params=params(16),
        cost_estimate=cost(2 * clips * w_expand.size, 2 * MIB),
    )(pooled, w_expand)


def embed_grad_kernel(coefficient, own_ref, gram_ref, centered_ref, w_ref, grad_ref, pool_ref):
    clips = centered_ref.shape[0]
    centered = centered_ref[...]
    gram = jnp.sum(gram_ref[...], axis=0)
    gram = [gram[:, i : i + clips] for i in range(0, gram.shape[1], clips)]
    gram = jnp.concatenate(gram, axis=0)
    variances = jnp.sum(centered * centered, axis=0, keepdims=True) / (clips - 1)
    mixed = dot(gram, centered, precision=lax.Precision.HIGHEST)
    grads = coefficient * (mixed / (clips - 1) - centered * variances)
    grad_ref[...] = grads.astype(BF16)
    row = lax.broadcasted_iota(jnp.int32, grads.shape, 0)
    own = jnp.sum(jnp.where(row == own_ref[0], grads, 0.0), axis=0, keepdims=True)
    own = jnp.broadcast_to(own, (16, own.shape[1])).astype(BF16)
    part = row_tiles(dot(own, w_ref[...], NT)[0:1])
    for copy in range(pool_ref.shape[0]):
        pool_ref[copy] = part


def embed_grads(own_index, gram_parts, centered, w_expand, coefficient):
    width = w_expand.shape[0]
    return pl.pallas_call(
        lambda *refs: embed_grad_kernel(coefficient, *refs),
        in_specs=[SMEM, VMEM, VMEM, VMEM],
        out_shape=(
            jax.ShapeDtypeStruct(centered.shape, BF16),
            jax.ShapeDtypeStruct((gram_parts.shape[0], 8, width // 8), F32),
        ),
        compiler_params=params(16),
        cost_estimate=cost(2 * 16 * w_expand.size, 2 * MIB),
    )(own_index, gram_parts, centered, w_expand)


DP = ("zh", "x", "y")
FRAME = ("zl", "core")
SIZES = {"zh": 2, "x": 4, "y": 4, "zl": 4, "core": 2}
SWAP = [(0, 1), (1, 0)]


def to_each(array, axis):
    return lax.all_to_all(array, axis, split_axis=0, concat_axis=0, tiled=True)


def per_device(clip_tokens, out_grad, ln_gain, w_project, w_expand):
    frame_count = lax.axis_size(FRAME)
    clip_count = lax.axis_size(DP)
    halves, steps = lax.axis_size("zh"), lax.axis_size("zl")
    plane = lax.axis_size(("x", "y"))
    core = lax.axis_index("core").reshape(1)
    own_frame = lax.axis_index(FRAME).reshape(1)
    own_clip = lax.axis_index(DP)
    frames_dev, patches, width = clip_tokens.shape[1:]
    patches_dev = patches // frame_count
    rows = frames_dev * patches
    tokens_clip = frames_dev * frame_count * patches
    column_block = 3 * width // frame_count
    block_rows = width // clip_count
    gain = ln_gain[None, :]

    w_flipped = flip(w_project)
    tokens = to_each(pack(clip_tokens[0], frame_count), FRAME)
    out_grad, tokens, w_flipped = lax.optimization_barrier((out_grad, tokens, w_flipped))
    gathered = lax.all_gather(out_grad[0], FRAME, axis=0, tiled=True)
    tokens, normed, projected, pool_parts = forward(
        tokens, gain, w_project, patches_dev, halves * frame_count
    )
    other_normed = lax.ppermute(normed, "core", SWAP)

    pool_parts = to_each(pool_parts, ("zh",) + FRAME)
    pooled = to_each(pool(pool_parts, halves, tokens_clip, plane), ("x", "y"))
    rounded, norm = attend(projected, patches_dev)
    pooled, rounded, norm = lax.optimization_barrier((pooled, rounded, norm))
    pooled_all, centered, gram_parts = embed(pooled, w_expand, frame_count, halves)
    gram_parts = to_each(gram_parts, FRAME)
    flipped = flip(normed, other_normed)
    gram_parts, flipped = lax.optimization_barrier((gram_parts, flipped))
    coefficient = 100.0 * tokens_clip / (w_expand.shape[1] * frame_count * (clip_count - 1))
    embed_grad, share_parts = embed_grads(
        own_clip.reshape(1), gram_parts, centered, w_expand, coefficient
    )
    share_parts = to_each(share_parts, FRAME)
    row_part = lax.dynamic_slice_in_dim(pooled_all, own_clip * block_rows, block_rows, 1)
    expand_grad = dot(row_part, embed_grad, TN)

    gathered, _ = lax.optimization_barrier((gathered, gram_parts))
    gathered = gathered.reshape(-1, frame_count, patches_dev, width)

    kept, outgoing, token_part, gain_part = backward(
        core,
        own_frame,
        tokens,
        projected,
        gathered,
        share_parts,
        rounded,
        norm,
        gain,
        w_flipped,
        column_block,
        tokens_clip,
        frame_count,
    )
    token_parts = lax.all_gather(token_part, FRAME)
    incoming, other_gain = lax.ppermute((outgoing, gain_part), "core", SWAP)
    terms = weight_terms(
        flipped, kept, incoming, gain_part, other_gain, plane, halves, steps
    )
    terms = to_each(terms, ("x", "y"))
    terms = regroup(terms, halves, steps, block_rows)
    terms = to_each(terms.reshape((-1,) + terms.shape[2:]), ("zh", "zl"))
    token_grad = place(own_frame, token_parts, frames_dev)[None]
    terms, token_grad = lax.optimization_barrier((terms, token_grad))
    project_grad, gain_grad = finish(terms, block_rows)
    return (token_grad, project_grad, expand_grad, gain_grad[0])


def solution(mesh):
    split = jax.sharding.Mesh(
        mesh.devices.reshape(tuple(SIZES.values())), tuple(SIZES)
    )
    return jax.shard_map(
        per_device,
        mesh=split,
        in_specs=(
            P(DP, FRAME, None, None),
            P(DP, FRAME, None, None),
            P(),
            P(),
            P(None, FRAME),
        ),
        out_specs=(P(DP, FRAME, None, None), P(DP, FRAME), P(DP, FRAME), P()),
        check_vma=False,
    )
```

```python
import jax
import jax.numpy as jnp
from jax import lax
from jax.experimental import pallas as pl
from jax.experimental.pallas import tpu as pltpu
from jax.sharding import PartitionSpec as P

HEADS = 16
PARTS = 2
EPSILON = 1e-05
F32 = jnp.float32
BF16 = jnp.bfloat16
MIB = 1 << 20
NT = (((1,), (1,)), ((), ()))
TN = (((0,), (0,)), ((), ()))


def dot(a, b, dims=(((1,), (0,)), ((), ())), precision=None):
    return lax.dot_general(a, b, dims, precision=precision, preferred_element_type=F32)


def standardize(inputs):
    center = inputs - jnp.mean(inputs, axis=-1, keepdims=True)
    spread = lax.rsqrt(jnp.mean(center * center, axis=-1, keepdims=True) + EPSILON)
    return center * spread, spread


def far(array):
    return pltpu.with_memory_space_constraint(array, pltpu.HBM)


def far_shape(shape, dtype):
    return pltpu.HBM(shape, dtype)


def near_shape(shape, dtype):
    return pltpu.VMEM(shape, dtype)


VMEM = pl.BlockSpec(memory_space=pltpu.VMEM)
SMEM = pl.BlockSpec(memory_space=pltpu.SMEM)
HBM = pl.BlockSpec(memory_space=pltpu.HBM)


def params(mib):
    return pltpu.CompilerParams(vmem_limit_bytes=mib * MIB)


def cost(flops, moved, exps=0):
    return pl.CostEstimate(flops=flops, bytes_accessed=moved, transcendentals=exps)


def pack_kernel(source, packed):
    groups, parts, rows, _ = packed.shape
    frames = source.shape[0]
    size = rows // frames
    for group in range(groups):
        for part in range(parts):
            at = (group * parts + part) * size
            pieces = [source[frame, at : at + size].astype(F32) for frame in range(frames)]
            packed[group, part] = jnp.concatenate(pieces, axis=0).astype(BF16)


def pack(array, groups):
    frames, patches, width = array.shape
    rows = frames * patches // (groups * PARTS)
    return pl.pallas_call(
        pack_kernel,
        out_shape=jax.ShapeDtypeStruct((groups, PARTS, rows, width), array.dtype),
        compiler_params=params(8),
        cost_estimate=cost(0, 4 * array.size),
    )(array)


def place_kernel(index_ref, source, target, own, arrived):
    load = pltpu.make_async_copy(source.at[:, index_ref[0]], own, arrived.at[0])
    load.start()
    load.wait()
    frames = target.shape[0]
    groups, parts, rows, _ = own.shape
    size = rows // frames
    for group in range(groups):
        for frame in range(frames):
            pieces = [
                own[group, part, frame * size : (frame + 1) * size].astype(F32)
                for part in range(parts)
            ]
            target[frame, group] = jnp.concatenate(pieces, axis=0).astype(BF16)


def place(index, gathered, frames):
    groups, _, parts, rows, width = gathered.shape
    size = parts * rows // frames
    placed = pl.pallas_call(
        place_kernel,
        in_specs=[SMEM, HBM],
        out_specs=VMEM,
        out_shape=jax.ShapeDtypeStruct((frames, groups, size, width), BF16),
        scratch_shapes=[
            pltpu.VMEM((groups, parts, rows, width), BF16),
            pltpu.SemaphoreType.DMA((1,)),
        ],
        compiler_params=params(8),
        cost_estimate=cost(0, 4 * groups * parts * rows * width),
    )(index, far(gathered))
    return placed.reshape(frames, groups * size, width)


def row_tiles(row):
    tile = row.shape[1] // 8
    return jnp.concatenate([row[:, i * tile : (i + 1) * tile] for i in range(8)], axis=0)


def tiles_row(tiles):
    return jnp.concatenate([tiles[i : i + 1] for i in range(tiles.shape[0])], axis=1)


def lane_halves(slab):
    lane = lax.broadcasted_iota(jnp.int32, slab.shape, 1)
    low = lane < slab.shape[1] // 2
    zero = jnp.zeros_like(slab)
    return jnp.where(low, slab, zero), jnp.where(low, zero, slab)


def same_patch(rows, columns, patches):
    first = lax.broadcasted_iota(jnp.int32, (rows, columns), 0)
    second = lax.broadcasted_iota(jnp.int32, (rows, columns), 1)
    return lax.rem(first, patches) == lax.rem(second, patches)


def stacked(slab):
    return jnp.concatenate(lane_halves(slab), axis=0)


def side_by_side(array):
    rows = array.shape[0] // 2
    return jnp.concatenate([array[:rows], array[rows:]], axis=1)


def forward_kernel(
    patches,
    x_ref,
    gain_ref,
    w_hbm,
    inputs_hbm,
    normed_hbm,
    proj_hbm,
    pool_ref,
    inputs_ref,
    normed_ref,
    proj_ref,
    total,
    sent,
    w_ref,
    arrived,
):
    rows, width = normed_ref.shape
    block_rows = rows // PARTS
    parts = sent.shape[0] - 1
    chunk = w_ref.shape[1] // parts
    chunks = [pl.ds(part * chunk, chunk) for part in range(parts)]
    loads = [
        pltpu.make_async_copy(w_hbm.at[:, cols], w_ref.at[:, cols], arrived.at[part])
        for part, cols in enumerate(chunks)
    ]
    for load in loads:
        load.start()
    for part in range(PARTS):
        block = x_ref[:, part]
        inputs_ref[part * block_rows : (part + 1) * block_rows] = block.reshape(block_rows, width)
    stores = [pltpu.make_async_copy(inputs_ref, inputs_hbm, sent.at[parts, 1])]
    stores[-1].start()
    inputs = inputs_ref[...].astype(F32)
    standard, _ = standardize(inputs)
    normed = (standard * gain_ref[...]).astype(BF16)
    normed_ref[...] = normed
    stores.append(pltpu.make_async_copy(normed_ref, normed_hbm, sent.at[parts, 0]))
    stores[-1].start()
    total[...] = jnp.sum(inputs, axis=0, keepdims=True)
    for part, cols in enumerate(chunks):
        loads[part].wait()
        proj_ref[:, cols] = dot(normed, w_ref[:, cols]).astype(BF16)
        for pair in range(proj_hbm.shape[0]):
            lanes = pl.ds(part * chunk + pair * proj_hbm.shape[3], proj_hbm.shape[3])
            stores.append(
                pltpu.make_async_copy(
                    proj_ref.at[:, lanes], proj_hbm.at[pair, part], sent.at[part, pair]
                )
            )
            stores[-1].start()
    mask = same_patch(2 * block_rows, block_rows, patches // PARTS)
    slab = 2 * width // HEADS
    scale = (width // HEADS) ** -0.5
    for pair in range(HEADS // 2):
        at = pair * slab
        for part in range(PARTS):
            own = pl.ds(part * block_rows, block_rows)
            query = proj_ref[own, at : at + slab]
            keys = proj_ref[own, width + at : width + at + slab]
            values = proj_ref[own, 2 * width + at : 2 * width + at + slab]
            scores = jnp.where(mask, dot(stacked(query), keys, NT) * scale, -jnp.inf)
            weights = jnp.exp(scores - jnp.max(scores, axis=1, keepdims=True))
            probs = (weights / jnp.sum(weights, axis=1, keepdims=True)).astype(BF16)
            attended = dot(side_by_side(probs), stacked(values)).astype(BF16).astype(F32)
            total[:, at : at + slab] += jnp.sum(attended, axis=0, keepdims=True)
    tiles = row_tiles(total[...])
    for copy in range(pool_ref.shape[0]):
        pool_ref[copy] = tiles
    for store in stores:
        store.wait()


def forward(tokens, gain, w_project, patches, copies):
    width = tokens.shape[-1]
    rows = tokens.size // width
    parts = 3
    return pl.pallas_call(
        lambda *refs: forward_kernel(patches, *refs),
        in_specs=[VMEM, VMEM, HBM],
        out_specs=[HBM, HBM, HBM, VMEM],
        out_shape=(
            far_shape((rows, width), BF16),
            far_shape((rows, width), BF16),
            far_shape((HEADS // 2, 3, rows, 2 * width // HEADS), BF16),
            jax.ShapeDtypeStruct((copies, 8, width // 8), F32),
        ),
        scratch_shapes=[
            pltpu.VMEM((rows, width), BF16),
            pltpu.VMEM((rows, width), BF16),
            pltpu.VMEM((rows, 3 * width), BF16),
            pltpu.VMEM((1, width), F32),
            pltpu.SemaphoreType.DMA((parts + 1, HEADS // 2)),
            pltpu.VMEM(w_project.shape, BF16),
            pltpu.SemaphoreType.DMA((parts,)),
        ],
        compiler_params=params(32),
        cost_estimate=cost(10 * rows * width * width, 10 * MIB, HEADS * rows * rows),
    )(tokens, gain, far(w_project))


def flip_kernel(*refs):
    *sources, target = refs
    at = 0
    for source in sources:
        rows, width = source.shape
        step = 256
        for start in range(0, width, step):
            target[start : start + step, at : at + rows] = source[:, start : start + step].T
        at += rows


def flip(*arrays):
    shape = (arrays[0].shape[1], sum(a.shape[0] for a in arrays))
    return pl.pallas_call(
        flip_kernel,
        in_specs=[VMEM] * len(arrays),
        out_shape=jax.ShapeDtypeStruct(shape, BF16),
        compiler_params=params(50),
        cost_estimate=cost(0, 4 * shape[0] * shape[1]),
    )(*arrays)


def attend_kernel(patches, proj_ref, rounded, norm):
    rows = rounded.shape[3]
    mask = same_patch(2 * rows, rows, patches // PARTS)
    scale = (proj_ref.shape[3] // 2) ** -0.5
    for pair in range(HEADS // 2):
        for part in range(PARTS):
            own = pl.ds(part * rows, rows)
            query = proj_ref[pair, 0, own]
            keys = proj_ref[pair, 1, own]
            scores = jnp.where(mask, dot(stacked(keys), query, NT) * scale, -jnp.inf)
            for head in range(2):
                score = scores[head * rows : (head + 1) * rows]
                weights = jnp.exp(score - jnp.max(score, axis=0, keepdims=True))
                probs = (weights / jnp.sum(weights, axis=0, keepdims=True)).astype(BF16)
                rounded[pair, part, head * rows : (head + 1) * rows] = probs
                number = (pair * PARTS + part) * 2 + head
                norm[number : number + 1] = 1.0 / jnp.sum(
                    probs.astype(F32), axis=0, keepdims=True
                )


def attend(projected, patches):
    rows = projected.shape[2] // PARTS
    pairs = HEADS // 2
    return pl.pallas_call(
        lambda *refs: attend_kernel(patches, *refs),
        in_specs=[VMEM],
        out_shape=(
            jax.ShapeDtypeStruct((pairs, PARTS, 2 * rows, rows), BF16),
            jax.ShapeDtypeStruct((HEADS * PARTS, rows), F32),
        ),
        compiler_params=params(50),
        cost_estimate=cost(8 * rows * rows * projected.shape[3], 6 * MIB, HEADS * rows * rows),
    )(projected)


def total_share(parts_ref, count):
    return tiles_row(jnp.sum(parts_ref[...], axis=0)) / count


def backward_kernel(
    block,
    count,
    core_ref,
    frame_ref,
    x_hbm,
    proj_hbm,
    gathered_hbm,
    parts_ref,
    rounded_hbm,
    norm_ref,
    gain_ref,
    w_hbm,
    keep_hbm,
    send_hbm,
    token_ref,
    gain_out,
    proj_grad,
    sorted_grad,
    w_ref,
    received,
    grad_ref,
    x_ref,
    proj_ref,
    rounded,
    arrived,
    ready,
):
    rows, width = grad_ref.shape
    block_rows = rows // PARTS
    load = pltpu.make_async_copy(gathered_hbm.at[:, frame_ref[0]], received, arrived.at[3])
    load.start()
    pairs = []
    for pair in range(HEADS // 2):
        pairs.append(
            [
                pltpu.make_async_copy(proj_hbm.at[pair], proj_ref.at[pair], ready.at[pair, 0]),
                pltpu.make_async_copy(rounded_hbm.at[pair], rounded.at[pair], ready.at[pair, 1]),
            ]
        )
        for pair_load in pairs[-1]:
            pair_load.start()
    x_load = pltpu.make_async_copy(x_hbm, x_ref, arrived.at[4])
    x_load.start()
    w_load = pltpu.make_async_copy(w_hbm, w_ref, arrived.at[0])
    w_load.start()
    load.wait()
    frames, size, _ = received.shape
    run = token_ref.shape[2] * PARTS // size
    size = size // PARTS
    for part in range(PARTS):
        for first in range(0, frames, run):
            pieces = [
                received[frame, part * size : (part + 1) * size].astype(F32)
                for frame in range(first, first + run)
            ]
            start = part * block_rows + first * size
            grad_ref[start : start + run * size] = jnp.concatenate(pieces, axis=0).astype(BF16)
    share = tiles_row(jnp.sum(parts_ref[...], axis=0)) / count
    slab = 2 * width // HEADS
    scale = (width // HEADS) ** -0.5
    for pair in range(HEADS // 2):
        at = pair * slab
        if pair % 2 == 0:
            for pair_load in pairs[pair] + pairs[pair + 1]:
                pair_load.wait()
        for part in range(PARTS):
            own = pl.ds(part * block_rows, block_rows)
            query = proj_ref[pair, 0, own]
            keys = proj_ref[pair, 1, own]
            values = proj_ref[pair, 2, own]
            grads = grad_ref[own, at : at + slab].astype(F32) + share[:, at : at + slab]
            grads = grads.astype(BF16)
            probs = rounded[pair, part]
            prob_grad = dot(stacked(values), grads, NT)
            score_grads = []
            for head in range(2):
                mine = slice(head * block_rows, (head + 1) * block_rows)
                number = (pair * PARTS + part) * 2 + head
                weights = probs[mine].astype(F32)
                moved = prob_grad[mine]
                mean = jnp.sum(weights * moved, axis=0, keepdims=True)
                mean = mean * norm_ref[number : number + 1]
                score_grads.append((weights * (moved - mean) * scale).astype(BF16))
            key_grad = dot(jnp.concatenate(score_grads, 1), stacked(query))
            query_grad = dot(jnp.concatenate(score_grads, 0), stacked(keys), TN)
            value_grad = dot(side_by_side(probs), stacked(grads))
            for first, grad in zip((0, width, 2 * width), (query_grad, key_grad, value_grad)):
                start = first + at
                grad = grad.astype(BF16)
                proj_grad[own, start : start + slab] = grad
                number, inside = divmod(start, block)
                owner, place = number % 2, number // 2 * block + inside
                sorted_grad[core_ref[0] ^ owner, own, place : place + slab] = grad

    stores = [
        pltpu.make_async_copy(sorted_grad.at[number], target, arrived.at[1 + number])
        for number, target in enumerate((keep_hbm, send_hbm))
    ]
    for store in stores:
        store.start()
    x_load.wait()
    w_load.wait()
    normed_grad = dot(proj_grad[...], w_ref[...])
    standard, spread = standardize(x_ref[...].astype(F32))
    gain_out[...] = row_tiles(jnp.sum(normed_grad * standard, axis=0, keepdims=True))
    scaled = normed_grad * gain_ref[...]
    centered = (
        scaled
        - jnp.mean(scaled, axis=-1, keepdims=True)
        - standard * jnp.mean(scaled * standard, axis=-1, keepdims=True)
    )
    total_grad = grad_ref[...].astype(F32) + share
    token_grad = (total_grad + spread * centered).astype(BF16)
    owners, _, size, _ = token_ref.shape
    for part in range(PARTS):
        for owner in range(owners):
            start = part * block_rows + owner * size
            token_ref[owner, part] = token_grad[start : start + size]
    for store in stores:
        store.wait()


def backward(
    core,
    index,
    tokens,
    projected,
    gathered,
    share_parts,
    rounded,
    norm,
    gain,
    w_flipped,
    block,
    count,
    owners,
):
    rows, width = tokens.shape
    half = jax.ShapeDtypeStruct((rows, 3 * width // 2), BF16)
    return pl.pallas_call(
        lambda *refs: backward_kernel(block, count, *refs),
        in_specs=[SMEM, SMEM, HBM, HBM, HBM, VMEM, HBM, VMEM, VMEM, HBM],
        out_specs=[HBM, HBM, VMEM, VMEM],
        out_shape=(
            half,
            half,
            far_shape((owners, PARTS, rows // (owners * PARTS), width), BF16),
            jax.ShapeDtypeStruct((8, width // 8), F32),
        ),
        scratch_shapes=[
            pltpu.VMEM((rows, 3 * width), BF16),
            pltpu.VMEM((2, rows, 3 * width // 2), BF16),
            pltpu.VMEM(w_flipped.shape, BF16),
            pltpu.VMEM(gathered.shape[:1] + gathered.shape[2:], BF16),
            pltpu.VMEM((rows, width), BF16),
            pltpu.VMEM(tokens.shape, BF16),
            pltpu.VMEM(projected.shape, BF16),
            pltpu.VMEM(rounded.shape, BF16),
            pltpu.SemaphoreType.DMA((5,)),
            pltpu.SemaphoreType.DMA((HEADS // 2, 2)),
        ],
        compiler_params=params(52),
        cost_estimate=cost(14 * rows * rows * width, 12 * MIB),
    )(
        core,
        index,
        far(tokens),
        far(projected),
        far(gathered),
        share_parts,
        far(rounded),
        norm,
        gain,
        far(w_flipped),
    )


def split_sum(tiles):
    high = tiles.astype(BF16).astype(F32)
    return jnp.concatenate([high, tiles - high], axis=0).astype(BF16)


def weight_kernel(
    halves, steps, flipped, grad_ref, other_ref, gain_ref, other_gain, out_ref
):
    groups, total_rows, lanes = out_ref.shape
    width = flipped.shape[0]
    rows, cols = grad_ref.shape
    block = width // (groups * halves)
    cols = cols // steps
    tiles = cols // lanes
    span = tiles * halves * block
    spans = [pl.ds(step * cols, cols) for step in range(steps)]
    for step, at in enumerate(spans):
        both = jnp.concatenate([grad_ref[:, at], other_ref[:, at]], axis=0)
        terms = dot(flipped[...], both).astype(BF16)
        for tile in range(tiles):
            for half in range(halves):
                for group in range(groups):
                    start = (half * groups + group) * block
                    place = step * span + (tile * halves + half) * block
                    out_ref[group, place : place + block] = terms[
                        start : start + block, tile * lanes : (tile + 1) * lanes
                    ]
    tail = split_sum(gain_ref[...] + other_gain[...])
    for group in range(groups):
        out_ref[group, steps * span :] = tail


def weight_terms(flipped, grads, other_grads, gain, other_gain, groups, halves, steps):
    width, rows = flipped.shape
    lanes = 128
    shape = (groups, width // groups * grads.shape[1] // lanes + 16, lanes)
    return pl.pallas_call(
        lambda *refs: weight_kernel(halves, steps, *refs),
        in_specs=[VMEM] * 5,
        out_specs=VMEM,
        out_shape=near_shape(shape, BF16),
        compiler_params=params(24),
        cost_estimate=cost(2 * rows * width * grads.shape[1], 6 * MIB),
    )(flipped, grads, other_grads, gain, other_gain)


def regroup_kernel(block, terms_ref, out_ref):
    halves, steps, rows, _ = out_ref.shape
    tiles = (rows - 16) // block
    total = jnp.sum(terms_ref[...].astype(F32), axis=0)
    terms = total.astype(BF16)
    end = total.shape[0] - 16
    gains = split_sum(total[end : end + 8] + total[end + 8 :])
    for half in range(halves):
        for step in range(steps):
            for tile in range(tiles):
                start = ((step * tiles + tile) * halves + half) * block
                out_ref[half, step, tile * block : (tile + 1) * block] = terms[
                    start : start + block
                ]
            out_ref[half, step, tiles * block :] = gains


def regroup(terms, halves, steps, block):
    count, rows, lanes = terms.shape
    shape = (halves, steps, (rows - 16) // (halves * steps) + 16, lanes)
    return pl.pallas_call(
        lambda *refs: regroup_kernel(block, *refs),
        in_specs=[VMEM],
        out_shape=jax.ShapeDtypeStruct(shape, BF16),
        compiler_params=params(32),
        cost_estimate=cost(terms.size, 4 * MIB),
    )(terms)


def finish_kernel(terms_ref, out_ref, gain_ref):
    total = jnp.sum(terms_ref[...].astype(F32), axis=0)
    block = out_ref.shape[0]
    lanes = total.shape[1]
    for tile in range(out_ref.shape[1] // lanes):
        out_ref[:, tile * lanes : (tile + 1) * lanes] = total[tile * block : (tile + 1) * block]
    end = total.shape[0] - 16
    gain_ref[...] = tiles_row(total[end : end + 8] + total[end + 8 :])


def finish(terms, block):
    count, rows, lanes = terms.shape
    return pl.pallas_call(
        finish_kernel,
        in_specs=[VMEM],
        out_shape=(
            jax.ShapeDtypeStruct((block, (rows - 16) // block * lanes), F32),
            jax.ShapeDtypeStruct((1, 8 * lanes), F32),
        ),
        compiler_params=params(16),
        cost_estimate=cost(terms.size, MIB),
    )(terms)


def pool_kernel(halves, tokens, parts_ref, out_ref):
    per_clip = parts_ref.shape[0] // halves
    means = []
    for half in range(halves):
        pooled = jnp.sum(parts_ref[half * per_clip : (half + 1) * per_clip], axis=0) / tokens
        means.append(pooled)
    means = jnp.concatenate(means, axis=0).astype(BF16)
    for copy in range(out_ref.shape[0]):
        out_ref[copy] = means


def pool(parts, halves, tokens, copies):
    return pl.pallas_call(
        lambda *refs: pool_kernel(halves, tokens, *refs),
        in_specs=[VMEM],
        out_shape=jax.ShapeDtypeStruct((copies, halves * parts.shape[1], parts.shape[2]), BF16),
        compiler_params=params(8),
        cost_estimate=cost(parts.size, MIB),
    )(parts)


def embed_kernel(halves, pooled_ref, w_ref, pooled_out, centered_ref, gram_ref, rows_ref):
    groups, tiles, lanes = pooled_ref.shape
    tiles = tiles // halves
    means = pooled_ref[...].astype(F32)
    for half in range(halves):
        for tile in range(tiles):
            rows_ref[half * groups : (half + 1) * groups, tile * lanes : (tile + 1) * lanes] = (
                means[:, half * tiles + tile, :]
            )
    pooled = rows_ref[...].astype(BF16)
    pooled_out[...] = pooled
    embedding = dot(pooled, w_ref[...])
    centered = embedding - jnp.mean(embedding, axis=0, keepdims=True)
    centered_ref[...] = centered
    gram = dot(centered, centered, NT, lax.Precision.HIGHEST)
    size = gram_ref.shape[1]
    gram = [gram[i : i + size] for i in range(0, gram.shape[0], size)]
    gram = jnp.concatenate(gram, axis=1)
    for copy in range(gram_ref.shape[0]):
        gram_ref[copy] = gram


def embed(pooled, w_expand, copies, halves):
    clips = pooled.shape[0] * halves
    width, columns = w_expand.shape
    return pl.pallas_call(
        lambda *refs: embed_kernel(halves, *refs),
        in_specs=[VMEM, VMEM],
        out_shape=(
            jax.ShapeDtypeStruct((clips, width), BF16),
            jax.ShapeDtypeStruct((clips, columns), F32),
            jax.ShapeDtypeStruct((copies, min(clips, 8), clips * clips // min(clips, 8)), F32),
        ),
        scratch_shapes=[pltpu.VMEM((clips, width), F32)],
        compiler_params=params(16),
        cost_estimate=cost(2 * clips * w_expand.size, 2 * MIB),
    )(pooled, w_expand)


def embed_grad_kernel(coefficient, own_ref, gram_ref, centered_ref, w_ref, grad_ref, pool_ref):
    clips = centered_ref.shape[0]
    centered = centered_ref[...]
    gram = jnp.sum(gram_ref[...], axis=0)
    gram = [gram[:, i : i + clips] for i in range(0, gram.shape[1], clips)]
    gram = jnp.concatenate(gram, axis=0)
    variances = jnp.sum(centered * centered, axis=0, keepdims=True) / (clips - 1)
    mixed = dot(gram, centered, precision=lax.Precision.HIGHEST)
    grads = coefficient * (mixed / (clips - 1) - centered * variances)
    grad_ref[...] = grads.astype(BF16)
    row = lax.broadcasted_iota(jnp.int32, grads.shape, 0)
    own = jnp.sum(jnp.where(row == own_ref[0], grads, 0.0), axis=0, keepdims=True)
    own = jnp.broadcast_to(own, (16, own.shape[1])).astype(BF16)
    part = row_tiles(dot(own, w_ref[...], NT)[0:1])
    for copy in range(pool_ref.shape[0]):
        pool_ref[copy] = part


def embed_grads(own_index, gram_parts, centered, w_expand, coefficient):
    width = w_expand.shape[0]
    return pl.pallas_call(
        lambda *refs: embed_grad_kernel(coefficient, *refs),
        in_specs=[SMEM, VMEM, VMEM, VMEM],
        out_shape=(
            jax.ShapeDtypeStruct(centered.shape, BF16),
            jax.ShapeDtypeStruct((gram_parts.shape[0], 8, width // 8), F32),
        ),
        compiler_params=params(16),
        cost_estimate=cost(2 * 16 * w_expand.size, 2 * MIB),
    )(own_index, gram_parts, centered, w_expand)


DP = ("zh", "x", "y")
FRAME = ("zl", "core")
SIZES = {"zh": 2, "x": 4, "y": 4, "zl": 4, "core": 2}
SWAP = [(0, 1), (1, 0)]


def to_each(array, axis):
    return lax.all_to_all(array, axis, split_axis=0, concat_axis=0, tiled=True)


def per_device(clip_tokens, out_grad, ln_gain, w_project, w_expand):
    frame_count = lax.axis_size(FRAME)
    clip_count = lax.axis_size(DP)
    halves, steps = lax.axis_size("zh"), lax.axis_size("zl")
    plane = lax.axis_size(("x", "y"))
    core = lax.axis_index("core").reshape(1)
    own_frame = lax.axis_index(FRAME).reshape(1)
    own_clip = lax.axis_index(DP)
    frames_dev, patches, width = clip_tokens.shape[1:]
    patches_dev = patches // frame_count
    rows = frames_dev * patches
    tokens_clip = frames_dev * frame_count * patches
    column_block = 3 * width // frame_count
    block_rows = width // clip_count
    gain = ln_gain[None, :]

    w_flipped = flip(w_project)
    tokens = to_each(pack(clip_tokens[0], frame_count), FRAME)
    out_grad, tokens, w_flipped = lax.optimization_barrier((out_grad, tokens, w_flipped))
    gathered = lax.all_gather(out_grad[0], FRAME, axis=0, tiled=True)
    tokens, normed, projected, pool_parts = forward(
        tokens, gain, w_project, patches_dev, halves * frame_count
    )
    other_normed = lax.ppermute(normed, "core", SWAP)

    pool_parts = to_each(pool_parts, ("zh",) + FRAME)
    pooled = to_each(pool(pool_parts, halves, tokens_clip, plane), ("x", "y"))
    rounded, norm = attend(projected, patches_dev)
    pooled, rounded, norm = lax.optimization_barrier((pooled, rounded, norm))
    pooled_all, centered, gram_parts = embed(pooled, w_expand, frame_count, halves)
    gram_parts = to_each(gram_parts, FRAME)
    flipped = flip(normed, other_normed)
    gram_parts, flipped = lax.optimization_barrier((gram_parts, flipped))
    coefficient = 100.0 * tokens_clip / (w_expand.shape[1] * frame_count * (clip_count - 1))
    embed_grad, share_parts = embed_grads(
        own_clip.reshape(1), gram_parts, centered, w_expand, coefficient
    )
    share_parts = to_each(share_parts, FRAME)
    row_part = lax.dynamic_slice_in_dim(pooled_all, own_clip * block_rows, block_rows, 1)
    expand_grad = dot(row_part, embed_grad, TN)

    gathered, _ = lax.optimization_barrier((gathered, gram_parts))
    gathered = gathered.reshape(-1, frame_count, patches_dev, width)

    kept, outgoing, token_part, gain_part = backward(
        core,
        own_frame,
        tokens,
        projected,
        gathered,
        share_parts,
        rounded,
        norm,
        gain,
        w_flipped,
        column_block,
        tokens_clip,
        frame_count,
    )
    token_parts = lax.all_gather(token_part, FRAME)
    incoming, other_gain = lax.ppermute((outgoing, gain_part), "core", SWAP)
    terms = weight_terms(
        flipped, kept, incoming, gain_part, other_gain, plane, halves, steps
    )
    terms = to_each(terms, ("x", "y"))
    terms = regroup(terms, halves, steps, block_rows)
    terms = to_each(terms.reshape((-1,) + terms.shape[2:]), ("zh", "zl"))
    token_grad = place(own_frame, token_parts, frames_dev)[None]
    terms, token_grad = lax.optimization_barrier((terms, token_grad))
    project_grad, gain_grad = finish(terms, block_rows)
    return (token_grad, project_grad, expand_grad, gain_grad[0])


def solution(mesh):
    split = jax.sharding.Mesh(
        mesh.devices.reshape(tuple(SIZES.values())), tuple(SIZES)
    )
    return jax.shard_map(
        per_device,
        mesh=split,
        in_specs=(
            P(DP, FRAME, None, None),
            P(DP, FRAME, None, None),
            P(),
            P(),
            P(None, FRAME),
        ),
        out_specs=(P(DP, FRAME, None, None), P(DP, FRAME), P(DP, FRAME), P()),
        check_vma=False,
    )
```

```python
import jax
import jax.numpy as jnp
from jax import lax
from jax.experimental import pallas as pl
from jax.experimental.pallas import tpu as pltpu
from jax.sharding import PartitionSpec as P

HEADS = 16
PARTS = 2
EPSILON = 1e-05
F32 = jnp.float32
BF16 = jnp.bfloat16
MIB = 1 << 20
NT = (((1,), (1,)), ((), ()))
TN = (((0,), (0,)), ((), ()))


def dot(a, b, dims=(((1,), (0,)), ((), ())), precision=None):
    return lax.dot_general(a, b, dims, precision=precision, preferred_element_type=F32)


def standardize(inputs):
    center = inputs - jnp.mean(inputs, axis=-1, keepdims=True)
    spread = lax.rsqrt(jnp.mean(center * center, axis=-1, keepdims=True) + EPSILON)
    return center * spread, spread


def far(array):
    return pltpu.with_memory_space_constraint(array, pltpu.HBM)


def far_shape(shape, dtype):
    return pltpu.HBM(shape, dtype)


def near_shape(shape, dtype):
    return pltpu.VMEM(shape, dtype)


VMEM = pl.BlockSpec(memory_space=pltpu.VMEM)
SMEM = pl.BlockSpec(memory_space=pltpu.SMEM)
HBM = pl.BlockSpec(memory_space=pltpu.HBM)


def params(mib):
    return pltpu.CompilerParams(vmem_limit_bytes=mib * MIB)


def cost(flops, moved, exps=0):
    return pl.CostEstimate(flops=flops, bytes_accessed=moved, transcendentals=exps)


def pack_kernel(source, packed):
    groups, parts, rows, _ = packed.shape
    frames = source.shape[0]
    size = rows // frames
    for group in range(groups):
        for part in range(parts):
            at = (group * parts + part) * size
            pieces = [source[frame, at : at + size].astype(F32) for frame in range(frames)]
            packed[group, part] = jnp.concatenate(pieces, axis=0).astype(BF16)


def pack(array, groups):
    frames, patches, width = array.shape
    rows = frames * patches // (groups * PARTS)
    return pl.pallas_call(
        pack_kernel,
        out_shape=jax.ShapeDtypeStruct((groups, PARTS, rows, width), array.dtype),
        compiler_params=params(8),
        cost_estimate=cost(0, 4 * array.size),
    )(array)


def place_kernel(index_ref, source, target, own, arrived):
    load = pltpu.make_async_copy(source.at[:, index_ref[0]], own, arrived.at[0])
    load.start()
    load.wait()
    frames = target.shape[0]
    groups, parts, rows, _ = own.shape
    size = rows // frames
    for group in range(groups):
        for frame in range(frames):
            pieces = [
                own[group, part, frame * size : (frame + 1) * size].astype(F32)
                for part in range(parts)
            ]
            target[frame, group] = jnp.concatenate(pieces, axis=0).astype(BF16)


def place(index, gathered, frames):
    groups, _, parts, rows, width = gathered.shape
    size = parts * rows // frames
    placed = pl.pallas_call(
        place_kernel,
        in_specs=[SMEM, HBM],
        out_specs=VMEM,
        out_shape=jax.ShapeDtypeStruct((frames, groups, size, width), BF16),
        scratch_shapes=[
            pltpu.VMEM((groups, parts, rows, width), BF16),
            pltpu.SemaphoreType.DMA((1,)),
        ],
        compiler_params=params(8),
        cost_estimate=cost(0, 4 * groups * parts * rows * width),
    )(index, far(gathered))
    return placed.reshape(frames, groups * size, width)


def row_tiles(row):
    tile = row.shape[1] // 8
    return jnp.concatenate([row[:, i * tile : (i + 1) * tile] for i in range(8)], axis=0)


def tiles_row(tiles):
    return jnp.concatenate([tiles[i : i + 1] for i in range(tiles.shape[0])], axis=1)


def lane_halves(slab):
    lane = lax.broadcasted_iota(jnp.int32, slab.shape, 1)
    low = lane < slab.shape[1] // 2
    zero = jnp.zeros_like(slab)
    return jnp.where(low, slab, zero), jnp.where(low, zero, slab)


def same_patch(rows, columns, patches):
    first = lax.broadcasted_iota(jnp.int32, (rows, columns), 0)
    second = lax.broadcasted_iota(jnp.int32, (rows, columns), 1)
    return lax.rem(first, patches) == lax.rem(second, patches)


def stacked(slab):
    return jnp.concatenate(lane_halves(slab), axis=0)


def side_by_side(array):
    rows = array.shape[0] // 2
    return jnp.concatenate([array[:rows], array[rows:]], axis=1)


def forward_kernel(
    patches,
    x_ref,
    gain_ref,
    w_hbm,
    inputs_hbm,
    normed_hbm,
    proj_hbm,
    pool_ref,
    inputs_ref,
    normed_ref,
    proj_ref,
    total,
    sent,
    w_ref,
    arrived,
):
    rows, width = normed_ref.shape
    block_rows = rows // PARTS
    parts = sent.shape[0] - 1
    chunk = w_ref.shape[1] // parts
    chunks = [pl.ds(part * chunk, chunk) for part in range(parts)]
    loads = [
        pltpu.make_async_copy(w_hbm.at[:, cols], w_ref.at[:, cols], arrived.at[part])
        for part, cols in enumerate(chunks)
    ]
    for load in loads:
        load.start()
    for part in range(PARTS):
        block = x_ref[:, part]
        inputs_ref[part * block_rows : (part + 1) * block_rows] = block.reshape(block_rows, width)
    stores = [pltpu.make_async_copy(inputs_ref, inputs_hbm, sent.at[parts, 1])]
    stores[-1].start()
    inputs = inputs_ref[...].astype(F32)
    standard, _ = standardize(inputs)
    normed = (standard * gain_ref[...]).astype(BF16)
    normed_ref[...] = normed
    stores.append(pltpu.make_async_copy(normed_ref, normed_hbm, sent.at[parts, 0]))
    stores[-1].start()
    total[...] = jnp.sum(inputs, axis=0, keepdims=True)
    for part, cols in enumerate(chunks):
        loads[part].wait()
        proj_ref[:, cols] = dot(normed, w_ref[:, cols]).astype(BF16)
        for pair in range(proj_hbm.shape[0]):
            lanes = pl.ds(part * chunk + pair * proj_hbm.shape[3], proj_hbm.shape[3])
            stores.append(
                pltpu.make_async_copy(
                    proj_ref.at[:, lanes], proj_hbm.at[pair, part], sent.at[part, pair]
                )
            )
            stores[-1].start()
    mask = same_patch(2 * block_rows, block_rows, patches // PARTS)
    slab = 2 * width // HEADS
    scale = (width // HEADS) ** -0.5
    for pair in range(HEADS // 2):
        at = pair * slab
        for part in range(PARTS):
            own = pl.ds(part * block_rows, block_rows)
            query = proj_ref[own, at : at + slab]
            keys = proj_ref[own, width + at : width + at + slab]
            values = proj_ref[own, 2 * width + at : 2 * width + at + slab]
            scores = jnp.where(mask, dot(stacked(query), keys, NT) * scale, -jnp.inf)
            weights = jnp.exp(scores - jnp.max(scores, axis=1, keepdims=True))
            probs = (weights / jnp.sum(weights, axis=1, keepdims=True)).astype(BF16)
            attended = dot(side_by_side(probs), stacked(values)).astype(BF16).astype(F32)
            total[:, at : at + slab] += jnp.sum(attended, axis=0, keepdims=True)
    tiles = row_tiles(total[...])
    for copy in range(pool_ref.shape[0]):
        pool_ref[copy] = tiles
    for store in stores:
        store.wait()


def forward(tokens, gain, w_project, patches, copies):
    width = tokens.shape[-1]
    rows = tokens.size // width
    parts = 3
    return pl.pallas_call(
        lambda *refs: forward_kernel(patches, *refs),
        in_specs=[VMEM, VMEM, HBM],
        out_specs=[HBM, HBM, HBM, VMEM],
        out_shape=(
            far_shape((rows, width), BF16),
            far_shape((rows, width), BF16),
            far_shape((HEADS // 2, 3, rows, 2 * width // HEADS), BF16),
            jax.ShapeDtypeStruct((copies, 8, width // 8), F32),
        ),
        scratch_shapes=[
            pltpu.VMEM((rows, width), BF16),
            pltpu.VMEM((rows, width), BF16),
            pltpu.VMEM((rows, 3 * width), BF16),
            pltpu.VMEM((1, width), F32),
            pltpu.SemaphoreType.DMA((parts + 1, HEADS // 2)),
            pltpu.VMEM(w_project.shape, BF16),
            pltpu.SemaphoreType.DMA((parts,)),
        ],
        compiler_params=params(32),
        cost_estimate=cost(10 * rows * width * width, 10 * MIB, HEADS * rows * rows),
    )(tokens, gain, far(w_project))


def flip_kernel(*refs):
    *sources, target = refs
    at = 0
    for source in sources:
        rows, width = source.shape
        step = 256
        for start in range(0, width, step):
            target[start : start + step, at : at + rows] = source[:, start : start + step].T
        at += rows


def flip(*arrays):
    shape = (arrays[0].shape[1], sum(a.shape[0] for a in arrays))
    return pl.pallas_call(
        flip_kernel,
        in_specs=[VMEM] * len(arrays),
        out_shape=jax.ShapeDtypeStruct(shape, BF16),
        compiler_params=params(56),
        cost_estimate=cost(0, 4 * shape[0] * shape[1]),
    )(*arrays)


def attend_kernel(patches, proj_ref, rounded, norm):
    rows = rounded.shape[3]
    mask = same_patch(2 * rows, rows, patches // PARTS)
    scale = (proj_ref.shape[3] // 2) ** -0.5
    for pair in range(HEADS // 2):
        for part in range(PARTS):
            own = pl.ds(part * rows, rows)
            query = proj_ref[pair, 0, own]
            keys = proj_ref[pair, 1, own]
            scores = jnp.where(mask, dot(stacked(keys), query, NT) * scale, -jnp.inf)
            for head in range(2):
                score = scores[head * rows : (head + 1) * rows]
                weights = jnp.exp(score - jnp.max(score, axis=0, keepdims=True))
                probs = (weights / jnp.sum(weights, axis=0, keepdims=True)).astype(BF16)
                rounded[pair, part, head * rows : (head + 1) * rows] = probs
                number = (pair * PARTS + part) * 2 + head
                norm[number : number + 1] = 1.0 / jnp.sum(
                    probs.astype(F32), axis=0, keepdims=True
                )


def attend(projected, patches):
    rows = projected.shape[2] // PARTS
    pairs = HEADS // 2
    return pl.pallas_call(
        lambda *refs: attend_kernel(patches, *refs),
        in_specs=[VMEM],
        out_shape=(
            jax.ShapeDtypeStruct((pairs, PARTS, 2 * rows, rows), BF16),
            jax.ShapeDtypeStruct((HEADS * PARTS, rows), F32),
        ),
        compiler_params=params(56),
        cost_estimate=cost(8 * rows * rows * projected.shape[3], 6 * MIB, HEADS * rows * rows),
    )(projected)


def total_share(parts_ref, count):
    return tiles_row(jnp.sum(parts_ref[...], axis=0)) / count


def backward_kernel(
    block,
    count,
    core_ref,
    frame_ref,
    x_hbm,
    proj_hbm,
    gathered_hbm,
    parts_ref,
    rounded_hbm,
    norm_ref,
    gain_ref,
    w_hbm,
    keep_hbm,
    send_hbm,
    token_ref,
    gain_out,
    proj_grad,
    sorted_grad,
    w_ref,
    received,
    grad_ref,
    x_ref,
    proj_ref,
    rounded,
    arrived,
    ready,
):
    rows, width = grad_ref.shape
    block_rows = rows // PARTS
    load = pltpu.make_async_copy(gathered_hbm.at[:, frame_ref[0]], received, arrived.at[3])
    load.start()
    pairs = []
    for pair in range(HEADS // 2):
        pairs.append(
            [
                pltpu.make_async_copy(proj_hbm.at[pair], proj_ref.at[pair], ready.at[pair, 0]),
                pltpu.make_async_copy(rounded_hbm.at[pair], rounded.at[pair], ready.at[pair, 1]),
            ]
        )
        for pair_load in pairs[-1]:
            pair_load.start()
    x_load = pltpu.make_async_copy(x_hbm, x_ref, arrived.at[4])
    x_load.start()
    w_load = pltpu.make_async_copy(w_hbm, w_ref, arrived.at[0])
    w_load.start()
    load.wait()
    frames, size, _ = received.shape
    run = token_ref.shape[2] * PARTS // size
    size = size // PARTS
    for part in range(PARTS):
        for first in range(0, frames, run):
            pieces = [
                received[frame, part * size : (part + 1) * size].astype(F32)
                for frame in range(first, first + run)
            ]
            start = part * block_rows + first * size
            grad_ref[start : start + run * size] = jnp.concatenate(pieces, axis=0).astype(BF16)
    share = tiles_row(jnp.sum(parts_ref[...], axis=0)) / count
    slab = 2 * width // HEADS
    scale = (width // HEADS) ** -0.5
    for pair in range(HEADS // 2):
        at = pair * slab
        if pair % 4 == 0:
            for group in pairs[pair : pair + 4]:
                for pair_load in group:
                    pair_load.wait()
        for part in range(PARTS):
            own = pl.ds(part * block_rows, block_rows)
            query = proj_ref[pair, 0, own]
            keys = proj_ref[pair, 1, own]
            values = proj_ref[pair, 2, own]
            grads = grad_ref[own, at : at + slab].astype(F32) + share[:, at : at + slab]
            grads = grads.astype(BF16)
            probs = rounded[pair, part]
            prob_grad = dot(stacked(values), grads, NT)
            score_grads = []
            for head in range(2):
                mine = slice(head * block_rows, (head + 1) * block_rows)
                number = (pair * PARTS + part) * 2 + head
                weights = probs[mine].astype(F32)
                moved = prob_grad[mine]
                mean = jnp.sum(weights * moved, axis=0, keepdims=True)
                mean = mean * norm_ref[number : number + 1]
                score_grads.append((weights * (moved - mean) * scale).astype(BF16))
            key_grad = dot(jnp.concatenate(score_grads, 1), stacked(query))
            query_grad = dot(jnp.concatenate(score_grads, 0), stacked(keys), TN)
            value_grad = dot(side_by_side(probs), stacked(grads))
            for first, grad in zip((0, width, 2 * width), (query_grad, key_grad, value_grad)):
                start = first + at
                grad = grad.astype(BF16)
                proj_grad[own, start : start + slab] = grad
                number, inside = divmod(start, block)
                owner, place = number % 2, number // 2 * block + inside
                sorted_grad[core_ref[0] ^ owner, own, place : place + slab] = grad

    stores = [
        pltpu.make_async_copy(sorted_grad.at[number], target, arrived.at[1 + number])
        for number, target in enumerate((keep_hbm, send_hbm))
    ]
    for store in stores:
        store.start()
    x_load.wait()
    w_load.wait()
    normed_grad = dot(proj_grad[...], w_ref[...])
    standard, spread = standardize(x_ref[...].astype(F32))
    gain_out[...] = row_tiles(jnp.sum(normed_grad * standard, axis=0, keepdims=True))
    scaled = normed_grad * gain_ref[...]
    centered = (
        scaled
        - jnp.mean(scaled, axis=-1, keepdims=True)
        - standard * jnp.mean(scaled * standard, axis=-1, keepdims=True)
    )
    total_grad = grad_ref[...].astype(F32) + share
    token_grad = (total_grad + spread * centered).astype(BF16)
    owners, _, size, _ = token_ref.shape
    for part in range(PARTS):
        for owner in range(owners):
            start = part * block_rows + owner * size
            token_ref[owner, part] = token_grad[start : start + size]
    for store in stores:
        store.wait()


def backward(
    core,
    index,
    tokens,
    projected,
    gathered,
    share_parts,
    rounded,
    norm,
    gain,
    w_flipped,
    block,
    count,
    owners,
):
    rows, width = tokens.shape
    half = jax.ShapeDtypeStruct((rows, 3 * width // 2), BF16)
    return pl.pallas_call(
        lambda *refs: backward_kernel(block, count, *refs),
        in_specs=[SMEM, SMEM, HBM, HBM, HBM, VMEM, HBM, VMEM, VMEM, HBM],
        out_specs=[HBM, HBM, VMEM, VMEM],
        out_shape=(
            half,
            half,
            far_shape((owners, PARTS, rows // (owners * PARTS), width), BF16),
            jax.ShapeDtypeStruct((8, width // 8), F32),
        ),
        scratch_shapes=[
            pltpu.VMEM((rows, 3 * width), BF16),
            pltpu.VMEM((2, rows, 3 * width // 2), BF16),
            pltpu.VMEM(w_flipped.shape, BF16),
            pltpu.VMEM(gathered.shape[:1] + gathered.shape[2:], BF16),
            pltpu.VMEM((rows, width), BF16),
            pltpu.VMEM(tokens.shape, BF16),
            pltpu.VMEM(projected.shape, BF16),
            pltpu.VMEM(rounded.shape, BF16),
            pltpu.SemaphoreType.DMA((5,)),
            pltpu.SemaphoreType.DMA((HEADS // 2, 2)),
        ],
        compiler_params=params(52),
        cost_estimate=cost(14 * rows * rows * width, 12 * MIB),
    )(
        core,
        index,
        far(tokens),
        far(projected),
        far(gathered),
        share_parts,
        far(rounded),
        norm,
        gain,
        far(w_flipped),
    )


def split_sum(tiles):
    high = tiles.astype(BF16).astype(F32)
    return jnp.concatenate([high, tiles - high], axis=0).astype(BF16)


def weight_kernel(
    halves, steps, flipped, grad_ref, other_ref, gain_ref, other_gain, out_ref
):
    groups, total_rows, lanes = out_ref.shape
    width = flipped.shape[0]
    rows, cols = grad_ref.shape
    block = width // (groups * halves)
    cols = cols // steps
    tiles = cols // lanes
    span = tiles * halves * block
    spans = [pl.ds(step * cols, cols) for step in range(steps)]
    for step, at in enumerate(spans):
        both = jnp.concatenate([grad_ref[:, at], other_ref[:, at]], axis=0)
        terms = dot(flipped[...], both).astype(BF16)
        for tile in range(tiles):
            for half in range(halves):
                for group in range(groups):
                    start = (half * groups + group) * block
                    place = step * span + (tile * halves + half) * block
                    out_ref[group, place : place + block] = terms[
                        start : start + block, tile * lanes : (tile + 1) * lanes
                    ]
    tail = split_sum(gain_ref[...] + other_gain[...])
    for group in range(groups):
        out_ref[group, steps * span :] = tail


def weight_terms(flipped, grads, other_grads, gain, other_gain, groups, halves, steps):
    width, rows = flipped.shape
    lanes = 128
    shape = (groups, width // groups * grads.shape[1] // lanes + 16, lanes)
    return pl.pallas_call(
        lambda *refs: weight_kernel(halves, steps, *refs),
        in_specs=[VMEM] * 5,
        out_specs=VMEM,
        out_shape=near_shape(shape, BF16),
        compiler_params=params(24),
        cost_estimate=cost(2 * rows * width * grads.shape[1], 6 * MIB),
    )(flipped, grads, other_grads, gain, other_gain)


def regroup_kernel(block, terms_ref, out_ref):
    halves, steps, rows, _ = out_ref.shape
    tiles = (rows - 16) // block
    total = jnp.sum(terms_ref[...].astype(F32), axis=0)
    terms = total.astype(BF16)
    end = total.shape[0] - 16
    gains = split_sum(total[end : end + 8] + total[end + 8 :])
    for half in range(halves):
        for step in range(steps):
            for tile in range(tiles):
                start = ((step * tiles + tile) * halves + half) * block
                out_ref[half, step, tile * block : (tile + 1) * block] = terms[
                    start : start + block
                ]
            out_ref[half, step, tiles * block :] = gains


def regroup(terms, halves, steps, block):
    count, rows, lanes = terms.shape
    shape = (halves, steps, (rows - 16) // (halves * steps) + 16, lanes)
    return pl.pallas_call(
        lambda *refs: regroup_kernel(block, *refs),
        in_specs=[VMEM],
        out_shape=jax.ShapeDtypeStruct(shape, BF16),
        compiler_params=params(32),
        cost_estimate=cost(terms.size, 4 * MIB),
    )(terms)


def finish_kernel(terms_ref, out_ref, gain_ref):
    total = jnp.sum(terms_ref[...].astype(F32), axis=0)
    block = out_ref.shape[0]
    lanes = total.shape[1]
    for tile in range(out_ref.shape[1] // lanes):
        out_ref[:, tile * lanes : (tile + 1) * lanes] = total[tile * block : (tile + 1) * block]
    end = total.shape[0] - 16
    gain_ref[...] = tiles_row(total[end : end + 8] + total[end + 8 :])


def finish(terms, block):
    count, rows, lanes = terms.shape
    return pl.pallas_call(
        finish_kernel,
        in_specs=[VMEM],
        out_shape=(
            jax.ShapeDtypeStruct((block, (rows - 16) // block * lanes), F32),
            jax.ShapeDtypeStruct((1, 8 * lanes), F32),
        ),
        compiler_params=params(16),
        cost_estimate=cost(terms.size, MIB),
    )(terms)


def pool_kernel(halves, tokens, parts_ref, out_ref):
    per_clip = parts_ref.shape[0] // halves
    means = []
    for half in range(halves):
        pooled = jnp.sum(parts_ref[half * per_clip : (half + 1) * per_clip], axis=0) / tokens
        means.append(pooled)
    means = jnp.concatenate(means, axis=0).astype(BF16)
    for copy in range(out_ref.shape[0]):
        out_ref[copy] = means


def pool(parts, halves, tokens, copies):
    return pl.pallas_call(
        lambda *refs: pool_kernel(halves, tokens, *refs),
        in_specs=[VMEM],
        out_shape=jax.ShapeDtypeStruct((copies, halves * parts.shape[1], parts.shape[2]), BF16),
        compiler_params=params(8),
        cost_estimate=cost(parts.size, MIB),
    )(parts)


def embed_kernel(halves, pooled_ref, w_ref, pooled_out, centered_ref, gram_ref, rows_ref):
    groups, tiles, lanes = pooled_ref.shape
    tiles = tiles // halves
    means = pooled_ref[...].astype(F32)
    for half in range(halves):
        for tile in range(tiles):
            rows_ref[half * groups : (half + 1) * groups, tile * lanes : (tile + 1) * lanes] = (
                means[:, half * tiles + tile, :]
            )
    pooled = rows_ref[...].astype(BF16)
    pooled_out[...] = pooled
    embedding = dot(pooled, w_ref[...])
    centered = embedding - jnp.mean(embedding, axis=0, keepdims=True)
    centered_ref[...] = centered
    gram = dot(centered, centered, NT, lax.Precision.HIGHEST)
    size = gram_ref.shape[1]
    gram = [gram[i : i + size] for i in range(0, gram.shape[0], size)]
    gram = jnp.concatenate(gram, axis=1)
    for copy in range(gram_ref.shape[0]):
        gram_ref[copy] = gram


def embed(pooled, w_expand, copies, halves):
    clips = pooled.shape[0] * halves
    width, columns = w_expand.shape
    return pl.pallas_call(
        lambda *refs: embed_kernel(halves, *refs),
        in_specs=[VMEM, VMEM],
        out_shape=(
            jax.ShapeDtypeStruct((clips, width), BF16),
            jax.ShapeDtypeStruct((clips, columns), F32),
            jax.ShapeDtypeStruct((copies, min(clips, 8), clips * clips // min(clips, 8)), F32),
        ),
        scratch_shapes=[pltpu.VMEM((clips, width), F32)],
        compiler_params=params(16),
        cost_estimate=cost(2 * clips * w_expand.size, 2 * MIB),
    )(pooled, w_expand)


def embed_grad_kernel(coefficient, own_ref, gram_ref, centered_ref, w_ref, grad_ref, pool_ref):
    clips = centered_ref.shape[0]
    centered = centered_ref[...]
    gram = jnp.sum(gram_ref[...], axis=0)
    gram = [gram[:, i : i + clips] for i in range(0, gram.shape[1], clips)]
    gram = jnp.concatenate(gram, axis=0)
    variances = jnp.sum(centered * centered, axis=0, keepdims=True) / (clips - 1)
    mixed = dot(gram, centered, precision=lax.Precision.HIGHEST)
    grads = coefficient * (mixed / (clips - 1) - centered * variances)
    grad_ref[...] = grads.astype(BF16)
    row = lax.broadcasted_iota(jnp.int32, grads.shape, 0)
    own = jnp.sum(jnp.where(row == own_ref[0], grads, 0.0), axis=0, keepdims=True)
    own = jnp.broadcast_to(own, (16, own.shape[1])).astype(BF16)
    part = row_tiles(dot(own, w_ref[...], NT)[0:1])
    for copy in range(pool_ref.shape[0]):
        pool_ref[copy] = part


def embed_grads(own_index, gram_parts, centered, w_expand, coefficient):
    width = w_expand.shape[0]
    return pl.pallas_call(
        lambda *refs: embed_grad_kernel(coefficient, *refs),
        in_specs=[SMEM, VMEM, VMEM, VMEM],
        out_shape=(
            jax.ShapeDtypeStruct(centered.shape, BF16),
            jax.ShapeDtypeStruct((gram_parts.shape[0], 8, width // 8), F32),
        ),
        compiler_params=params(16),
        cost_estimate=cost(2 * 16 * w_expand.size, 2 * MIB),
    )(own_index, gram_parts, centered, w_expand)


DP = ("zh", "x", "y")
FRAME = ("zl", "core")
SIZES = {"zh": 2, "x": 4, "y": 4, "zl": 4, "core": 2}
SWAP = [(0, 1), (1, 0)]


def to_each(array, axis):
    return lax.all_to_all(array, axis, split_axis=0, concat_axis=0, tiled=True)


def per_device(clip_tokens, out_grad, ln_gain, w_project, w_expand):
    frame_count = lax.axis_size(FRAME)
    clip_count = lax.axis_size(DP)
    halves, steps = lax.axis_size("zh"), lax.axis_size("zl")
    plane = lax.axis_size(("x", "y"))
    core = lax.axis_index("core").reshape(1)
    own_frame = lax.axis_index(FRAME).reshape(1)
    own_clip = lax.axis_index(DP)
    frames_dev, patches, width = clip_tokens.shape[1:]
    patches_dev = patches // frame_count
    rows = frames_dev * patches
    tokens_clip = frames_dev * frame_count * patches
    column_block = 3 * width // frame_count
    block_rows = width // clip_count
    gain = ln_gain[None, :]

    w_flipped = flip(w_project)
    tokens = to_each(pack(clip_tokens[0], frame_count), FRAME)
    out_grad, tokens, w_flipped = lax.optimization_barrier((out_grad, tokens, w_flipped))
    gathered = lax.all_gather(out_grad[0], FRAME, axis=0, tiled=True)
    tokens, normed, projected, pool_parts = forward(
        tokens, gain, w_project, patches_dev, halves * frame_count
    )
    other_normed = lax.ppermute(normed, "core", SWAP)

    pool_parts = to_each(pool_parts, ("zh",) + FRAME)
    pooled = to_each(pool(pool_parts, halves, tokens_clip, plane), ("x", "y"))
    rounded, norm = attend(projected, patches_dev)
    pooled, rounded, norm = lax.optimization_barrier((pooled, rounded, norm))
    pooled_all, centered, gram_parts = embed(pooled, w_expand, frame_count, halves)
    gram_parts = to_each(gram_parts, FRAME)
    flipped = flip(normed, other_normed)
    gram_parts, flipped = lax.optimization_barrier((gram_parts, flipped))
    coefficient = 100.0 * tokens_clip / (w_expand.shape[1] * frame_count * (clip_count - 1))
    embed_grad, share_parts = embed_grads(
        own_clip.reshape(1), gram_parts, centered, w_expand, coefficient
    )
    share_parts = to_each(share_parts, FRAME)
    row_part = lax.dynamic_slice_in_dim(pooled_all, own_clip * block_rows, block_rows, 1)
    expand_grad = dot(row_part, embed_grad, TN)

    gathered, _ = lax.optimization_barrier((gathered, gram_parts))
    gathered = gathered.reshape(-1, frame_count, patches_dev, width)

    kept, outgoing, token_part, gain_part = backward(
        core,
        own_frame,
        tokens,
        projected,
        gathered,
        share_parts,
        rounded,
        norm,
        gain,
        w_flipped,
        column_block,
        tokens_clip,
        frame_count,
    )
    token_parts = lax.all_gather(token_part, FRAME)
    incoming, other_gain = lax.ppermute((outgoing, gain_part), "core", SWAP)
    terms = weight_terms(
        flipped, kept, incoming, gain_part, other_gain, plane, halves, steps
    )
    terms = to_each(terms, ("x", "y"))
    terms = regroup(terms, halves, steps, block_rows)
    terms = to_each(terms.reshape((-1,) + terms.shape[2:]), ("zh", "zl"))
    token_grad = place(own_frame, token_parts, frames_dev)[None]
    terms, token_grad = lax.optimization_barrier((terms, token_grad))
    project_grad, gain_grad = finish(terms, block_rows)
    return (token_grad, project_grad, expand_grad, gain_grad[0])


def solution(mesh):
    split = jax.sharding.Mesh(
        mesh.devices.reshape(tuple(SIZES.values())), tuple(SIZES)
    )
    return jax.shard_map(
        per_device,
        mesh=split,
        in_specs=(
            P(DP, FRAME, None, None),
            P(DP, FRAME, None, None),
            P(),
            P(),
            P(None, FRAME),
        ),
        out_specs=(P(DP, FRAME, None, None), P(DP, FRAME), P(DP, FRAME), P()),
        check_vma=False,
    )
```
